32 devices in a mesh: region: 4 (over x, core), patch: 8 (over z, y).
Axes of the slice: x: 2, y: 2, z: 4, core: 2. Of those that a mesh axis runs over, the one named last changes fastest.
Arguments:
- nodes: bfloat16 [8192, 512], P(('region', 'patch')), may hold values from -6 to 6
- edges: bfloat16 [32768, 512], P(('region', 'patch')), may hold values from -6 to 6
- node_cotan: bfloat16 [8192, 512], P(('region', 'patch')), may hold values from -6 to 6
- edge_cotan: bfloat16 [32768, 512], P(('region', 'patch')), may hold values from -6 to 6
- edge_inner: bfloat16 [1536, 512], replicated, may hold values from -0.15625 to 0.15625
- edge_outer: bfloat16 [512, 512], replicated, may hold values from -0.25 to 0.25
- node_inner: bfloat16 [1024, 512], replicated, may hold values from -0.1875 to 0.1875
- node_outer: bfloat16 [512, 512], replicated, may hold values from -0.25 to 0.25
- edge_shift: float32 [512], replicated, may hold values from -4 to 4
- edge_offset: float32 [512], replicated, may hold values from -4 to 4
- edge_gain: float32 [512], replicated, may hold values from 0.5 to 1.5
- node_shift: float32 [512], replicated, may hold values from -4 to 4
- node_offset: float32 [512], replicated, may hold values from -4 to 4
- node_gain: float32 [512], replicated, may hold values from 0.5 to 1.5
- send_rows: int32 [4, 8, 2, 32], P('region', 'patch'), may hold values from -1 to 255, as said below
- senders: int32 [32768], P(('region', 'patch')), may hold values from 0 to 319, as said below
- receivers: int32 [32768], P(('region', 'patch')), may hold values from 0 to 255
Outputs:
- grad_nodes: float32 [8192, 512], P(('region', 'patch'))
- grad_edges: bfloat16 [32768, 512], P(('region', 'patch'))
- grad_weights: float32 [1835008], P(('region', 'patch'))
- grad_vectors: float32 [3072], replicated
The draws below stay inside these ranges and needn't reach their ends.
Inputs may be any that keep to these rules, and one draw needn't show every extreme that they name: `send_rows`: list 0 of a patch goes to the patch one index below, list 1 to the one above, cyclically within its region. Live entries are distinct own-node indices and stand first, the rest are -1; each list has half of 32 to 32 live entries, and some list is full. `senders`: below 256 a sender is an own node; 256 + j is the j-th row received from the patch below, 288 + j the j-th from the patch above; only live rows are named.
All inputs are finite; a program needn't handle non-finite values.
Results may differ from the reference program's by a relative error of at most 0.0063.
Values may be sent and summed in bfloat16 or wider, within the bound.
No kernel may reach another device: no remote copies, remote signals or barrier semaphores. Data moves between devices by JAX's collectives and lax.ppermute only.
A program may use at most 128 MiB of HBM per device.

```python
import math
import jax
import jax.numpy as jnp
from jax import lax

D = 512
H = 512
NODE_DEV = 256
SEND = 32
EDGE_DEV = 1024
NODES = 8192
EDGES = 32768
N_REGION = 4
N_PATCH = 8


def halo_counts(key):
    counts = jax.random.randint(jax.random.fold_in(key, 11), (N_REGION * N_PATCH, 2), SEND // 2, SEND + 1)
    chosen = jax.random.randint(jax.random.fold_in(key, 12), (), 0, N_REGION * N_PATCH)
    places = jnp.arange(N_REGION * N_PATCH, dtype=jnp.int32)
    counts = jnp.where((places == chosen)[:, None], SEND, counts)
    return counts.reshape(N_REGION, N_PATCH, 2).astype(jnp.int32)


def draw_send_rows(key, part):
    counts = halo_counts(key).reshape(-1)
    list_keys = jax.random.split(jax.random.fold_in(key, 13), N_REGION * N_PATCH * 2)
    chosen = jax.vmap(lambda one_key: jax.random.permutation(one_key, NODE_DEV)[:SEND])(list_keys).astype(jnp.int32)
    slots = jnp.arange(SEND, dtype=jnp.int32)
    filled = jnp.where(slots[None, :] < counts[:, None], chosen, -1)
    return filled.reshape(N_REGION, N_PATCH, 2, SEND).astype(jnp.int32)


def draw_senders(key, part):
    counts = halo_counts(key)
    lower_count = jnp.roll(counts[:, :, 1], 1, axis=1).reshape(-1)
    upper_count = jnp.roll(counts[:, :, 0], -1, axis=1).reshape(-1)
    devices_all = N_REGION * N_PATCH
    shape = (devices_all, EDGE_DEV)
    kinds = jax.random.randint(jax.random.fold_in(key, 21), shape, 0, 10)
    own_pick = jax.random.randint(jax.random.fold_in(key, 22), shape, 0, NODE_DEV)
    lower_pick = NODE_DEV + jax.random.randint(jax.random.fold_in(key, 23), shape, 0, lower_count[:, None])
    upper_pick = NODE_DEV + SEND + jax.random.randint(jax.random.fold_in(key, 24), shape, 0, upper_count[:, None])
    chosen = jnp.where(kinds < 6, own_pick, jnp.where(kinds < 8, lower_pick, upper_pick))
    column = jnp.arange(EDGE_DEV, dtype=jnp.int32)[None, :]
    chosen = jnp.where(column == EDGE_DEV - 1, (NODE_DEV + SEND - 1 + upper_count)[:, None], chosen)
    chosen = jnp.where(column == EDGE_DEV - 2, (NODE_DEV - 1 + lower_count)[:, None], chosen)
    chosen = jnp.where(column == EDGE_DEV - 3, 0, chosen)
    return chosen.reshape(-1).astype(jnp.int32)


def plant(array, own_key, smallest, largest):
    longest = array.shape.index(max(array.shape))
    spots = []
    for shift in (0, 1):
        where = [jax.random.randint(jax.random.fold_in(own_key, axis), (), 0, length) for axis, length in enumerate(array.shape)]
        where[longest] = (where[longest] + shift) % array.shape[longest]
        spots.append(tuple(where))
    return array.at[spots[0]].set(smallest).at[spots[1]].set(largest)


def shard_levels(key, dims, cuts, low, high):
    gain, own = 1.0, jax.random.fold_in(key, 6)
    for axis_at, parts in cuts:
        heights = jnp.exp(jax.random.uniform(jax.random.fold_in(own, axis_at), (parts,), jnp.float32, low / len(cuts), high / len(cuts)))
        gain = gain * jnp.repeat(heights, dims[axis_at] // parts).reshape([-1 if axis == axis_at else 1 for axis in range(len(dims))])
    return gain


def scatter_about(own_key, extent, deviation, limit, shards=(), kind=jnp.bfloat16):
    drawn = deviation * jax.random.normal(own_key, extent, jnp.float32)
    if shards:
        drawn = drawn * shard_levels(own_key, extent, shards, -0.22, 0.18)
    return jnp.clip(drawn, -limit, limit).astype(kind)


def setup_inputs(seed: int = 0) -> dict:
    splits = jax.random.split(jax.random.key(seed), 18)
    nodes = scatter_about(splits[0], (NODES, D), 1.0, 6.0, ((0, 32),))
    edges = scatter_about(splits[1], (EDGES, D), 1.0, 6.0, ((0, 32),))
    node_cotan = scatter_about(splits[2], (NODES, D), 1.0, 6.0, ((0, 32),))
    edge_cotan = scatter_about(splits[3], (EDGES, D), 1.0, 6.0, ((0, 32),))
    edge_inner = scatter_about(splits[4], (3 * D, H), (3 * D) ** -0.5, 0.15625)
    edge_outer = scatter_about(splits[5], (H, D), H ** -0.5, 0.25)
    node_inner = scatter_about(splits[6], (2 * D, H), (2 * D) ** -0.5, 0.1875)
    node_outer = scatter_about(splits[7], (H, D), H ** -0.5, 0.25)
    edge_shift = scatter_about(splits[8], (H,), 1.0, 4.0, (), jnp.float32)
    edge_offset = scatter_about(splits[9], (D,), 1.0, 4.0, (), jnp.float32)
    edge_gain = jnp.clip(jax.random.uniform(splits[10], (D,), jnp.float32, 0.5, 1.5), 0.5, 1.5)
    node_shift = scatter_about(splits[11], (H,), 1.0, 4.0, (), jnp.float32)
    node_offset = scatter_about(splits[12], (D,), 1.0, 4.0, (), jnp.float32)
    node_gain = jnp.clip(jax.random.uniform(splits[13], (D,), jnp.float32, 0.5, 1.5), 0.5, 1.5)
    send_rows = draw_send_rows(jax.random.fold_in(splits[17], 71), 0)
    senders = draw_senders(jax.random.fold_in(splits[17], 71), 0)
    receivers = plant(jax.random.randint(splits[16], (EDGES,), 0, NODE_DEV), jax.random.fold_in(splits[16], 1), 0, NODE_DEV - 1).astype(jnp.int32)
    return dict(nodes=nodes, edges=edges, node_cotan=node_cotan, edge_cotan=edge_cotan, edge_inner=edge_inner, edge_outer=edge_outer, node_inner=node_inner, node_outer=node_outer, edge_shift=edge_shift, edge_offset=edge_offset, edge_gain=edge_gain, node_shift=node_shift, node_offset=node_offset, node_gain=node_gain, send_rows=send_rows, senders=senders, receivers=receivers)


def layer_norm(values):
    centred = values - lax.optimization_barrier(jnp.mean(values, axis=-1, keepdims=True))
    invstd = lax.rsqrt(lax.optimization_barrier(jnp.mean(centred * centred, axis=-1, keepdims=True)) + 1e-05)
    return (centred * invstd, invstd)

def norm_back(upstream, normed, invstd, gains):
    scaled = upstream * gains
    return invstd * (scaled - lax.optimization_barrier(jnp.mean(scaled, axis=-1, keepdims=True)) - normed * lax.optimization_barrier(jnp.mean(scaled * normed, axis=-1, keepdims=True)))

def activation_grad(preact):
    sigmoid_val = jax.nn.sigmoid(preact)
    return sigmoid_val * (1.0 + preact * (1.0 - sigmoid_val))

def contract_rows(left, right):
    return jnp.dot(left.T, right, preferred_element_type=jnp.float32)

def reference(nodes, edges, node_cotan, edge_cotan, edge_inner, edge_outer, node_inner, node_outer, edge_shift, edge_offset, edge_gain, node_shift, node_offset, node_gain, send_rows, senders, receivers):
    devices_all = N_REGION * N_PATCH
    node_blocks = nodes.reshape(devices_all, NODE_DEV, D)
    edge_blocks = edges.reshape(devices_all, EDGE_DEV, D)
    ncotan_blocks = node_cotan.reshape(devices_all, NODE_DEV, D)
    ecotan_blocks = edge_cotan.reshape(devices_all, EDGE_DEV, D)
    send_lists = send_rows.reshape(devices_all, 2 * SEND)
    sender_blocks = senders.reshape(devices_all, EDGE_DEV)
    receiver_blocks = receivers.reshape(devices_all, EDGE_DEV)
    node_ids = jnp.arange(NODE_DEV, dtype=jnp.int32)
    lookup_ids = jnp.arange(NODE_DEV + 2 * SEND, dtype=jnp.int32)
    edge_norm = 1.0 / math.sqrt(EDGES)
    node_norm = 1.0 / math.sqrt(NODES)

    def outgoing_rows(block, lists):
        pick = (lists[:, None] == node_ids[None, :]).astype(jnp.bfloat16)
        return jnp.dot(pick, block, preferred_element_type=jnp.float32).astype(jnp.bfloat16)
    outgoing = jax.vmap(outgoing_rows)(node_blocks, send_lists).reshape(N_REGION, N_PATCH, 2, SEND, D)
    from_lower = jnp.roll(outgoing[:, :, 1], 1, axis=1)
    from_upper = jnp.roll(outgoing[:, :, 0], -1, axis=1)
    received = jnp.concatenate([from_lower, from_upper], axis=2).reshape(devices_all, 2 * SEND, D)

    def local_pass(carry, items):
        flat_sum, vector_sum = carry
        own_nodes, own_edges, ncotan, ecotan, rows_in, sender_ids, receiver_ids = items
        lookup = jnp.concatenate([own_nodes, rows_in], axis=0)
        pick_sender = (sender_ids[:, None] == lookup_ids[None, :]).astype(jnp.bfloat16)
        pick_receiver = (receiver_ids[:, None] == node_ids[None, :]).astype(jnp.bfloat16)
        sender_rows = jnp.dot(pick_sender, lookup, preferred_element_type=jnp.float32).astype(jnp.bfloat16)
        receiver_rows = jnp.dot(pick_receiver, own_nodes, preferred_element_type=jnp.float32).astype(jnp.bfloat16)
        edge_inputs = jnp.concatenate([own_edges, sender_rows, receiver_rows], axis=1)
        edge_preact = jnp.dot(edge_inputs, edge_inner, preferred_element_type=jnp.float32) + edge_shift
        edge_hidden = jax.nn.silu(edge_preact).astype(jnp.bfloat16)
        edge_linear = jnp.dot(edge_hidden, edge_outer, preferred_element_type=jnp.float32) + edge_offset
        edge_normed, edge_invstd = layer_norm(edge_linear)
        edge_fresh = (own_edges.astype(jnp.float32) + edge_gain * edge_normed).astype(jnp.bfloat16)
        aggregate = contract_rows(pick_receiver, edge_fresh).astype(jnp.bfloat16)
        node_inputs = jnp.concatenate([own_nodes, aggregate], axis=1)
        node_preact = jnp.dot(node_inputs, node_inner, preferred_element_type=jnp.float32) + node_shift
        node_hidden = jax.nn.silu(node_preact).astype(jnp.bfloat16)
        node_linear = jnp.dot(node_hidden, node_outer, preferred_element_type=jnp.float32) + node_offset
        node_normed, node_invstd = layer_norm(node_linear)
        cotan_node = ncotan.astype(jnp.float32)
        linear_back = norm_back(cotan_node, node_normed, node_invstd, node_gain)
        linear_half = linear_back.astype(jnp.bfloat16)
        preact_back = jnp.dot(linear_half, node_outer.T, preferred_element_type=jnp.float32) * activation_grad(node_preact)
        preact_half = preact_back.astype(jnp.bfloat16)
        inputs_back = jnp.dot(preact_half, node_inner.T, preferred_element_type=jnp.float32)
        aggregate_half = inputs_back[:, D:].astype(jnp.bfloat16)
        fresh_back = ecotan.astype(jnp.float32) + jnp.dot(pick_receiver, aggregate_half, preferred_element_type=jnp.float32)
        elinear_back = norm_back(fresh_back, edge_normed, edge_invstd, edge_gain)
        elinear_half = elinear_back.astype(jnp.bfloat16)
        epreact_back = jnp.dot(elinear_half, edge_outer.T, preferred_element_type=jnp.float32) * activation_grad(edge_preact)
        epreact_half = epreact_back.astype(jnp.bfloat16)
        einputs_back = jnp.dot(epreact_half, edge_inner.T, preferred_element_type=jnp.float32)
        grad_edge_block = (fresh_back + einputs_back[:, :D]).astype(jnp.bfloat16)
        sender_half = einputs_back[:, D:2 * D].astype(jnp.bfloat16)
        receiver_half = einputs_back[:, 2 * D:].astype(jnp.bfloat16)
        lookup_back = contract_rows(pick_sender, sender_half)
        partial_nodes = cotan_node + inputs_back[:, :D] + lookup_back[:NODE_DEV] + contract_rows(pick_receiver, receiver_half)
        rim_back = lookup_back[NODE_DEV:].reshape(2, SEND, D)
        flat_terms = jnp.concatenate([(contract_rows(edge_inputs, epreact_half) * edge_norm).reshape(-1), (contract_rows(edge_hidden, elinear_half) * edge_norm).reshape(-1), (contract_rows(node_inputs, preact_half) * node_norm).reshape(-1), (contract_rows(node_hidden, linear_half) * node_norm).reshape(-1)])
        vector_terms = jnp.concatenate([lax.optimization_barrier(jnp.sum(epreact_back, axis=0)) * edge_norm, lax.optimization_barrier(jnp.sum(elinear_back, axis=0)) * edge_norm, lax.optimization_barrier(jnp.sum(fresh_back * edge_normed, axis=0)) * edge_norm, lax.optimization_barrier(jnp.sum(preact_back, axis=0)) * node_norm, lax.optimization_barrier(jnp.sum(linear_back, axis=0)) * node_norm, lax.optimization_barrier(jnp.sum(cotan_node * node_normed, axis=0)) * node_norm])
        return ((flat_sum + flat_terms, vector_sum + vector_terms), (partial_nodes, grad_edge_block, rim_back))
    start = (jnp.zeros((7 * D * H,), jnp.float32), jnp.zeros((2 * H + 4 * D,), jnp.float32))
    sums, stacked = lax.scan(local_pass, start, (node_blocks, edge_blocks, ncotan_blocks, ecotan_blocks, received, sender_blocks, receiver_blocks))
    grad_weights, grad_vectors = sums
    partial_nodes, grad_edge_blocks, rim_all = stacked
    rim_all = rim_all.reshape(N_REGION, N_PATCH, 2, SEND, D)
    back_lower = jnp.roll(rim_all[:, :, 1], 1, axis=1)
    back_upper = jnp.roll(rim_all[:, :, 0], -1, axis=1)
    back_rows = jnp.concatenate([back_lower, back_upper], axis=2).reshape(devices_all, 2 * SEND, D)

    def rim_add(lists, rows_back):
        pick = (lists[:, None] == node_ids[None, :]).astype(jnp.float32)
        return jnp.dot(pick.T, rows_back, precision=lax.Precision.HIGHEST, preferred_element_type=jnp.float32)
    from_rims = jax.vmap(rim_add)(send_lists, back_rows)
    grad_nodes = (partial_nodes + from_rims).reshape(NODES, D)
    grad_edges = grad_edge_blocks.reshape(EDGES, D)
    return (grad_nodes, grad_edges, grad_weights, grad_vectors)
```

```python
import math

import jax
import jax.numpy as jnp
from jax import lax
from jax.sharding import PartitionSpec as P


def extended(block, sides, width):
    for axis, dim in sides:
        count = lax.axis_size(axis)
        forward = [(i, i + 1) for i in range(count - 1)]
        forward.append((count - 1, 0))
        backward = [(target, source) for source, target in forward]
        low = lax.ppermute(
            lax.slice_in_dim(block, block.shape[dim] - width, None, axis=dim), axis, forward
        )
        high = lax.ppermute(lax.slice_in_dim(block, 0, width, axis=dim), axis, backward)
        block = jnp.concatenate([low, block, high], axis=dim)
    return block


def layer_norm(values):
    centred = values - jnp.mean(values, axis=-1, keepdims=True)
    invstd = lax.rsqrt(jnp.mean(centred * centred, axis=-1, keepdims=True) + 1e-05)
    return (centred * invstd, invstd)


def norm_back(upstream, normed, invstd, gains):
    scaled = upstream * gains
    return invstd * (
        scaled
        - jnp.mean(scaled, axis=-1, keepdims=True)
        - normed * jnp.mean(scaled * normed, axis=-1, keepdims=True)
    )


def activation_grad(preact):
    sigmoid_val = jax.nn.sigmoid(preact)
    return sigmoid_val * (1.0 + preact * (1.0 - sigmoid_val))


def contract_rows(left, right):
    return lax.dot_general(
        left, right, (((0,), (0,)), ((), ())), preferred_element_type=jnp.float32
    )


def halving_orders():
    core_bit = lax.axis_size("patch")
    high = [core_bit << k for k in range(1, (lax.axis_size("region")).bit_length() - 1)]
    low = [1 << k for k in range(core_bit.bit_length() - 1)]
    return core_bit, high + low, low[:-1] + high + low[-1:]


def permute_by(values, first, second, core_bit):
    count = lax.axis_size("region") * lax.axis_size("patch")
    pairs = [(i, i ^ (second if i & core_bit else first)) for i in range(count)]
    return lax.ppermute(values, ("region", "patch"), pairs)


def reduce_all(flat, vectors):
    core_bit, first, second = halving_orders()
    count = lax.axis_size("region") * lax.axis_size("patch")
    me = lax.axis_index(("region", "patch"))
    core = (me & core_bit) // core_bit
    depth = count.bit_length() - 1
    flat = flat.reshape((2,) * depth + (-1, flat.shape[1]))

    def ordered(order):
        axes = [depth - bit.bit_length() for bit in [core_bit] + order]
        return jnp.transpose(flat, axes + [depth, depth + 1])

    blocks = jnp.stack([ordered(first)[0], ordered(second)[1]]).reshape(2, -1, flat.shape[-1])
    kept = lax.dynamic_index_in_dim(blocks, core, 0, keepdims=False)
    sent = lax.dynamic_index_in_dim(blocks, 1 - core, 0, keepdims=False).astype(jnp.bfloat16)
    got = permute_by(sent, core_bit, core_bit, core_bit)
    total = kept + got.astype(jnp.float32)
    for one, two in zip(first, second):
        bit = jnp.where(core == 1, (me & two) // two, (me & one) // one)
        halves = total.reshape(2, -1, flat.shape[-1])
        kept = lax.dynamic_index_in_dim(halves, bit, 0, keepdims=False)
        sent = lax.dynamic_index_in_dim(halves, 1 - bit, 0, keepdims=False).astype(jnp.bfloat16)
        got = permute_by(sent, one, two, core_bit)
        vectors = vectors + permute_by(vectors, one, two, core_bit)
        total = kept + got.astype(jnp.float32)
    vectors = vectors + permute_by(vectors, core_bit, core_bit, core_bit)
    return total.reshape(-1), vectors.reshape(-1)


def per_device(
    nodes,
    edges,
    node_cotan,
    edge_cotan,
    edge_inner,
    edge_outer,
    node_inner,
    node_outer,
    edge_shift,
    edge_offset,
    edge_gain,
    node_shift,
    node_offset,
    node_gain,
    send_rows,
    senders,
    receivers,
):
    node_count = nodes.shape[0]
    edge_count = edges.shape[0]
    feature_width = nodes.shape[1]
    send_lists = send_rows.reshape(-1)
    slot_count = send_lists.shape[0] // 2
    devices_all = lax.axis_size("region") * lax.axis_size("patch")
    edge_norm = 1.0 / math.sqrt(edge_count * devices_all)
    node_norm = 1.0 / math.sqrt(node_count * devices_all)
    node_ids = jnp.arange(node_count, dtype=jnp.int32)
    pick_send = (send_lists[:, None] == node_ids[None, :]).astype(jnp.bfloat16)
    outgoing = jnp.dot(pick_send, nodes, preferred_element_type=jnp.float32).astype(jnp.bfloat16)
    received = extended(outgoing.reshape(2, slot_count, feature_width), (("patch", 0),), 1)
    lookup = jnp.concatenate([nodes, received[0], received[3]], axis=0)
    lookup_ids = jnp.arange(lookup.shape[0], dtype=jnp.int32)
    pick_sender = (senders[:, None] == lookup_ids[None, :]).astype(jnp.bfloat16)
    pick_receiver = (receivers[:, None] == node_ids[None, :]).astype(jnp.bfloat16)
    sender_rows = jnp.dot(pick_sender, lookup, preferred_element_type=jnp.float32).astype(
        jnp.bfloat16
    )
    receiver_rows = jnp.dot(pick_receiver, nodes, preferred_element_type=jnp.float32).astype(
        jnp.bfloat16
    )
    edge_inputs = jnp.concatenate([edges, sender_rows, receiver_rows], axis=1)
    edge_preact = jnp.dot(edge_inputs, edge_inner, preferred_element_type=jnp.float32) + edge_shift
    edge_hidden = jax.nn.silu(edge_preact).astype(jnp.bfloat16)
    edge_linear = jnp.dot(edge_hidden, edge_outer, preferred_element_type=jnp.float32) + edge_offset
    edge_normed, edge_invstd = layer_norm(edge_linear)
    edge_fresh = (edges.astype(jnp.float32) + edge_gain * edge_normed).astype(jnp.bfloat16)
    aggregate = contract_rows(pick_receiver, edge_fresh).astype(jnp.bfloat16)
    node_inputs = jnp.concatenate([nodes, aggregate], axis=1)
    node_preact = jnp.dot(node_inputs, node_inner, preferred_element_type=jnp.float32) + node_shift
    node_hidden = jax.nn.silu(node_preact).astype(jnp.bfloat16)
    node_linear = jnp.dot(node_hidden, node_outer, preferred_element_type=jnp.float32) + node_offset
    node_normed, node_invstd = layer_norm(node_linear)
    cotan_node = node_cotan.astype(jnp.float32)
    linear_back = norm_back(cotan_node, node_normed, node_invstd, node_gain)
    linear_half = linear_back.astype(jnp.bfloat16)
    preact_back = jnp.dot(
        linear_half, node_outer.T, preferred_element_type=jnp.float32
    ) * activation_grad(node_preact)
    preact_half = preact_back.astype(jnp.bfloat16)
    inputs_back = jnp.dot(preact_half, node_inner.T, preferred_element_type=jnp.float32)
    aggregate_half = inputs_back[:, feature_width:].astype(jnp.bfloat16)
    fresh_back = edge_cotan.astype(jnp.float32) + jnp.dot(
        pick_receiver, aggregate_half, preferred_element_type=jnp.float32
    )
    elinear_back = norm_back(fresh_back, edge_normed, edge_invstd, edge_gain)
    elinear_half = elinear_back.astype(jnp.bfloat16)
    epreact_back = jnp.dot(
        elinear_half, edge_outer.T, preferred_element_type=jnp.float32
    ) * activation_grad(edge_preact)
    epreact_half = epreact_back.astype(jnp.bfloat16)
    einputs_back = jnp.dot(epreact_half, edge_inner.T, preferred_element_type=jnp.float32)
    grad_edges = (fresh_back + einputs_back[:, :feature_width]).astype(jnp.bfloat16)
    sender_half = einputs_back[:, feature_width : 2 * feature_width].astype(jnp.bfloat16)
    receiver_half = einputs_back[:, 2 * feature_width :].astype(jnp.bfloat16)
    lookup_back = contract_rows(pick_sender, sender_half)
    rim_back = lookup_back[node_count:].reshape(2, slot_count, feature_width)
    returned = extended(rim_back.astype(jnp.bfloat16), (("patch", 0),), 1).astype(rim_back.dtype)
    back_rows = jnp.concatenate([returned[0], returned[3]], axis=0)
    from_rims = lax.dot_general(
        pick_send.astype(jnp.float32),
        back_rows,
        (((0,), (0,)), ((), ())),
        precision=lax.Precision.HIGHEST,
        preferred_element_type=jnp.float32,
    )
    grad_nodes = (
        cotan_node
        + inputs_back[:, :feature_width]
        + lookup_back[:node_count]
        + contract_rows(pick_receiver, receiver_half)
        + from_rims
    )
    flat_terms = jnp.concatenate(
        [
            contract_rows(edge_inputs, epreact_half) * edge_norm,
            contract_rows(edge_hidden, elinear_half) * edge_norm,
            contract_rows(node_inputs, preact_half) * node_norm,
            contract_rows(node_hidden, linear_half) * node_norm,
        ]
    )
    vector_terms = jnp.concatenate(
        [
            jnp.sum(epreact_back, axis=0) * edge_norm,
            jnp.sum(elinear_back, axis=0) * edge_norm,
            jnp.sum(fresh_back * edge_normed, axis=0) * edge_norm,
            jnp.sum(preact_back, axis=0) * node_norm,
            jnp.sum(linear_back, axis=0) * node_norm,
            jnp.sum(cotan_node * node_normed, axis=0) * node_norm,
        ]
    )
    grad_weights, grad_vectors = reduce_all(flat_terms, vector_terms.reshape(-1, feature_width))
    return (grad_nodes, grad_edges, grad_weights, grad_vectors)


def solution(mesh):
    in_specs = (
        P(("region", "patch"), None),
        P(("region", "patch"), None),
        P(("region", "patch"), None),
        P(("region", "patch"), None),
        P(),
        P(),
        P(),
        P(),
        P(),
        P(),
        P(),
        P(),
        P(),
        P(),
        P("region", "patch", None, None),
        P(("region", "patch")),
        P(("region", "patch")),
    )
    out_specs = (
        P(("region", "patch"), None),
        P(("region", "patch"), None),
        P(("region", "patch")),
        P(),
    )
    return jax.shard_map(
        per_device, mesh=mesh, in_specs=in_specs, out_specs=out_specs, check_vma=False
    )
```

```python
import functools
import math

import jax
import jax.numpy as jnp
from jax import lax
from jax.experimental import pallas as pl
from jax.experimental.pallas import tpu as pltpu
from jax.sharding import PartitionSpec as P

BF = jnp.bfloat16
F32 = jnp.float32
LANES = 128
VMEM = pltpu.VMEM
AXES = ("region", "patch")


def pinned(shape, dtype):
    return pltpu.VMEM(shape, dtype)


def mm(a, b):
    return jnp.dot(a, b, preferred_element_type=F32)


def mm_nt(a, b):
    return lax.dot_general(a, b, (((1,), (1,)), ((), ())), preferred_element_type=F32)


def mm_tn(a, b):
    return lax.dot_general(a, b, (((0,), (0,)), ((), ())), preferred_element_type=F32)


def call(body, outs, *args, scalars=0, flops=0, limit=24 << 20, name=None, outs_plain=()):
    vmem = pl.BlockSpec(memory_space=pltpu.VMEM)
    smem = pl.BlockSpec(memory_space=pltpu.SMEM)
    held = [
        a if i < scalars else pltpu.with_memory_space_constraint(a, pltpu.VMEM)
        for i, a in enumerate(args)
    ]
    shapes = [
        jax.ShapeDtypeStruct(s, d) if i in outs_plain else pinned(s, d)
        for i, (s, d) in enumerate(outs)
    ]
    moved = sum(math.prod(s) * jnp.dtype(d).itemsize for s, d in outs)
    return pl.pallas_call(
        body,
        out_shape=shapes,
        in_specs=[smem if i < scalars else vmem for i in range(len(args))],
        out_specs=[vmem] * len(outs),
        compiler_params=pltpu.CompilerParams(vmem_limit_bytes=limit),
        cost_estimate=pl.CostEstimate(flops=flops, bytes_accessed=moved, transcendentals=0),
        name=name,
    )(*held)


def layer_norm(values):
    centred = values - jnp.mean(values, axis=-1, keepdims=True)
    invstd = lax.rsqrt(jnp.mean(centred * centred, axis=-1, keepdims=True) + 1e-05)
    return centred * invstd, invstd


def norm_back(upstream, normed, invstd, gains):
    scaled = upstream * gains
    return invstd * (
        scaled
        - jnp.mean(scaled, axis=-1, keepdims=True)
        - normed * jnp.mean(scaled * normed, axis=-1, keepdims=True)
    )


def silu_and_slope(preact):
    gate = 1.0 / (1.0 + jnp.exp(-preact))
    hidden = preact * gate
    return hidden, gate + hidden * (1.0 - gate)


def column_sum(values):
    return jnp.sum(values, axis=0, keepdims=True)


def pick_kernel(lists_ref, nodes_ref, out_ref):
    slots, count = lists_ref.shape[1], nodes_ref.shape[0]
    rows = lax.broadcasted_iota(jnp.int32, (count, slots), 0)
    pick = jnp.where(rows == lists_ref[...], 1.0, 0.0).astype(BF)
    out_ref[...] = mm_tn(pick, nodes_ref[...]).astype(BF)


def table_kernel(
    senders_ref, receivers_ref, edges_ref, nodes_ref, inner_ref, shift_ref,
    part_ref, own_ref, pick_ref, turned_ref,
):
    edge_count, width = edges_ref.shape
    count = nodes_ref.shape[0]
    senders = senders_ref[...]
    receivers = receivers_ref[...] + count
    senders = jnp.where(senders < count, senders, senders + count)
    wide_send = jnp.transpose(jnp.broadcast_to(senders, (LANES, edge_count)))
    wide_recv = jnp.transpose(jnp.broadcast_to(receivers, (LANES, edge_count)))
    lane = lax.broadcasted_iota(jnp.int32, (edge_count, LANES), 1)
    row = lax.broadcasted_iota(jnp.int32, (LANES, edge_count), 0)
    for start in range(0, pick_ref.shape[1], LANES):
        own_part = count <= start < 2 * count
        tall = wide_recv if own_part else wide_send
        flat = receivers if own_part else senders
        pick_ref[:, start : start + LANES] = jnp.where(tall == lane + start, 1.0, 0.0).astype(BF)
        turned_ref[start : start + LANES, :] = jnp.where(flat == row + start, 1.0, 0.0).astype(BF)
    nodes = nodes_ref[...]
    own_ref[:count, :] = mm(nodes, inner_ref[width : 2 * width, :]).astype(BF)
    own_ref[count:, :] = mm(nodes, inner_ref[2 * width :, :]).astype(BF)
    tile = edge_count // 4
    for start in range(0, edge_count, tile):
        part_ref[start : start + tile, :] = (
            mm(edges_ref[start : start + tile, :], inner_ref[:width, :]) + shift_ref[...]
        )


def forward_kernel(
    part_ref, own_ref, pick_ref, turned_ref, low_ref, high_ref, edges_ref, nodes_ref, cotan_ref,
    einner_ref, eouter_ref, ninner_ref, nouter_ref, eoffset_ref, egain_ref, nshift_ref, noffset_ref,
    ngain_ref,
    hidden_ref, slope_ref, normed_ref, invstd_ref, pulled_ref, partial_ref, weights_ref, sums_ref,
    *, scale,
):
    edge_count, width = edges_ref.shape
    count = nodes_ref.shape[0]
    rim = jnp.concatenate([low_ref[...], high_ref[...]], axis=0)
    far = mm(rim, einner_ref[width : 2 * width, :]).astype(BF)
    slots = rim.shape[0]
    tile = edge_count // 4
    total = jnp.zeros((count, width), F32)
    for start in range(0, edge_count, tile):
        rows = slice(start, start + tile)
        preact = (
            part_ref[rows, :]
            + mm(pick_ref[rows, : 2 * count], own_ref[...])
            + mm(pick_ref[rows, 2 * count : 2 * count + slots], far)
        )
        hidden, slope = silu_and_slope(preact)
        hidden = hidden.astype(BF)
        hidden_ref[rows, :] = hidden
        slope_ref[rows, :] = slope
        normed, invstd = layer_norm(mm(hidden, eouter_ref[...]) + eoffset_ref[...])
        normed_ref[rows, :] = normed
        invstd_ref[rows, :] = invstd
        fresh = (edges_ref[rows, :].astype(F32) + egain_ref[...] * normed).astype(BF)
        total += mm(turned_ref[count : 2 * count, rows], fresh)
    aggregate = total.astype(BF)
    nodes = nodes_ref[...]
    preact = (
        mm(nodes, ninner_ref[:width, :]) + mm(aggregate, ninner_ref[width:, :]) + nshift_ref[...]
    )
    hidden, slope = silu_and_slope(preact)
    hidden = hidden.astype(BF)
    normed, invstd = layer_norm(mm(hidden, nouter_ref[...]) + noffset_ref[...])
    cotan = cotan_ref[...].astype(F32)
    linear_back = norm_back(cotan, normed, invstd, ngain_ref[...])
    linear_half = linear_back.astype(BF)
    preact_back = mm_nt(linear_half, nouter_ref[...]) * slope
    preact_half = preact_back.astype(BF)
    pulled_ref[...] = mm_nt(preact_half, ninner_ref[width:, :]).astype(BF)
    partial_ref[...] = cotan + mm_nt(preact_half, ninner_ref[:width, :])
    hidden_width = preact.shape[1]
    weights_ref[:width, :] = mm_tn(nodes, preact_half) * scale
    weights_ref[width : 2 * width, :] = mm_tn(aggregate, preact_half) * scale
    weights_ref[2 * width : 2 * width + hidden_width, :] = mm_tn(hidden, linear_half) * scale
    sums_ref[0:1, :] = column_sum(preact_back) * scale
    sums_ref[1:2, :] = column_sum(linear_back) * scale
    sums_ref[2:3, :] = column_sum(cotan * normed) * scale


def backward_kernel(
    pick_ref, turned_ref, edges_ref, ecotan_ref, nodes_ref, low_ref, high_ref, hidden_ref, slope_ref,
    normed_ref, invstd_ref, pulled_ref, eouter_ref, egain_ref,
    fresh_ref, preact_ref, spread_ref, weights_ref, sums_ref,
    linear_ref,
    *, scale,
):
    edge_count, width = edges_ref.shape
    count = nodes_ref.shape[0]
    tile = edge_count // 4
    sums = [0.0, 0.0, 0.0]
    for start in range(0, edge_count, tile):
        rows = slice(start, start + tile)
        fresh_back = ecotan_ref[rows, :].astype(F32) + mm(
            pick_ref[rows, count : 2 * count], pulled_ref[...]
        )
        fresh_ref[rows, :] = fresh_back
        normed = normed_ref[rows, :]
        linear_back = norm_back(fresh_back, normed, invstd_ref[rows, :], egain_ref[...])
        linear_half = linear_back.astype(BF)
        linear_ref[rows, :] = linear_half
        preact_back = mm_nt(linear_half, eouter_ref[...]) * slope_ref[rows, :]
        preact_ref[rows, :] = preact_back.astype(BF)
        sums[0] += column_sum(preact_back)
        sums[1] += column_sum(linear_back)
        sums[2] += column_sum(fresh_back * normed)
    for k in range(3):
        sums_ref[k : k + 1, :] = sums[k] * scale
    used = spread_ref.shape[0]
    spread = mm(turned_ref[:used, :], preact_ref[...]).astype(BF)
    spread_ref[...] = spread
    weights_ref[:width, :] = mm_tn(edges_ref[...], preact_ref[...]) * scale
    rim = jnp.concatenate([low_ref[...], high_ref[...]], axis=0)
    nodes = nodes_ref[...]
    weights_ref[width : 2 * width, :] = (
        mm_tn(nodes, spread[:count]) + mm_tn(rim, spread[2 * count :])
    ) * scale
    weights_ref[2 * width : 3 * width, :] = mm_tn(nodes, spread[count : 2 * count]) * scale
    weights_ref[3 * width :, :] = mm_tn(hidden_ref[...], linear_ref[...]) * scale


def rim_kernel(spread_ref, inner_ref, out_ref, *, count):
    width = spread_ref.shape[1]
    out_ref[...] = mm_nt(spread_ref[2 * count :, :], inner_ref[width : 2 * width, :]).astype(BF)


def grads_kernel(spread_ref, inner_ref, partial_ref, fresh_ref, preact_ref, nodes_ref, edges_ref):
    count, width = partial_ref.shape
    nodes_ref[...] = (
        partial_ref[...]
        + mm_nt(spread_ref[:count, :], inner_ref[width : 2 * width, :])
        + mm_nt(spread_ref[count : 2 * count, :], inner_ref[2 * width :, :])
    )
    edge_count = preact_ref.shape[0]
    tile = edge_count // 4
    for start in range(0, edge_count, tile):
        rows = slice(start, start + tile)
        edges_ref[rows, :] = (
            fresh_ref[rows, :] + mm_nt(preact_ref[rows, :], inner_ref[:width, :])
        ).astype(BF)


def rims_kernel(lists_ref, partial_ref, low_ref, high_ref, out_ref):
    count, slots = partial_ref.shape[0], lists_ref.shape[1]
    rows = lax.broadcasted_iota(jnp.int32, (count, slots), 0)
    pick = jnp.where(rows == lists_ref[...], 1.0, 0.0).astype(BF)
    back = jnp.concatenate([low_ref[...], high_ref[...]], axis=0)
    out_ref[...] = partial_ref[...] + mm(pick, back)


def ring(values, step):
    count = lax.axis_size("patch")
    return lax.ppermute(values, "patch", [(i, (i + step) % count) for i in range(count)])


def halving_orders():
    core_bit = lax.axis_size("patch")
    high = [core_bit << k for k in range(1, lax.axis_size("region").bit_length() - 1)]
    low = [1 << k for k in range(core_bit.bit_length() - 1)]
    return core_bit, high + low, low[:-1] + high + low[-1:]


def permute_by(values, first, second, core_bit):
    count = lax.axis_size("region") * lax.axis_size("patch")
    pairs = [(i, i ^ (second if i & core_bit else first)) for i in range(count)]
    return lax.ppermute(values, AXES, pairs)


def reduce_all(flat, vectors):
    core_bit, first, second = halving_orders()
    count = lax.axis_size("region") * lax.axis_size("patch")
    me = lax.axis_index(AXES)
    core = (me & core_bit) // core_bit
    depth = count.bit_length() - 1
    flat = flat.reshape((2,) * depth + (-1, flat.shape[1]))

    def ordered(order):
        axes = [depth - bit.bit_length() for bit in [core_bit] + order]
        return jnp.transpose(flat, axes + [depth, depth + 1])

    blocks = jnp.stack([ordered(first)[0], ordered(second)[1]]).reshape(2, -1, flat.shape[-1])
    kept = lax.dynamic_index_in_dim(blocks, core, 0, keepdims=False)
    sent = lax.dynamic_index_in_dim(blocks, 1 - core, 0, keepdims=False).astype(BF)
    got = permute_by(sent, core_bit, core_bit, core_bit)
    total = kept + got
    for one, two in zip(first, second):
        bit = jnp.where(core == 1, (me & two) // two, (me & one) // one)
        halves = total.reshape(2, -1, flat.shape[-1])
        kept = lax.dynamic_index_in_dim(halves, bit, 0, keepdims=False)
        sent = lax.dynamic_index_in_dim(halves, 1 - bit, 0, keepdims=False).astype(BF)
        got = permute_by(sent, one, two, core_bit)
        vectors = vectors + permute_by(vectors, one, two, core_bit)
        total = kept + got
    vectors = vectors + permute_by(vectors, core_bit, core_bit, core_bit)
    return total.reshape(-1), vectors.reshape(-1)


def per_device(
    nodes, edges, node_cotan, edge_cotan, edge_inner, edge_outer, node_inner, node_outer, edge_shift,
    edge_offset, edge_gain, node_shift, node_offset, node_gain, send_rows, senders, receivers,
):
    count, width = nodes.shape
    edge_count = edges.shape[0]
    hidden_width = edge_outer.shape[0]
    lists = send_rows.reshape(1, -1)
    slots = lists.shape[1]
    half = slots // 2
    devices_all = lax.axis_size("region") * lax.axis_size("patch")
    edge_norm = 1.0 / math.sqrt(edge_count * devices_all)
    node_norm = 1.0 / math.sqrt(count * devices_all)
    picked = 2 * count + -(-slots // LANES) * LANES
    edge_shift, edge_offset, edge_gain, node_shift, node_offset, node_gain = (
        v.reshape(1, -1)
        for v in (edge_shift, edge_offset, edge_gain, node_shift, node_offset, node_gain)
    )

    (outgoing,) = call(
        pick_kernel, [((slots, width), BF)], lists, nodes, name="pick", limit=4 << 20
    )
    low = ring(outgoing[half:], 1)
    high = ring(outgoing[:half], -1)

    part, own, pick, turned = call(
        table_kernel,
        [
            ((edge_count, hidden_width), F32),
            ((2 * count, hidden_width), BF),
            ((edge_count, picked), BF),
            ((picked, edge_count), BF),
        ],
        senders.reshape(1, -1), receivers.reshape(1, -1), edges, nodes, edge_inner, edge_shift,
        name="table", flops=2 * (edge_count + 2 * count) * width * hidden_width,
    )
    hidden, slope, normed, invstd, pulled, partial, node_weights, node_sums = call(
        functools.partial(forward_kernel, scale=node_norm),
        [
            ((edge_count, hidden_width), BF),
            ((edge_count, hidden_width), F32),
            ((edge_count, width), F32),
            ((edge_count, 1), F32),
            ((count, width), BF),
            ((count, width), F32),
            ((2 * width + hidden_width, hidden_width), F32),
            ((3, width), F32),
        ],
        part, own, pick, turned, low, high, edges, nodes, node_cotan, edge_inner, edge_outer,
        node_inner, node_outer, edge_offset, edge_gain, node_shift, node_offset, node_gain,
        name="forward", flops=5 << 30,
    )
    fresh, preact, spread, edge_weights, edge_sums, _ = call(
        functools.partial(backward_kernel, scale=edge_norm),
        [
            ((edge_count, width), F32),
            ((edge_count, hidden_width), BF),
            ((2 * count + slots, hidden_width), BF),
            ((3 * width + hidden_width, hidden_width), F32),
            ((3, width), F32),
            ((edge_count, width), BF),
        ],
        pick, turned, edges, edge_cotan, nodes, low, high, hidden, slope, normed, invstd, pulled,
        edge_outer, edge_gain,
        name="backward", flops=5 << 30,
    )
    (rim_back,) = call(
        functools.partial(rim_kernel, count=count), [((slots, width), BF)], spread, edge_inner,
        name="rim", limit=4 << 20,
    )
    back_low = ring(rim_back[half:], 1)
    back_high = ring(rim_back[:half], -1)
    grad_weights, grad_vectors = reduce_all(
        jnp.concatenate([edge_weights, node_weights]), jnp.concatenate([edge_sums, node_sums])
    )
    nodes_part, grad_edges = call(
        grads_kernel,
        [((count, width), F32), ((edge_count, width), BF)],
        spread, edge_inner, partial, fresh, preact,
        name="grads", flops=2 << 30, outs_plain=(1,),
    )
    (grad_nodes,) = call(
        rims_kernel, [((count, width), F32)], lists, nodes_part, back_low, back_high, name="rims",
        outs_plain=(0,), limit=4 << 20,
    )
    return (grad_nodes, grad_edges, grad_weights, grad_vectors)


def solution(mesh):
    in_specs = (
        P(AXES, None), P(AXES, None), P(AXES, None), P(AXES, None),
        P(), P(), P(), P(), P(), P(), P(), P(), P(), P(),
        P("region", "patch", None, None), P(AXES), P(AXES),
    )
    out_specs = (P(AXES, None), P(AXES, None), P(AXES), P())
    return jax.shard_map(
        per_device, mesh=mesh, in_specs=in_specs, out_specs=out_specs, check_vma=False
    )
```

```python
import functools
import math

import jax
import jax.numpy as jnp
from jax import lax
from jax.experimental import pallas as pl
from jax.experimental.pallas import tpu as pltpu
from jax.sharding import PartitionSpec as P

BF = jnp.bfloat16
F32 = jnp.float32
LANES = 128
VMEM = pltpu.VMEM
AXES = ("region", "patch")


def pinned(shape, dtype):
    return pltpu.VMEM(shape, dtype)


def mm(a, b):
    return jnp.dot(a, b, preferred_element_type=F32)


def mm_nt(a, b):
    return lax.dot_general(a, b, (((1,), (1,)), ((), ())), preferred_element_type=F32)


def mm_tn(a, b):
    return lax.dot_general(a, b, (((0,), (0,)), ((), ())), preferred_element_type=F32)


def call(body, outs, *args, flops=0, limit=24 << 20, name=None, plain=(), hbm=(), scratch=()):
    vmem = pl.BlockSpec(memory_space=pltpu.VMEM)
    anywhere = pl.BlockSpec(memory_space=pltpu.HBM)
    shapes = [
        jax.ShapeDtypeStruct(s, d) if i in plain else pinned(s, d) for i, (s, d) in enumerate(outs)
    ]
    moved = sum(math.prod(s) * jnp.dtype(d).itemsize for s, d in outs)
    return pl.pallas_call(
        body,
        out_shape=shapes,
        in_specs=[anywhere if i in hbm else vmem for i in range(len(args))],
        out_specs=[vmem] * len(outs),
        scratch_shapes=list(scratch),
        compiler_params=pltpu.CompilerParams(vmem_limit_bytes=limit),
        cost_estimate=pl.CostEstimate(flops=flops, bytes_accessed=moved, transcendentals=0),
        name=name,
    )(*[far(a) if i in hbm else a for i, a in enumerate(args)])


def far(array):
    return pltpu.with_memory_space_constraint(array, pltpu.HBM)


def near(array):
    return pltpu.with_memory_space_constraint(array, pltpu.VMEM)


def start_copies(pairs, sems):
    copies = [pltpu.make_async_copy(a, b, sems.at[i]) for i, (a, b) in enumerate(pairs)]
    for copy in copies:
        copy.start()
    return copies


def layer_norm(values):
    centred = values - jnp.mean(values, axis=-1, keepdims=True)
    invstd = lax.rsqrt(jnp.mean(centred * centred, axis=-1, keepdims=True) + 1e-05)
    return centred * invstd, invstd


def norm_back(upstream, normed, invstd, gains):
    scaled = upstream * gains
    return invstd * (
        scaled
        - jnp.mean(scaled, axis=-1, keepdims=True)
        - normed * jnp.mean(scaled * normed, axis=-1, keepdims=True)
    )


def silu_and_slope(preact):
    gate = 1.0 / (1.0 + jnp.exp(-preact))
    hidden = preact * gate
    return hidden, gate + hidden * (1.0 - gate)


def column_sum(values):
    return jnp.sum(values, axis=0, keepdims=True)


def pick_kernel(lists_hbm, nodes_hbm, low_ref, high_ref, lists_ref, nodes_ref, sems):
    for copy in start_copies([(lists_hbm, lists_ref), (nodes_hbm, nodes_ref)], sems):
        copy.wait()
    slots, count = lists_ref.shape[1], nodes_ref.shape[0]
    rows = lax.broadcasted_iota(jnp.int32, (count, slots), 0)
    for k, out_ref in enumerate((low_ref, high_ref)):
        pick = jnp.where(rows == lists_ref[k : k + 1, :], 1.0, 0.0).astype(BF)
        out_ref[...] = mm_tn(pick, nodes_ref[...]).astype(BF)


def table_kernel(
    *refs, given,
):
    part_ref, own_ref, pick_ref, turned_ref = refs[given : given + 4]
    loaded, sems = refs[given + 4 : -1], refs[-1]
    copies = start_copies(list(zip(refs[:given], loaded)), sems)
    senders_ref, receivers_ref, shift_ref, nodes_ref, inner_ref, edges_ref = loaded[:6]
    copies[0].wait()
    copies[1].wait()
    edge_count, width = edges_ref.shape
    count = nodes_ref.shape[0]
    senders = senders_ref[...]
    receivers = receivers_ref[...] + count
    senders = jnp.where(senders < count, senders, senders + count)
    wide_send = jnp.transpose(jnp.broadcast_to(senders, (LANES, edge_count)))
    wide_recv = jnp.transpose(jnp.broadcast_to(receivers, (LANES, edge_count)))
    lane = lax.broadcasted_iota(jnp.int32, (edge_count, LANES), 1)
    row = lax.broadcasted_iota(jnp.int32, (LANES, edge_count), 0)
    for start in range(0, pick_ref.shape[1], LANES):
        own_part = count <= start < 2 * count
        tall = wide_recv if own_part else wide_send
        flat = receivers if own_part else senders
        pick_ref[:, start : start + LANES] = jnp.where(tall == lane + start, 1.0, 0.0).astype(BF)
        turned_ref[start : start + LANES, :] = jnp.where(flat == row + start, 1.0, 0.0).astype(BF)
    copies[3].wait()
    copies[4].wait()
    nodes = nodes_ref[...]
    own_ref[:count, :] = mm(nodes, inner_ref[width : 2 * width, :]).astype(BF)
    own_ref[count:, :] = mm(nodes, inner_ref[2 * width :, :]).astype(BF)
    copies[2].wait()
    copies[5].wait()
    tile = edge_count // 4
    for start in range(0, edge_count, tile):
        part_ref[start : start + tile, :] = (
            mm(edges_ref[start : start + tile, :], inner_ref[:width, :]) + shift_ref[...]
        )
    for copy in copies[6:]:
        copy.wait()


def forward_kernel(
    part_ref, own_ref, pick_ref, turned_ref, low_ref, high_ref, edges_ref, nodes_ref,
    einner_ref, eouter_ref, eoffset_ref, egain_ref, nshift_ref, noffset_ref, ngain_ref,
    ninner_hbm, nouter_hbm, cotan_hbm, ecotan_hbm,
    hidden_ref, slope_ref, normed_ref, invstd_ref, pulled_ref, partial_ref, weights_ref, sums_ref,
    ecotan_ref, ninner_ref, nouter_ref, cotan_ref, sems,
    *, scale,
):
    copies = start_copies(
        [
            (ninner_hbm, ninner_ref), (nouter_hbm, nouter_ref), (cotan_hbm, cotan_ref),
            (ecotan_hbm, ecotan_ref),
        ],
        sems,
    )
    edge_count, width = edges_ref.shape
    count = nodes_ref.shape[0]
    rim = jnp.concatenate([low_ref[...], high_ref[...]], axis=0)
    far = mm(rim, einner_ref[width : 2 * width, :]).astype(BF)
    slots = rim.shape[0]
    tile = edge_count // 4
    total = jnp.zeros((count, width), F32)
    for start in range(0, edge_count, tile):
        rows = slice(start, start + tile)
        preact = (
            part_ref[rows, :]
            + mm(pick_ref[rows, : 2 * count], own_ref[...])
            + mm(pick_ref[rows, 2 * count : 2 * count + slots], far)
        )
        hidden, slope = silu_and_slope(preact)
        hidden = hidden.astype(BF)
        hidden_ref[rows, :] = hidden
        slope_ref[rows, :] = slope
        normed, invstd = layer_norm(mm(hidden, eouter_ref[...]) + eoffset_ref[...])
        normed_ref[rows, :] = normed
        invstd_ref[rows, :] = invstd
        fresh = (edges_ref[rows, :].astype(F32) + egain_ref[...] * normed).astype(BF)
        total += mm(turned_ref[count : 2 * count, rows], fresh)
    aggregate = total.astype(BF)
    for copy in copies:
        copy.wait()
    nodes = nodes_ref[...]
    preact = (
        mm(nodes, ninner_ref[:width, :]) + mm(aggregate, ninner_ref[width:, :]) + nshift_ref[...]
    )
    hidden, slope = silu_and_slope(preact)
    hidden = hidden.astype(BF)
    normed, invstd = layer_norm(mm(hidden, nouter_ref[...]) + noffset_ref[...])
    cotan = cotan_ref[...].astype(F32)
    linear_back = norm_back(cotan, normed, invstd, ngain_ref[...])
    linear_half = linear_back.astype(BF)
    preact_back = mm_nt(linear_half, nouter_ref[...]) * slope
    preact_half = preact_back.astype(BF)
    pulled_ref[...] = mm_nt(preact_half, ninner_ref[width:, :]).astype(BF)
    partial_ref[...] = cotan + mm_nt(preact_half, ninner_ref[:width, :])
    hidden_width = preact.shape[1]
    weights_ref[:width, :] = mm_tn(nodes, preact_half) * scale
    weights_ref[width : 2 * width, :] = mm_tn(aggregate, preact_half) * scale
    weights_ref[2 * width :, :] = mm_tn(hidden, linear_half) * scale
    sums_ref[0:1, :] = column_sum(preact_back) * scale
    sums_ref[1:2, :] = column_sum(linear_back) * scale
    sums_ref[2:3, :] = column_sum(cotan * normed) * scale


def backward_kernel(
    pick_ref, turned_ref, edges_ref, ecotan_ref, nodes_ref, low_ref, high_ref, hidden_ref, slope_ref,
    normed_ref, invstd_ref, pulled_ref, eouter_ref, egain_ref, node_sums_ref, node_weights_ref,
    fresh_ref, preact_ref, spread_ref, weights_ref, sums_ref, *rest, scale, split,
):
    linear_ref = rest[-1]
    weights_ref[weights_ref.shape[0] - node_weights_ref.shape[0] :, :] = node_weights_ref[...]
    edge_count, width = edges_ref.shape
    count = nodes_ref.shape[0]
    tile = edge_count // 4
    sums = [0.0, 0.0, 0.0]
    for start in range(0, edge_count, tile):
        rows = slice(start, start + tile)
        fresh_back = ecotan_ref[rows, :].astype(F32) + mm(
            pick_ref[rows, count : 2 * count], pulled_ref[...]
        )
        fresh_ref[rows, :] = fresh_back
        normed = normed_ref[rows, :]
        linear_back = norm_back(fresh_back, normed, invstd_ref[rows, :], egain_ref[...])
        linear_half = linear_back.astype(BF)
        linear_ref[rows, :] = linear_half
        preact_back = mm_nt(linear_half, eouter_ref[...]) * slope_ref[rows, :]
        preact_ref[rows, :] = preact_back.astype(BF)
        sums[0] += column_sum(preact_back)
        sums[1] += column_sum(linear_back)
        sums[2] += column_sum(fresh_back * normed)
    for k in range(3):
        sums_ref[k : k + 1, :] = sums[k] * scale
    sums_ref[3:, :] = node_sums_ref[...]
    used = spread_ref.shape[0]
    spread = mm(turned_ref[:used, :], preact_ref[...]).astype(BF)
    spread_ref[...] = spread
    weights_ref[:width, :] = mm_tn(edges_ref[...], preact_ref[...]) * scale
    rim = jnp.concatenate([low_ref[...], high_ref[...]], axis=0)
    nodes = nodes_ref[...]
    weights_ref[width : 2 * width, :] = (
        mm_tn(nodes, spread[:count]) + mm_tn(rim, spread[2 * count :])
    ) * scale
    weights_ref[2 * width : 3 * width, :] = mm_tn(nodes, spread[count : 2 * count]) * scale
    weights_ref[3 * width : 3 * width + hidden_ref.shape[1], :] = (
        mm_tn(hidden_ref[...], linear_ref[...]) * scale
    )
    if split is not None:
        split.first_send(weights_ref, rest[0])


def rim_kernel(spread_ref, inner_ref, _, low_ref, high_ref, *, count):
    width, slots = spread_ref.shape[1], low_ref.shape[0]
    for k, out_ref in enumerate((low_ref, high_ref)):
        start = 2 * count + k * slots
        out_ref[...] = mm_nt(
            spread_ref[start : start + slots, :], inner_ref[width : 2 * width, :]
        ).astype(BF)


def grads_kernel(spread_ref, inner_ref, partial_ref, fresh_ref, preact_ref, _, nodes_ref, edges_ref):
    count, width = partial_ref.shape
    nodes_ref[...] = (
        partial_ref[...]
        + mm_nt(spread_ref[:count, :], inner_ref[width : 2 * width, :])
        + mm_nt(spread_ref[count : 2 * count, :], inner_ref[2 * width :, :])
    )
    edge_count = preact_ref.shape[0]
    tile = edge_count // 4
    for start in range(0, edge_count, tile):
        rows = slice(start, start + tile)
        edges_ref[rows, :] = (
            fresh_ref[rows, :] + mm_nt(preact_ref[rows, :], inner_ref[:width, :])
        ).astype(BF)


def rims_kernel(lists_ref, partial_ref, low_ref, high_ref, out_ref):
    count, slots = partial_ref.shape[0], lists_ref.shape[1]
    rows = lax.broadcasted_iota(jnp.int32, (count, slots), 0)
    total = partial_ref[...]
    for k, back_ref in enumerate((low_ref, high_ref)):
        pick = jnp.where(rows == lists_ref[k : k + 1, :], 1.0, 0.0).astype(BF)
        total += mm(pick, back_ref[...])
    out_ref[...] = total


def ring(values, step):
    count = lax.axis_size("patch")
    return lax.ppermute(values, "patch", [(i, (i + step) % count) for i in range(count)])


def halving_orders():
    core_bit = lax.axis_size("patch")
    high = [core_bit << k for k in range(1, lax.axis_size("region").bit_length() - 1)]
    low = [1 << k for k in range(core_bit.bit_length() - 1)]
    return core_bit, high + low, low[:-1] + high + low[-1:]


def permute_by(values, first, second, core_bit):
    count = lax.axis_size("region") * lax.axis_size("patch")
    pairs = [(i, i ^ (second if i & core_bit else first)) for i in range(count)]
    return lax.ppermute(values, AXES, pairs)


def reduce_all(flat, vectors):
    core_bit, first, second = halving_orders()
    count = lax.axis_size("region") * lax.axis_size("patch")
    me = lax.axis_index(AXES)
    core = (me & core_bit) // core_bit
    depth = count.bit_length() - 1
    flat = flat.reshape((2,) * depth + (-1, flat.shape[1]))

    def ordered(order):
        axes = [depth - bit.bit_length() for bit in [core_bit] + order]
        return jnp.transpose(flat, axes + [depth, depth + 1])

    blocks = jnp.stack([ordered(first)[0], ordered(second)[1]]).reshape(2, -1, flat.shape[-1])
    kept = lax.dynamic_index_in_dim(blocks, core, 0, keepdims=False)
    sent = lax.dynamic_index_in_dim(blocks, 1 - core, 0, keepdims=False).astype(BF)
    got = permute_by(sent, core_bit, core_bit, core_bit)
    total = kept + got
    for one, two in zip(first, second):
        bit = jnp.where(core == 1, (me & two) // two, (me & one) // one)
        halves = total.reshape(2, -1, flat.shape[-1])
        kept = lax.dynamic_index_in_dim(halves, bit, 0, keepdims=False)
        sent = lax.dynamic_index_in_dim(halves, 1 - bit, 0, keepdims=False).astype(BF)
        got = permute_by(sent, one, two, core_bit)
        vectors = vectors + permute_by(vectors, one, two, core_bit)
        total = kept + got
    vectors = vectors + permute_by(vectors, core_bit, core_bit, core_bit)
    return total.reshape(-1), vectors.reshape(-1)


class Halving:
    def __init__(self, rows):
        self.core_bit, self.first, self.second = halving_orders()
        self.count = lax.axis_size("region") * lax.axis_size("patch")
        self.block = rows // self.count
        self.rows = rows // 2
        self.steps = len(self.first)
        self.aligned = rows % (16 * self.count) == 0

    def place(self, order, core, position):
        block = self.core_bit if core else 0
        for k, bit in enumerate(order):
            if (position >> (self.steps - 1 - k)) & 1:
                block |= bit
        return block * self.block

    def me(self):
        return lax.axis_index("region") * self.core_bit + lax.axis_index("patch")

    def core(self):
        return lax.rem(self.me() // self.core_bit, 2)

    def bit(self, step):
        me = self.me()
        one, two = self.first[step], self.second[step]
        return jnp.where(self.core() == 1, lax.rem(me // two, 2), lax.rem(me // one, 2))

    def source(self, position, core):
        zero, one = self.place(self.first, 0, position), self.place(self.second, 1, position)
        return pl.multiple_of(jnp.where(core == 1, one, zero), 8)

    def first_send(self, weights_ref, send_ref):
        other = 1 - self.core()
        for position in range(self.count // 2):
            start = position * self.block
            send_ref[start : start + self.block, :] = weights_ref[
                pl.ds(self.source(position, other), self.block), :
            ].astype(BF)


def halve_kernel(src_ref, got_ref, out_ref, *, plan, step, side):
    half = plan.rows >> (step + 1)
    bit = plan.bit(step)
    chosen = 1 - bit if side else bit
    if step:
        start = pl.multiple_of(chosen * half, 16)
        held = src_ref[pl.ds(start, half), :]
        out_ref[:half, :] = (held + got_ref[pl.ds(start, half), :]).astype(out_ref.dtype)
        return
    core = plan.core()
    per_half = half // plan.block
    for k in range(per_half):
        low, high = plan.source(k, core), plan.source(k + per_half, core)
        held = src_ref[pl.ds(pl.multiple_of(jnp.where(chosen == 1, high, low), 8), plan.block), :]
        start = pl.multiple_of(chosen * half + k * plan.block, 16)
        got = got_ref[pl.ds(start, plan.block), :]
        out_ref[k * plan.block : (k + 1) * plan.block, :] = (held + got).astype(out_ref.dtype)


def vector_parts(ref, start, count):
    return ref[start : start + count, :].astype(F32) + ref[start + 8 : start + 8 + count, :].astype(F32)


def send_kernel(src_ref, got_ref, vec_ref, out_ref, new_ref, *, plan, step):
    halve_kernel(src_ref, got_ref, out_ref, plan=plan, step=step, side=1)
    half = plan.rows >> (step + 1)
    count = vec_ref.shape[0]
    vec = vec_ref[...]
    if step:
        vec = vec + vector_parts(got_ref, 2 * half, count)
    upper = vec.astype(BF)
    lower = (vec - upper.astype(F32)).astype(BF)
    out_ref[half:, :] = jnp.zeros_like(out_ref[half:, :])
    out_ref[half : half + count, :] = upper
    out_ref[half + 8 : half + 8 + count, :] = lower
    new_ref[...] = upper.astype(F32) + lower.astype(F32)


def last_kernel(src_ref, got_ref, vec_ref, out_ref, new_ref):
    rows, width = src_ref.shape
    total = src_ref[...] + got_ref[:rows, :]
    parts = width // LANES
    for k in range(parts):
        out_ref[pl.ds(k, rows, stride=parts), :] = total[:, k * LANES : (k + 1) * LANES]
    new_ref[...] = vec_ref[...] + vector_parts(got_ref, rows, vec_ref.shape[0])


def reduce_kernels(plan, held, sent, vec):
    width = held.shape[1]
    vec_shape = (vec.shape, F32)
    got = permute_by(sent, plan.core_bit, plan.core_bit, plan.core_bit)
    marks = []
    for step in range(plan.steps):
        half = plan.rows >> (step + 1)
        send, vec = call(
            functools.partial(send_kernel, plan=plan, step=step),
            [((half + 16, width), BF), vec_shape], near(held), near(got), near(vec), name=f"send{step}",
        )
        marks.append(send)
        held_late, got_late, send = lax.optimization_barrier((held, got, send))
        incoming = permute_by(send, plan.first[step], plan.second[step], plan.core_bit)
        (held,) = call(
            functools.partial(halve_kernel, plan=plan, step=step, side=0),
            [((half, width), F32)], near(held_late), near(got_late), name=f"keep{step}",
        )
        got = incoming
    out, vec = call(
        last_kernel, [((plan.block * width // LANES, LANES), F32), vec_shape], near(held), near(got),
        near(vec), name="last", plain=(0,),
    )
    vec = vec + permute_by(vec, plan.core_bit, plan.core_bit, plan.core_bit)
    return out.reshape(-1), vec.reshape(-1), marks


def per_device(
    nodes, edges, node_cotan, edge_cotan, edge_inner, edge_outer, node_inner, node_outer, edge_shift,
    edge_offset, edge_gain, node_shift, node_offset, node_gain, send_rows, senders, receivers,
):
    count, width = nodes.shape
    edge_count = edges.shape[0]
    hidden_width = edge_outer.shape[0]
    lists = send_rows.reshape(send_rows.shape[2:])
    half = lists.shape[1]
    slots = 2 * half
    devices_all = lax.axis_size("region") * lax.axis_size("patch")
    edge_norm = 1.0 / math.sqrt(edge_count * devices_all)
    node_norm = 1.0 / math.sqrt(count * devices_all)
    picked = 2 * count + -(-slots // LANES) * LANES
    edge_rows = 3 * width + hidden_width
    weight_rows = edge_rows + 2 * width + hidden_width
    plan = Halving(weight_rows)
    edge_shift, edge_offset, edge_gain, node_shift, node_offset, node_gain = (
        v.reshape(1, -1)
        for v in (edge_shift, edge_offset, edge_gain, node_shift, node_offset, node_gain)
    )

    out_low, out_high = call(
        pick_kernel, [((half, width), BF)] * 2, lists, nodes, name="pick", limit=4 << 20, hbm=(0, 1),
        scratch=[
            pltpu.VMEM(lists.shape, jnp.int32), pltpu.VMEM(nodes.shape, BF),
            pltpu.SemaphoreType.DMA((2,)),
        ],
    )
    low = ring(out_high, 1)
    high = ring(out_low, -1)

    given = [
        senders.reshape(1, -1), receivers.reshape(1, -1), edge_shift, nodes, edge_inner, edges,
        edge_outer, edge_offset, edge_gain, node_shift, node_offset, node_gain,
    ]
    part, own, pick, turned, *loaded = call(
        functools.partial(table_kernel, given=len(given)),
        [
            ((edge_count, hidden_width), F32),
            ((2 * count, hidden_width), BF),
            ((edge_count, picked), BF),
            ((picked, edge_count), BF),
        ] + [(a.shape, a.dtype) for a in given],
        *given, name="table", flops=2 * (edge_count + 2 * count) * width * hidden_width,
        hbm=range(len(given)), scratch=[pltpu.SemaphoreType.DMA((len(given),))],
    )
    nodes_near, inner_near, edges_near, outer_near, *vectors = loaded[3:]
    gain_near = vectors[1]
    hidden, slope, normed, invstd, pulled, partial, node_weights, node_sums, ecotan_near = call(
        functools.partial(forward_kernel, scale=node_norm),
        [
            ((edge_count, hidden_width), BF),
            ((edge_count, hidden_width), F32),
            ((edge_count, width), F32),
            ((edge_count, 1), F32),
            ((count, width), BF),
            ((count, width), F32),
            ((weight_rows - edge_rows, hidden_width), F32),
            ((3, width), F32),
            ((edge_count, width), BF),
        ],
        near(part), near(own), near(pick), near(turned), near(low), near(high), near(edges_near),
        near(nodes_near), near(inner_near), near(outer_near),
        *[near(v) for v in vectors],
        node_inner, node_outer, node_cotan, edge_cotan,
        name="forward", flops=5 << 30, hbm=(15, 16, 17, 18),
        scratch=[
            pltpu.VMEM(node_inner.shape, BF), pltpu.VMEM(node_outer.shape, BF),
            pltpu.VMEM(node_cotan.shape, BF), pltpu.SemaphoreType.DMA((4,)),
        ],
    )
    sends = [((plan.rows, hidden_width), BF)] if plan.aligned else []
    fresh, preact, spread, weights, sums, *sent = call(
        functools.partial(backward_kernel, scale=edge_norm, split=plan if plan.aligned else None),
        [
            ((edge_count, width), F32),
            ((edge_count, hidden_width), BF),
            ((2 * count + slots, hidden_width), BF),
            ((weight_rows, hidden_width), F32),
            ((6, width), F32),
            *sends,
        ],
        near(pick), near(turned), near(edges_near), near(ecotan_near), near(nodes_near), near(low),
        near(high), near(hidden), near(slope), near(normed), near(invstd), near(pulled),
        near(outer_near), near(gain_near), near(node_sums), near(node_weights),
        name="backward", flops=5 << 30,
        scratch=[pltpu.VMEM((edge_count, width), BF)],
    )
    if plan.aligned:
        grad_weights, grad_vectors, marks = reduce_kernels(plan, weights, sent[0], sums)
        mark = marks[0]
    else:
        grad_weights, grad_vectors = reduce_all(weights, sums)
        mark = sums
    rim_low, rim_high = call(
        functools.partial(rim_kernel, count=count), [((half, width), BF)] * 2, near(spread),
        near(inner_near), near(mark), name="rim", limit=4 << 20,
    )
    back_low = ring(rim_high, 1)
    back_high = ring(rim_low, -1)
    nodes_part, grad_edges = call(
        grads_kernel,
        [((count, width), F32), ((edge_count, width), BF)],
        near(spread), near(inner_near), near(partial), near(fresh), near(preact), near(mark),
        name="grads", flops=2 << 30, plain=(1,),
    )
    (grad_nodes,) = call(
        rims_kernel, [((count, width), F32)], lists, near(nodes_part), near(back_low),
        near(back_high), name="rims", plain=(0,), limit=4 << 20,
    )
    return (grad_nodes, grad_edges, grad_weights, grad_vectors)


def solution(mesh):
    in_specs = (
        P(AXES, None), P(AXES, None), P(AXES, None), P(AXES, None),
        P(), P(), P(), P(), P(), P(), P(), P(), P(), P(),
        P("region", "patch", None, None), P(AXES), P(AXES),
    )
    out_specs = (P(AXES, None), P(AXES, None), P(AXES), P())
    return jax.shard_map(
        per_device, mesh=mesh, in_specs=in_specs, out_specs=out_specs, check_vma=False
    )
```

```python
import functools
import math

import jax
import jax.numpy as jnp
from jax import lax
from jax.experimental import pallas as pl
from jax.experimental.pallas import tpu as pltpu
from jax.sharding import PartitionSpec as P

BF = jnp.bfloat16
F32 = jnp.float32
LANES = 128
VMEM = pltpu.VMEM
AXES = ("region", "patch")


def pinned(shape, dtype):
    return pltpu.VMEM(shape, dtype)


def mm(a, b):
    return jnp.dot(a, b, preferred_element_type=F32)


def mm_nt(a, b):
    return lax.dot_general(a, b, (((1,), (1,)), ((), ())), preferred_element_type=F32)


def mm_tn(a, b):
    return lax.dot_general(a, b, (((0,), (0,)), ((), ())), preferred_element_type=F32)


def call(body, outs, *args, flops=0, limit=24 << 20, name=None, plain=(), hbm=(), scratch=()):
    vmem = pl.BlockSpec(memory_space=pltpu.VMEM)
    anywhere = pl.BlockSpec(memory_space=pltpu.HBM)
    shapes = [
        jax.ShapeDtypeStruct(s, d) if i in plain else pinned(s, d) for i, (s, d) in enumerate(outs)
    ]
    moved = sum(math.prod(s) * jnp.dtype(d).itemsize for s, d in outs)
    return pl.pallas_call(
        body,
        out_shape=shapes,
        in_specs=[anywhere if i in hbm else vmem for i in range(len(args))],
        out_specs=[vmem] * len(outs),
        scratch_shapes=list(scratch),
        compiler_params=pltpu.CompilerParams(vmem_limit_bytes=limit),
        cost_estimate=pl.CostEstimate(flops=flops, bytes_accessed=moved, transcendentals=0),
        name=name,
    )(*[far(a) if i in hbm else a for i, a in enumerate(args)])


def far(array):
    return pltpu.with_memory_space_constraint(array, pltpu.HBM)


def near(array):
    return pltpu.with_memory_space_constraint(array, pltpu.VMEM)


def start_copies(pairs, sems):
    copies = [pltpu.make_async_copy(a, b, sems.at[i]) for i, (a, b) in enumerate(pairs)]
    for copy in copies:
        copy.start()
    return copies


def layer_norm(values):
    centred = values - jnp.mean(values, axis=-1, keepdims=True)
    invstd = lax.rsqrt(jnp.mean(centred * centred, axis=-1, keepdims=True) + 1e-05)
    return centred * invstd, invstd


def norm_back(upstream, normed, invstd, gains):
    scaled = upstream * gains
    return invstd * (
        scaled
        - jnp.mean(scaled, axis=-1, keepdims=True)
        - normed * jnp.mean(scaled * normed, axis=-1, keepdims=True)
    )


def silu_and_slope(preact):
    gate = 1.0 / (1.0 + jnp.exp(-preact))
    hidden = preact * gate
    return hidden, gate + hidden * (1.0 - gate)


def column_sum(values):
    return jnp.sum(values, axis=0, keepdims=True)


def pick_kernel(lists_hbm, nodes_hbm, low_ref, high_ref, lists_ref, nodes_ref, sems):
    for copy in start_copies([(lists_hbm, lists_ref), (nodes_hbm, nodes_ref)], sems):
        copy.wait()
    slots, count = lists_ref.shape[1], nodes_ref.shape[0]
    rows = lax.broadcasted_iota(jnp.int32, (count, slots), 0)
    for k, out_ref in enumerate((low_ref, high_ref)):
        pick = jnp.where(rows == lists_ref[k : k + 1, :], 1.0, 0.0).astype(BF)
        out_ref[...] = mm_tn(pick, nodes_ref[...]).astype(BF)


def table_kernel(
    senders_ref, receivers_ref, shift_ref, nodes_ref, inner_ref, edges_ref,
    part_ref, own_ref, pick_ref, turned_ref,
):
    edge_count, width = edges_ref.shape
    count = nodes_ref.shape[0]
    senders = senders_ref[...]
    receivers = receivers_ref[...] + count
    senders = jnp.where(senders < count, senders, senders + count)
    wide_send = jnp.transpose(jnp.broadcast_to(senders, (LANES, edge_count)))
    wide_recv = jnp.transpose(jnp.broadcast_to(receivers, (LANES, edge_count)))
    lane = lax.broadcasted_iota(jnp.int32, (edge_count, LANES), 1)
    row = lax.broadcasted_iota(jnp.int32, (LANES, edge_count), 0)
    for start in range(0, pick_ref.shape[1], LANES):
        own_part = count <= start < 2 * count
        tall = wide_recv if own_part else wide_send
        flat = receivers if own_part else senders
        pick_ref[:, start : start + LANES] = jnp.where(tall == lane + start, 1.0, 0.0).astype(BF)
        turned_ref[start : start + LANES, :] = jnp.where(flat == row + start, 1.0, 0.0).astype(BF)
    nodes = nodes_ref[...]
    own_ref[:count, :] = mm(nodes, inner_ref[width : 2 * width, :]).astype(BF)
    own_ref[count:, :] = mm(nodes, inner_ref[2 * width :, :]).astype(BF)
    tile = edge_count // 4
    for start in range(0, edge_count, tile):
        part_ref[start : start + tile, :] = (
            mm(edges_ref[start : start + tile, :], inner_ref[:width, :]) + shift_ref[...]
        )


def forward_kernel(
    part_ref, own_ref, pick_ref, turned_ref, low_ref, high_ref, edges_ref, nodes_ref,
    einner_ref, eouter_ref, eoffset_ref, egain_ref, nshift_ref, noffset_ref, ngain_ref,
    ninner_ref, nouter_ref, cotan_ref,
    hidden_ref, slope_ref, normed_ref, invstd_ref, pulled_ref, partial_ref, weights_ref, sums_ref,
    *, scale,
):
    edge_count, width = edges_ref.shape
    count = nodes_ref.shape[0]
    rim = jnp.concatenate([low_ref[...], high_ref[...]], axis=0)
    far = mm(rim, einner_ref[width : 2 * width, :]).astype(BF)
    slots = rim.shape[0]
    tile = edge_count // 4
    total = jnp.zeros((count, width), F32)
    for start in range(0, edge_count, tile):
        rows = slice(start, start + tile)
        preact = (
            part_ref[rows, :]
            + mm(pick_ref[rows, : 2 * count], own_ref[...])
            + mm(pick_ref[rows, 2 * count : 2 * count + slots], far)
        )
        hidden, slope = silu_and_slope(preact)
        hidden = hidden.astype(BF)
        hidden_ref[rows, :] = hidden
        slope_ref[rows, :] = slope
        normed, invstd = layer_norm(mm(hidden, eouter_ref[...]) + eoffset_ref[...])
        normed_ref[rows, :] = normed
        invstd_ref[rows, :] = invstd
        fresh = (edges_ref[rows, :].astype(F32) + egain_ref[...] * normed).astype(BF)
        total += mm(turned_ref[count : 2 * count, rows], fresh)
    aggregate = total.astype(BF)
    nodes = nodes_ref[...]
    preact = (
        mm(nodes, ninner_ref[:width, :]) + mm(aggregate, ninner_ref[width:, :]) + nshift_ref[...]
    )
    hidden, slope = silu_and_slope(preact)
    hidden = hidden.astype(BF)
    normed, invstd = layer_norm(mm(hidden, nouter_ref[...]) + noffset_ref[...])
    cotan = cotan_ref[...].astype(F32)
    linear_back = norm_back(cotan, normed, invstd, ngain_ref[...])
    linear_half = linear_back.astype(BF)
    preact_back = mm_nt(linear_half, nouter_ref[...]) * slope
    preact_half = preact_back.astype(BF)
    pulled_ref[...] = mm_nt(preact_half, ninner_ref[width:, :]).astype(BF)
    partial_ref[...] = cotan + mm_nt(preact_half, ninner_ref[:width, :])
    hidden_width = preact.shape[1]
    weights_ref[:width, :] = mm_tn(nodes, preact_half) * scale
    weights_ref[width : 2 * width, :] = mm_tn(aggregate, preact_half) * scale
    weights_ref[2 * width :, :] = mm_tn(hidden, linear_half) * scale
    sums_ref[0:1, :] = column_sum(preact_back) * scale
    sums_ref[1:2, :] = column_sum(linear_back) * scale
    sums_ref[2:3, :] = column_sum(cotan * normed) * scale


def backward_kernel(
    pick_ref, turned_ref, edges_ref, ecotan_ref, nodes_ref, low_ref, high_ref, hidden_ref, slope_ref,
    normed_ref, invstd_ref, pulled_ref, eouter_ref, egain_ref, node_sums_ref, node_weights_ref,
    fresh_ref, preact_ref, spread_ref, weights_ref, sums_ref, linear_ref, *, scale,
):
    weights_ref[weights_ref.shape[0] - node_weights_ref.shape[0] :, :] = node_weights_ref[...]
    edge_count, width = edges_ref.shape
    count = nodes_ref.shape[0]
    tile = edge_count // 4
    sums = [0.0, 0.0, 0.0]
    for start in range(0, edge_count, tile):
        rows = slice(start, start + tile)
        fresh_back = ecotan_ref[rows, :].astype(F32) + mm(
            pick_ref[rows, count : 2 * count], pulled_ref[...]
        )
        fresh_ref[rows, :] = fresh_back
        normed = normed_ref[rows, :]
        linear_back = norm_back(fresh_back, normed, invstd_ref[rows, :], egain_ref[...])
        linear_half = linear_back.astype(BF)
        linear_ref[rows, :] = linear_half
        preact_back = mm_nt(linear_half, eouter_ref[...]) * slope_ref[rows, :]
        preact_ref[rows, :] = preact_back.astype(BF)
        sums[0] += column_sum(preact_back)
        sums[1] += column_sum(linear_back)
        sums[2] += column_sum(fresh_back * normed)
    for k in range(3):
        sums_ref[k : k + 1, :] = sums[k] * scale
    sums_ref[3:, :] = node_sums_ref[...]
    used = spread_ref.shape[0]
    spread = mm(turned_ref[:used, :], preact_ref[...]).astype(BF)
    spread_ref[...] = spread
    weights_ref[:width, :] = mm_tn(edges_ref[...], preact_ref[...]) * scale
    rim = jnp.concatenate([low_ref[...], high_ref[...]], axis=0)
    nodes = nodes_ref[...]
    weights_ref[width : 2 * width, :] = (
        mm_tn(nodes, spread[:count]) + mm_tn(rim, spread[2 * count :])
    ) * scale
    weights_ref[2 * width : 3 * width, :] = mm_tn(nodes, spread[count : 2 * count]) * scale
    weights_ref[3 * width : 3 * width + hidden_ref.shape[1], :] = (
        mm_tn(hidden_ref[...], linear_ref[...]) * scale
    )


def rim_kernel(spread_ref, inner_ref, low_ref, high_ref, *, count):
    width, slots = spread_ref.shape[1], low_ref.shape[0]
    for k, out_ref in enumerate((low_ref, high_ref)):
        start = 2 * count + k * slots
        out_ref[...] = mm_nt(
            spread_ref[start : start + slots, :], inner_ref[width : 2 * width, :]
        ).astype(BF)


def grads_kernel(spread_ref, inner_ref, partial_ref, fresh_ref, preact_ref, nodes_ref, edges_ref):
    count, width = partial_ref.shape
    nodes_ref[...] = (
        partial_ref[...]
        + mm_nt(spread_ref[:count, :], inner_ref[width : 2 * width, :])
        + mm_nt(spread_ref[count : 2 * count, :], inner_ref[2 * width :, :])
    )
    edge_count = preact_ref.shape[0]
    tile = edge_count // 4
    for start in range(0, edge_count, tile):
        rows = slice(start, start + tile)
        edges_ref[rows, :] = (
            fresh_ref[rows, :] + mm_nt(preact_ref[rows, :], inner_ref[:width, :])
        ).astype(BF)


def rims_kernel(lists_ref, partial_ref, low_ref, high_ref, out_ref):
    count, slots = partial_ref.shape[0], lists_ref.shape[1]
    rows = lax.broadcasted_iota(jnp.int32, (count, slots), 0)
    total = partial_ref[...]
    for k, back_ref in enumerate((low_ref, high_ref)):
        pick = jnp.where(rows == lists_ref[k : k + 1, :], 1.0, 0.0).astype(BF)
        total += mm(pick, back_ref[...])
    out_ref[...] = total


def ring(values, step):
    count = lax.axis_size("patch")
    return lax.ppermute(values, "patch", [(i, (i + step) % count) for i in range(count)])


def halving_orders():
    core_bit = lax.axis_size("patch")
    high = [core_bit << k for k in range(1, lax.axis_size("region").bit_length() - 1)]
    low = [1 << k for k in range(core_bit.bit_length() - 1)]
    return core_bit, high + low, low[:-1] + high + low[-1:]


def permute_by(values, first, second, core_bit):
    count = lax.axis_size("region") * lax.axis_size("patch")
    pairs = [(i, i ^ (second if i & core_bit else first)) for i in range(count)]
    return lax.ppermute(values, AXES, pairs)


def reduce_all(flat, vectors):
    core_bit, first, second = halving_orders()
    count = lax.axis_size("region") * lax.axis_size("patch")
    me = lax.axis_index(AXES)
    core = (me & core_bit) // core_bit
    depth = count.bit_length() - 1
    flat = flat.reshape((2,) * depth + (-1, flat.shape[1]))

    def ordered(order):
        axes = [depth - bit.bit_length() for bit in [core_bit] + order]
        return jnp.transpose(flat, axes + [depth, depth + 1])

    blocks = jnp.stack([ordered(first)[0], ordered(second)[1]]).reshape(2, -1, flat.shape[-1])
    kept = lax.dynamic_index_in_dim(blocks, core, 0, keepdims=False)
    sent = lax.dynamic_index_in_dim(blocks, 1 - core, 0, keepdims=False).astype(BF)
    got = permute_by(sent, core_bit, core_bit, core_bit)
    total = kept + got
    for one, two in zip(first, second):
        bit = jnp.where(core == 1, (me & two) // two, (me & one) // one)
        halves = total.reshape(2, -1, flat.shape[-1])
        kept = lax.dynamic_index_in_dim(halves, bit, 0, keepdims=False)
        sent = lax.dynamic_index_in_dim(halves, 1 - bit, 0, keepdims=False).astype(BF)
        got = permute_by(sent, one, two, core_bit)
        vectors = vectors + permute_by(vectors, one, two, core_bit)
        total = kept + got
    vectors = vectors + permute_by(vectors, core_bit, core_bit, core_bit)
    return total.reshape(-1), vectors.reshape(-1)


class Halving:
    def __init__(self, rows, columns, orders, carries):
        self.core_bit, (self.first, self.second) = lax.axis_size("patch"), orders
        self.count = lax.axis_size("region") * lax.axis_size("patch")
        self.block = rows // self.count
        self.rows = rows // 2
        self.columns = columns
        self.width = columns.stop - columns.start
        self.steps = len(self.first)
        self.carries = carries

    def place(self, order, core, position):
        block = self.core_bit if core else 0
        for k, bit in enumerate(order):
            if (position >> (self.steps - 1 - k)) & 1:
                block |= bit
        return block * self.block

    def me(self):
        return lax.axis_index("region") * self.core_bit + lax.axis_index("patch")

    def core(self):
        return lax.rem(self.me() // self.core_bit, 2)

    def bit(self, step):
        me = self.me()
        one, two = self.first[step], self.second[step]
        return jnp.where(self.core() == 1, lax.rem(me // two, 2), lax.rem(me // one, 2))

    def source(self, position, core):
        zero, one = self.place(self.first, 0, position), self.place(self.second, 1, position)
        return pl.multiple_of(jnp.where(core == 1, one, zero), 8)

    def extra(self, vec_width):
        return 16 * (vec_width // self.width) if self.carries else 0


def first_kernel(weights_ref, *refs, plan):
    send_ref = refs[-1]
    other = 1 - plan.core()
    for position in range(plan.count // 2):
        start = position * plan.block
        send_ref[start : start + plan.block, :] = weights_ref[
            pl.ds(plan.source(position, other), plan.block), plan.columns
        ].astype(BF)


def halve(src_ref, got_ref, out_ref, plan, step, side):
    half = plan.rows >> (step + 1)
    bit = plan.bit(step)
    chosen = 1 - bit if side else bit
    if step:
        start = pl.multiple_of(chosen * half, 16)
        held = src_ref[pl.ds(start, half), :]
        out_ref[:half, :] = (held + got_ref[pl.ds(start, half), :]).astype(out_ref.dtype)
        return
    core = plan.core()
    per_half = half // plan.block
    for k in range(per_half):
        low, high = plan.source(k, core), plan.source(k + per_half, core)
        row = pl.multiple_of(jnp.where(chosen == 1, high, low), 8)
        held = src_ref[pl.ds(row, plan.block), plan.columns]
        start = pl.multiple_of(chosen * half + k * plan.block, 16)
        got = got_ref[pl.ds(start, plan.block), :]
        out_ref[k * plan.block : (k + 1) * plan.block, :] = (held + got).astype(out_ref.dtype)


def keep_kernel(src_ref, got_ref, out_ref, *, plan, step):
    halve(src_ref, got_ref, out_ref, plan, step, 0)


def add_vectors(vec_ref, got_ref, start, plan):
    pieces = vec_ref.shape[1] // plan.width
    count = vec_ref.shape[0]
    parts = []
    for k in range(pieces):
        low = start + 8 * (pieces + k)
        high = start + 8 * k
        parts.append(
            got_ref[high : high + count, :].astype(F32) + got_ref[low : low + count, :].astype(F32)
        )
    return vec_ref[...] + jnp.concatenate(parts, axis=1)


def send_kernel(src_ref, got_ref, *refs, plan, step):
    if not plan.carries:
        halve(src_ref, got_ref, refs[0], plan, step, 1)
        return
    vec_ref, out_ref, new_ref = refs
    halve(src_ref, got_ref, out_ref, plan, step, 1)
    half = plan.rows >> (step + 1)
    count = vec_ref.shape[0]
    vec = add_vectors(vec_ref, got_ref, 2 * half, plan) if step else vec_ref[...]
    upper = vec.astype(BF)
    lower = (vec - upper.astype(F32)).astype(BF)
    pieces = vec.shape[1] // plan.width
    out_ref[half:, :] = jnp.zeros_like(out_ref[half:, :])
    for k in range(pieces):
        cut = slice(k * plan.width, (k + 1) * plan.width)
        high, low = half + 8 * k, half + 8 * (pieces + k)
        out_ref[high : high + count, :] = upper[:, cut]
        out_ref[low : low + count, :] = lower[:, cut]
    new_ref[...] = upper.astype(F32) + lower.astype(F32)


def vector_kernel(vec_ref, got_ref, new_ref, *, plan):
    new_ref[...] = add_vectors(vec_ref, got_ref, plan.block, plan)


def sum_kernel(held_ref, got_ref, out_ref):
    out_ref[...] = held_ref[...] + got_ref[: held_ref.shape[0], :]


def join_kernel(*refs, plans):
    out_ref = refs[-1]
    pieces = out_ref.shape[0] // plans[0].block
    for plan, part_ref in zip(plans, refs):
        for k in range(0, plan.width, LANES):
            piece = (plan.columns.start + k) // LANES
            out_ref[pl.ds(piece, plan.block, stride=pieces), :] = part_ref[:, k : k + LANES]


def after(marks, *values):
    return lax.optimization_barrier((*values, *marks))[: len(values)]


def reduce_kernels(plans, weights, vec, beside):
    vec_shape = (vec.shape, F32)
    held = {plan: weights for plan in plans}
    got, carrier = {}, None
    marks = ()
    for plan in plans:
        (weights_late,) = after(marks, weights)
        (sent,) = marks = call(
            functools.partial(first_kernel, plan=plan), [((plan.rows, plan.width), BF)],
            near(weights_late), name="first",
        )
        got[plan] = permute_by(sent, plan.core_bit, plan.core_bit, plan.core_bit)
    marks = beside[-1](marks)
    for step in range(plans[0].steps):
        for plan in plans:
            half = plan.rows >> (step + 1)
            source, came = after(marks, held[plan], got[plan])
            rows = half + plan.extra(vec.shape[1])
            vectors = [near(vec)] if plan.carries else []
            sent, *new = call(
                functools.partial(send_kernel, plan=plan, step=step),
                [((rows, plan.width), BF)] + ([vec_shape] if plan.carries else []),
                near(source), near(came), *vectors, name=f"send{step}",
            )
            if plan.carries:
                (vec,) = new
            marks = (sent,)
            source, came = after(marks, source, came)
            incoming = permute_by(sent, plan.first[step], plan.second[step], plan.core_bit)
            (held[plan],) = call(
                functools.partial(keep_kernel, plan=plan, step=step),
                [((half, plan.width), F32)], near(source), near(came), name=f"keep{step}",
            )
            got[plan] = incoming
        if step in beside:
            marks = beside[step](marks)
    for plan in plans:
        if plan.carries:
            (vec,) = call(
                functools.partial(vector_kernel, plan=plan), [vec_shape], near(vec), near(got[plan]),
                name="vectors",
            )
            vec = vec + permute_by(vec, plan.core_bit, plan.core_bit, plan.core_bit)
    parts = []
    for plan in plans:
        source, came = after(marks, held[plan], got[plan])
        marks = call(
            sum_kernel, [((plan.block, plan.width), F32)], near(source), near(came), name="sum"
        )
        parts.append(near(marks[0]))
    (out,) = call(
        functools.partial(join_kernel, plans=plans),
        [((plans[0].block * weights.shape[1] // LANES, LANES), F32)], *parts, name="join", plain=(0,),
    )
    return out.reshape(-1), vec.reshape(-1)


def make_plans(rows, width):
    count = lax.axis_size("region") * lax.axis_size("patch")
    core_bit, first, second = halving_orders()
    if rows % (16 * count) or width % (4 * LANES):
        return []
    high = [b for b in first if b > core_bit]
    low = [b for b in first if b < core_bit]
    turned = low[1:-1] + high + low[:1] + low[-1:]
    quarter = width // 4
    chunks = CHUNKS
    return [
        Halving(
            rows, slice(a * quarter, b * quarter),
            (turned, turned) if kind else (first, second), i == 0,
        )
        for i, (a, b, kind) in enumerate(chunks)
    ]


PICK = 20 << 30
CHUNKS = ((0, 2, 0), (2, 4, 0))


def per_device(
    nodes, edges, node_cotan, edge_cotan, edge_inner, edge_outer, node_inner, node_outer, edge_shift,
    edge_offset, edge_gain, node_shift, node_offset, node_gain, send_rows, senders, receivers,
):
    count, width = nodes.shape
    edge_count = edges.shape[0]
    hidden_width = edge_outer.shape[0]
    lists = send_rows.reshape(send_rows.shape[2:])
    half = lists.shape[1]
    slots = 2 * half
    devices_all = lax.axis_size("region") * lax.axis_size("patch")
    edge_norm = 1.0 / math.sqrt(edge_count * devices_all)
    node_norm = 1.0 / math.sqrt(count * devices_all)
    picked = 2 * count + -(-slots // LANES) * LANES
    edge_rows = 3 * width + hidden_width
    weight_rows = edge_rows + 2 * width + hidden_width
    plans = make_plans(weight_rows, hidden_width)
    edge_shift, edge_offset, edge_gain, node_shift, node_offset, node_gain = (
        v.reshape(1, -1)
        for v in (edge_shift, edge_offset, edge_gain, node_shift, node_offset, node_gain)
    )

    out_low, out_high = call(
        pick_kernel, [((half, width), BF)] * 2, lists, nodes, name="pick", limit=4 << 20, hbm=(0, 1), flops=PICK,
        scratch=[
            pltpu.VMEM(lists.shape, jnp.int32), pltpu.VMEM(nodes.shape, BF),
            pltpu.SemaphoreType.DMA((2,)),
        ],
    )
    low = ring(out_high, 1)
    high = ring(out_low, -1)

    part, own, pick, turned = call(
        table_kernel,
        [
            ((edge_count, hidden_width), F32),
            ((2 * count, hidden_width), BF),
            ((edge_count, picked), BF),
            ((picked, edge_count), BF),
        ],
        senders.reshape(1, -1), receivers.reshape(1, -1), edge_shift, nodes, edge_inner, edges,
        name="table", flops=2 * (edge_count + 2 * count) * width * hidden_width,
    )
    hidden, slope, normed, invstd, pulled, partial, node_weights, node_sums = call(
        functools.partial(forward_kernel, scale=node_norm),
        [
            ((edge_count, hidden_width), BF),
            ((edge_count, hidden_width), F32),
            ((edge_count, width), F32),
            ((edge_count, 1), F32),
            ((count, width), BF),
            ((count, width), F32),
            ((weight_rows - edge_rows, hidden_width), F32),
            ((3, width), F32),
        ],
        near(part), near(own), near(pick), near(turned), near(low), near(high), edges, nodes,
        edge_inner, edge_outer, edge_offset, edge_gain, node_shift, node_offset, node_gain,
        node_inner, node_outer, node_cotan, name="forward", flops=5 << 30,
    )
    fresh, preact, spread, weights, sums = call(
        functools.partial(backward_kernel, scale=edge_norm),
        [
            ((edge_count, width), F32),
            ((edge_count, hidden_width), BF),
            ((2 * count + slots, hidden_width), BF),
            ((weight_rows, hidden_width), F32),
            ((6, width), F32),
        ],
        near(pick), near(turned), edges, edge_cotan, nodes, near(low),
        near(high), near(hidden), near(slope), near(normed), near(invstd), near(pulled),
        edge_outer, edge_gain, near(node_sums), near(node_weights),
        name="backward", flops=5 << 30,
        scratch=[pltpu.VMEM((edge_count, width), BF)],
    )
    results = {}

    def rim_side(marks):
        (spread_late,) = after(marks, spread)
        rim_low, rim_high = call(
            functools.partial(rim_kernel, count=count), [((half, width), BF)] * 2,
            near(spread_late), edge_inner, name="rim", limit=4 << 20,
        )
        results["low"], results["high"] = ring(rim_high, 1), ring(rim_low, -1)
        return rim_low, rim_high

    def edge_side(marks):
        spread_late, fresh_late = after(marks, spread, fresh)
        results["nodes"], results["edges"] = call(
            grads_kernel,
            [((count, width), F32), ((edge_count, width), BF)],
            near(spread_late), edge_inner, near(partial), near(fresh_late), near(preact),
            name="grads", flops=2 << 30, plain=(1,),
        )
        return results["nodes"], results["low"], results["high"]

    def node_side(marks):
        (part_late,) = after(marks, results["nodes"])
        (results["nodes"],) = call(
            rims_kernel, [((count, width), F32)], lists, near(part_late),
            near(results["low"]), near(results["high"]), name="rims", plain=(0,), limit=4 << 20,
        )
        return (results["nodes"],)

    if plans:
        grad_weights, grad_vectors = reduce_kernels(plans, weights, sums, {-1: rim_side, 0: edge_side, 1: node_side})
    else:
        grad_weights, grad_vectors = reduce_all(weights, sums)
        node_side(edge_side(rim_side((sums,))))
    return (results["nodes"], results["edges"], grad_weights, grad_vectors)


def solution(mesh):
    in_specs = (
        P(AXES, None), P(AXES, None), P(AXES, None), P(AXES, None),
        P(), P(), P(), P(), P(), P(), P(), P(), P(), P(),
        P("region", "patch", None, None), P(AXES), P(AXES),
    )
    out_specs = (P(AXES, None), P(AXES, None), P(AXES), P())
    return jax.shard_map(
        per_device, mesh=mesh, in_specs=in_specs, out_specs=out_specs, check_vma=False
    )
```

```python
import collections
import functools
import math

import jax
import jax.numpy as jnp
from jax import lax
from jax.experimental import pallas as pl
from jax.experimental.pallas import tpu as pltpu
from jax.sharding import PartitionSpec as P

BF = jnp.bfloat16
F32 = jnp.float32
LANES = 128
VMEM = pltpu.VMEM
AXES = ("region", "patch")


def pinned(shape, dtype):
    return pltpu.VMEM(shape, dtype)


def mm(a, b):
    return jnp.dot(a, b, preferred_element_type=F32)


def mm_nt(a, b):
    return lax.dot_general(a, b, (((1,), (1,)), ((), ())), preferred_element_type=F32)


def mm_tn(a, b):
    return lax.dot_general(a, b, (((0,), (0,)), ((), ())), preferred_element_type=F32)


def call(body, outs, *args, flops=0, limit=24 << 20, name=None, plain=(), hbm=(), scratch=()):
    vmem = pl.BlockSpec(memory_space=pltpu.VMEM)
    anywhere = pl.BlockSpec(memory_space=pltpu.HBM)
    shapes = [
        jax.ShapeDtypeStruct(s, d) if i in plain else pinned(s, d) for i, (s, d) in enumerate(outs)
    ]
    moved = sum(math.prod(s) * jnp.dtype(d).itemsize for s, d in outs)
    return pl.pallas_call(
        body,
        out_shape=shapes,
        in_specs=[anywhere if i in hbm else vmem for i in range(len(args))],
        out_specs=[vmem] * len(outs),
        scratch_shapes=list(scratch),
        compiler_params=pltpu.CompilerParams(vmem_limit_bytes=limit),
        cost_estimate=pl.CostEstimate(flops=flops, bytes_accessed=moved, transcendentals=0),
        name=name,
    )(*[far(a) if i in hbm else a for i, a in enumerate(args)])


def far(array):
    return pltpu.with_memory_space_constraint(array, pltpu.HBM)


def near(array):
    return pltpu.with_memory_space_constraint(array, pltpu.VMEM)


def start_copies(pairs, sems):
    copies = [pltpu.make_async_copy(a, b, sems.at[i]) for i, (a, b) in enumerate(pairs)]
    for copy in copies:
        copy.start()
    return copies


def layer_norm(values):
    centred = values - jnp.mean(values, axis=-1, keepdims=True)
    invstd = lax.rsqrt(jnp.mean(centred * centred, axis=-1, keepdims=True) + 1e-05)
    return centred * invstd, invstd


def norm_back(upstream, normed, invstd, gains):
    scaled = upstream * gains
    return invstd * (
        scaled
        - jnp.mean(scaled, axis=-1, keepdims=True)
        - normed * jnp.mean(scaled * normed, axis=-1, keepdims=True)
    )


def silu_and_slope(preact):
    gate = 1.0 / (1.0 + jnp.exp(-preact))
    hidden = preact * gate
    return hidden, gate + hidden * (1.0 - gate)


def column_sum(values):
    return jnp.sum(values, axis=0, keepdims=True)


def pick_kernel(lists_hbm, nodes_hbm, low_ref, high_ref, lists_ref, nodes_ref, sems):
    for copy in start_copies([(lists_hbm, lists_ref), (nodes_hbm, nodes_ref)], sems):
        copy.wait()
    slots, count = lists_ref.shape[1], nodes_ref.shape[0]
    rows = lax.broadcasted_iota(jnp.int32, (count, slots), 0)
    for k, out_ref in enumerate((low_ref, high_ref)):
        pick = jnp.where(rows == lists_ref[k : k + 1, :], 1.0, 0.0).astype(BF)
        out_ref[...] = mm_tn(pick, nodes_ref[...]).astype(BF)


def table_kernel(
    senders_ref, receivers_ref, shift_ref, nodes_ref, inner_ref, edges_ref,
    part_ref, own_ref, pick_ref, turned_ref,
):
    edge_count, width = edges_ref.shape
    count = nodes_ref.shape[0]
    senders = senders_ref[...]
    receivers = receivers_ref[...] + count
    senders = jnp.where(senders < count, senders, senders + count)
    wide_send = jnp.transpose(jnp.broadcast_to(senders, (LANES, edge_count)))
    wide_recv = jnp.transpose(jnp.broadcast_to(receivers, (LANES, edge_count)))
    lane = lax.broadcasted_iota(jnp.int32, (edge_count, LANES), 1)
    row = lax.broadcasted_iota(jnp.int32, (LANES, edge_count), 0)
    for start in range(0, pick_ref.shape[1], LANES):
        own_part = count <= start < 2 * count
        tall = wide_recv if own_part else wide_send
        flat = receivers if own_part else senders
        pick_ref[:, start : start + LANES] = jnp.where(tall == lane + start, 1.0, 0.0).astype(BF)
        turned_ref[start : start + LANES, :] = jnp.where(flat == row + start, 1.0, 0.0).astype(BF)
    nodes = nodes_ref[...]
    own_ref[:count, :] = mm(nodes, inner_ref[width : 2 * width, :]).astype(BF)
    own_ref[count:, :] = mm(nodes, inner_ref[2 * width :, :]).astype(BF)
    tile = edge_count // 4
    for start in range(0, edge_count, tile):
        part_ref[start : start + tile, :] = (
            mm(edges_ref[start : start + tile, :], inner_ref[:width, :]) + shift_ref[...]
        )


def forward_kernel(
    part_ref, own_ref, pick_ref, turned_ref, low_ref, high_ref, edges_ref, nodes_ref,
    einner_ref, eouter_ref, eoffset_ref, egain_ref, nshift_ref, noffset_ref, ngain_ref,
    ninner_ref, nouter_ref, cotan_ref,
    hidden_ref, slope_ref, normed_ref, invstd_ref, pulled_ref, partial_ref, weights_ref, sums_ref,
    *, scale,
):
    edge_count, width = edges_ref.shape
    count = nodes_ref.shape[0]
    rim = jnp.concatenate([low_ref[...], high_ref[...]], axis=0)
    far = mm(rim, einner_ref[width : 2 * width, :]).astype(BF)
    slots = rim.shape[0]
    tile = edge_count // 4
    total = jnp.zeros((count, width), F32)
    for start in range(0, edge_count, tile):
        rows = slice(start, start + tile)
        preact = (
            part_ref[rows, :]
            + mm(pick_ref[rows, : 2 * count], own_ref[...])
            + mm(pick_ref[rows, 2 * count : 2 * count + slots], far)
        )
        hidden, slope = silu_and_slope(preact)
        hidden = hidden.astype(BF)
        hidden_ref[rows, :] = hidden
        slope_ref[rows, :] = slope
        normed, invstd = layer_norm(mm(hidden, eouter_ref[...]) + eoffset_ref[...])
        normed_ref[rows, :] = normed
        invstd_ref[rows, :] = invstd
        fresh = (edges_ref[rows, :].astype(F32) + egain_ref[...] * normed).astype(BF)
        total += mm(turned_ref[count : 2 * count, rows], fresh)
    aggregate = total.astype(BF)
    nodes = nodes_ref[...]
    preact = (
        mm(nodes, ninner_ref[:width, :]) + mm(aggregate, ninner_ref[width:, :]) + nshift_ref[...]
    )
    hidden, slope = silu_and_slope(preact)
    hidden = hidden.astype(BF)
    normed, invstd = layer_norm(mm(hidden, nouter_ref[...]) + noffset_ref[...])
    cotan = cotan_ref[...].astype(F32)
    linear_back = norm_back(cotan, normed, invstd, ngain_ref[...])
    linear_half = linear_back.astype(BF)
    preact_back = mm_nt(linear_half, nouter_ref[...]) * slope
    preact_half = preact_back.astype(BF)
    pulled_ref[...] = mm_nt(preact_half, ninner_ref[width:, :]).astype(BF)
    partial_ref[...] = cotan + mm_nt(preact_half, ninner_ref[:width, :])
    hidden_width = preact.shape[1]
    weights_ref[:width, :] = mm_tn(nodes, preact_half) * scale
    weights_ref[width : 2 * width, :] = mm_tn(aggregate, preact_half) * scale
    weights_ref[2 * width :, :] = mm_tn(hidden, linear_half) * scale
    sums_ref[0:1, :] = column_sum(preact_back) * scale
    sums_ref[1:2, :] = column_sum(linear_back) * scale
    sums_ref[2:3, :] = column_sum(cotan * normed) * scale


def backward_kernel(
    pick_ref, turned_ref, edges_ref, ecotan_ref, nodes_ref, low_ref, high_ref, hidden_ref, slope_ref,
    normed_ref, invstd_ref, pulled_ref, eouter_ref, egain_ref, node_sums_ref, node_weights_ref,
    fresh_ref, preact_ref, spread_ref, weights_ref, sums_ref, linear_ref, *, scale,
):
    weights_ref[weights_ref.shape[0] - node_weights_ref.shape[0] :, :] = node_weights_ref[...]
    edge_count, width = edges_ref.shape
    count = nodes_ref.shape[0]
    tile = edge_count // 4
    sums = [0.0, 0.0, 0.0]
    for start in range(0, edge_count, tile):
        rows = slice(start, start + tile)
        fresh_back = ecotan_ref[rows, :].astype(F32) + mm(
            pick_ref[rows, count : 2 * count], pulled_ref[...]
        )
        fresh_ref[rows, :] = fresh_back
        normed = normed_ref[rows, :]
        linear_back = norm_back(fresh_back, normed, invstd_ref[rows, :], egain_ref[...])
        linear_half = linear_back.astype(BF)
        linear_ref[rows, :] = linear_half
        preact_back = mm_nt(linear_half, eouter_ref[...]) * slope_ref[rows, :]
        preact_ref[rows, :] = preact_back.astype(BF)
        sums[0] += column_sum(preact_back)
        sums[1] += column_sum(linear_back)
        sums[2] += column_sum(fresh_back * normed)
    for k in range(3):
        sums_ref[k : k + 1, :] = sums[k] * scale
    sums_ref[3:, :] = node_sums_ref[...]
    used = spread_ref.shape[0]
    spread = mm(turned_ref[:used, :], preact_ref[...]).astype(BF)
    spread_ref[...] = spread
    weights_ref[:width, :] = mm_tn(edges_ref[...], preact_ref[...]) * scale
    rim = jnp.concatenate([low_ref[...], high_ref[...]], axis=0)
    nodes = nodes_ref[...]
    weights_ref[width : 2 * width, :] = (
        mm_tn(nodes, spread[:count]) + mm_tn(rim, spread[2 * count :])
    ) * scale
    weights_ref[2 * width : 3 * width, :] = mm_tn(nodes, spread[count : 2 * count]) * scale
    weights_ref[3 * width : 3 * width + hidden_ref.shape[1], :] = (
        mm_tn(hidden_ref[...], linear_ref[...]) * scale
    )


def rim_kernel(spread_ref, inner_ref, out_ref, *, count):
    width, slots = spread_ref.shape[1], out_ref.shape[0]
    rows = mm_nt(spread_ref[2 * count :, :], inner_ref[width : 2 * width, :]).astype(BF)
    out_ref[: slots // 2, :] = rows[slots // 2 :]
    out_ref[slots // 2 :, :] = rows[: slots // 2]


def grads_kernel(spread_ref, inner_ref, partial_ref, fresh_ref, preact_ref, nodes_ref, edges_ref):
    count, width = partial_ref.shape
    nodes_ref[...] = (
        partial_ref[...]
        + mm_nt(spread_ref[:count, :], inner_ref[width : 2 * width, :])
        + mm_nt(spread_ref[count : 2 * count, :], inner_ref[2 * width :, :])
    )
    edge_count = preact_ref.shape[0]
    tile = edge_count // 4
    for start in range(0, edge_count, tile):
        rows = slice(start, start + tile)
        edges_ref[rows, :] = (
            fresh_ref[rows, :] + mm_nt(preact_ref[rows, :], inner_ref[:width, :])
        ).astype(BF)


def rims_kernel(lists_ref, partial_ref, back_ref, out_ref):
    count, half = partial_ref.shape[0], lists_ref.shape[1]
    rows = lax.broadcasted_iota(jnp.int32, (count, half), 0)
    total = partial_ref[...]
    for k in range(2):
        pick = jnp.where(rows == lists_ref[k : k + 1, :], 1.0, 0.0).astype(BF)
        total += mm(pick, back_ref[k * half : (k + 1) * half, :])
    out_ref[...] = total


def ring(values, step):
    count = lax.axis_size("patch")
    return lax.ppermute(values, "patch", [(i, (i + step) % count) for i in range(count)])


def halving_orders():
    core_bit = lax.axis_size("patch")
    high = [core_bit << k for k in range(1, lax.axis_size("region").bit_length() - 1)]
    low = [1 << k for k in range(core_bit.bit_length() - 1)]
    return core_bit, high + low, low[:-1] + high + low[-1:]


def permute_by(values, first, second, core_bit):
    count = lax.axis_size("region") * lax.axis_size("patch")
    pairs = [(i, i ^ (second if i & core_bit else first)) for i in range(count)]
    return lax.ppermute(values, AXES, pairs)


def reduce_all(flat, vectors):
    core_bit, first, second = halving_orders()
    count = lax.axis_size("region") * lax.axis_size("patch")
    me = lax.axis_index(AXES)
    core = (me & core_bit) // core_bit
    depth = count.bit_length() - 1
    flat = flat.reshape((2,) * depth + (-1, flat.shape[1]))

    def ordered(order):
        axes = [depth - bit.bit_length() for bit in [core_bit] + order]
        return jnp.transpose(flat, axes + [depth, depth + 1])

    blocks = jnp.stack([ordered(first)[0], ordered(second)[1]]).reshape(2, -1, flat.shape[-1])
    kept = lax.dynamic_index_in_dim(blocks, core, 0, keepdims=False)
    sent = lax.dynamic_index_in_dim(blocks, 1 - core, 0, keepdims=False).astype(BF)
    got = permute_by(sent, core_bit, core_bit, core_bit)
    total = kept + got
    for one, two in zip(first, second):
        bit = jnp.where(core == 1, (me & two) // two, (me & one) // one)
        halves = total.reshape(2, -1, flat.shape[-1])
        kept = lax.dynamic_index_in_dim(halves, bit, 0, keepdims=False)
        sent = lax.dynamic_index_in_dim(halves, 1 - bit, 0, keepdims=False).astype(BF)
        got = permute_by(sent, one, two, core_bit)
        vectors = vectors + permute_by(vectors, one, two, core_bit)
        total = kept + got
    vectors = vectors + permute_by(vectors, core_bit, core_bit, core_bit)
    return total.reshape(-1), vectors.reshape(-1)


Sides = collections.namedtuple("Sides", ("early", "late", "last"))


class Halving:
    def __init__(self, rows, columns, orders, carries):
        self.core_bit, (self.first, self.second) = lax.axis_size("patch"), orders
        self.count = lax.axis_size("region") * lax.axis_size("patch")
        self.block = rows // self.count
        self.rows = rows // 2
        self.columns = columns
        self.width = columns.stop - columns.start
        self.steps = len(self.first)
        self.carries = carries

    def place(self, order, core, position):
        block = self.core_bit if core else 0
        for k, bit in enumerate(order):
            if (position >> (self.steps - 1 - k)) & 1:
                block |= bit
        return block * self.block

    def me(self):
        return lax.axis_index("region") * self.core_bit + lax.axis_index("patch")

    def core(self):
        return lax.rem(self.me() // self.core_bit, 2)

    def bit(self, step):
        me = self.me()
        one, two = self.first[step], self.second[step]
        return jnp.where(self.core() == 1, lax.rem(me // two, 2), lax.rem(me // one, 2))

    def source(self, position, core):
        zero, one = self.place(self.first, 0, position), self.place(self.second, 1, position)
        return pl.multiple_of(jnp.where(core == 1, one, zero), 8)

    def pieces(self, full):
        return full // self.width

    def extra(self, full):
        return 16 * self.pieces(full) if self.carries else 0

    def slots(self, step, rows):
        if not self.carries:
            return 0
        bits = (self.first[step], self.second[step])
        return rows if 1 in bits else rows // 2 if min(bits) < self.core_bit else 0

    def taken(self, step):
        place = lax.rem(self.me(), self.core_bit)
        even = lax.rem(place, 2) == 0
        answers = []
        for bit in (self.first[step], self.second[step]):
            if bit == 1 or bit > self.core_bit:
                answers.append((bit == 1, bit == 1))
                continue
            between = lax.rem(place, bit) // 2
            up = jnp.logical_and(even, between == 0)
            down = jnp.logical_and(jnp.logical_not(even), between == bit // 2 - 1)
            answers.append((up, down))
        core = self.core() == 1
        return tuple(jnp.where(core, b, a) for a, b in zip(*answers))


def first_kernel(weights_ref, *refs, plan):
    send_ref = refs[-1]
    other = 1 - plan.core()
    for position in range(plan.count // 2):
        start = position * plan.block
        send_ref[start : start + plan.block, :] = weights_ref[
            pl.ds(plan.source(position, other), plan.block), plan.columns
        ].astype(BF)


def halve(src_ref, got_ref, out_ref, plan, step, side):
    half = plan.rows >> (step + 1)
    bit = plan.bit(step)
    chosen = 1 - bit if side else bit
    if step:
        start = pl.multiple_of(chosen * half, 16)
        held = src_ref[pl.ds(start, half), :]
        out_ref[:half, :] = (held + got_ref[pl.ds(start, half), :]).astype(out_ref.dtype)
        return
    core = plan.core()
    per_half = half // plan.block
    for k in range(per_half):
        low, high = plan.source(k, core), plan.source(k + per_half, core)
        row = pl.multiple_of(jnp.where(chosen == 1, high, low), 8)
        held = src_ref[pl.ds(row, plan.block), plan.columns]
        start = pl.multiple_of(chosen * half + k * plan.block, 16)
        got = got_ref[pl.ds(start, plan.block), :]
        out_ref[k * plan.block : (k + 1) * plan.block, :] = (held + got).astype(out_ref.dtype)


def keep_kernel(src_ref, got_ref, out_ref, *, plan, step):
    halve(src_ref, got_ref, out_ref, plan, step, 0)


def unpack(got_ref, start, rows, plan, full):
    parts = [
        got_ref[start + k * rows : start + (k + 1) * rows, :] for k in range(plan.pieces(full))
    ]
    return jnp.concatenate(parts, axis=1).astype(F32)


def pack(out_ref, start, values, plan):
    rows = values.shape[0]
    for k in range(plan.pieces(values.shape[1])):
        out_ref[start + k * rows : start + (k + 1) * rows, :] = values[
            :, k * plan.width : (k + 1) * plan.width
        ].astype(BF)


def add_vectors(vec_ref, got_ref, start, plan):
    count, full = vec_ref.shape
    both = unpack(got_ref, start, 16, plan, full)
    return vec_ref[...] + (both[:count] + both[8 : 8 + count])


def move_halo(state_ref, got_ref, start, plan, step):
    rows, full = state_ref.shape
    half = rows // 2
    slots = plan.slots(step, rows)
    state = state_ref[...].astype(F32)
    if not slots:
        return state
    came = unpack(got_ref, start, slots, plan, full)
    up, down = plan.taken(step)
    return jnp.concatenate(
        [
            jnp.where(up, came[:half], state[:half]),
            jnp.where(down, came[slots - half :], state[half:]),
        ],
        axis=0,
    )


def send_kernel(src_ref, got_ref, *refs, plan, step):
    if not plan.carries:
        halve(src_ref, got_ref, refs[0], plan, step, 1)
        return
    vec_ref, state_ref, out_ref, new_ref, moved_ref = refs
    halve(src_ref, got_ref, out_ref, plan, step, 1)
    half = plan.rows >> (step + 1)
    count, full = vec_ref.shape
    vec, state = vec_ref[...], state_ref[...].astype(F32)
    if step:
        vec = add_vectors(vec_ref, got_ref, 2 * half, plan)
        state = move_halo(state_ref, got_ref, 2 * half + plan.extra(full), plan, step - 1)
    upper = vec.astype(BF).astype(F32)
    lower = (vec - upper).astype(BF).astype(F32)
    gap = jnp.zeros((8 - count, full), F32)
    pack(out_ref, half, jnp.concatenate([upper, gap, lower, gap], axis=0), plan)
    new_ref[...] = upper + lower
    moved_ref[...] = state.astype(BF)
    rows = state.shape[0]
    slots = plan.slots(step, rows)
    if slots == rows:
        pack(out_ref, half + plan.extra(full), state, plan)
    elif slots:
        even = lax.rem(plan.me(), 2) == 0
        pack(
            out_ref, half + plan.extra(full),
            jnp.where(even, state[: rows // 2], state[rows // 2 :]), plan,
        )


def carried_kernel(vec_ref, state_ref, got_ref, new_ref, moved_ref, *, plan):
    new_ref[...] = add_vectors(vec_ref, got_ref, plan.block, plan)
    start = plan.block + plan.extra(vec_ref.shape[1])
    moved_ref[...] = move_halo(state_ref, got_ref, start, plan, plan.steps - 1).astype(BF)


def close_kernel(vec_ref, other_ref, *refs, plans):
    out_ref, vectors_ref = refs[-2:]
    pieces = out_ref.shape[0] // plans[0].block
    for plan, held_ref, got_ref in zip(plans, refs[0:-2:2], refs[1:-2:2]):
        total = held_ref[...] + got_ref[: plan.block, :]
        for k in range(0, plan.width, LANES):
            piece = (plan.columns.start + k) // LANES
            out_ref[pl.ds(piece, plan.block, stride=pieces), :] = total[:, k : k + LANES]
    vec = vec_ref[...] + other_ref[...]
    for k in range(pieces):
        vectors_ref[pl.ds(k, vec.shape[0], stride=pieces), :] = vec[:, k * LANES : (k + 1) * LANES]


def after(marks, *values):
    return lax.optimization_barrier((*values, *marks))[: len(values)]


def reduce_kernels(plans, weights, vec, sides):
    full = vec.shape[1]
    held = {plan: weights for plan in plans}
    got = {}
    marks = ()
    for plan in plans:
        (weights_late,) = after(marks, weights)
        (sent,) = marks = call(
            functools.partial(first_kernel, plan=plan), [((plan.rows, plan.width), BF)],
            near(weights_late), name="first",
        )
        got[plan] = permute_by(sent, plan.core_bit, plan.core_bit, plan.core_bit)
    state = sides.early(marks)
    marks = (state,)
    shapes = [(vec.shape, F32), (state.shape, BF)]
    for step in range(plans[0].steps):
        if step == 1:
            marks = sides.late(marks)
        for plan in plans:
            half = plan.rows >> (step + 1)
            source, came = after(marks, held[plan], got[plan])
            rows = half + plan.extra(full) + plan.slots(step, state.shape[0]) * plan.pieces(full)
            carried = [near(vec), near(state)] if plan.carries else []
            sent, *new = call(
                functools.partial(send_kernel, plan=plan, step=step),
                [((rows, plan.width), BF)] + (shapes if plan.carries else []),
                near(source), near(came), *carried, name=f"send{step}",
            )
            if plan.carries:
                vec, state = new
            marks = (sent,)
            source, came = after(marks, source, came)
            incoming = permute_by(sent, plan.first[step], plan.second[step], plan.core_bit)
            (held[plan],) = call(
                functools.partial(keep_kernel, plan=plan, step=step),
                [((half, plan.width), F32)], near(source), near(came), name=f"keep{step}",
            )
            got[plan] = incoming
    (carrier,) = [plan for plan in plans if plan.carries]
    vec, state = call(
        functools.partial(carried_kernel, plan=carrier), shapes, near(vec), near(state),
        near(got[carrier]), name="carried",
    )
    other = permute_by(vec, carrier.core_bit, carrier.core_bit, carrier.core_bit)
    sides.last(state)
    pairs = [near(a) for plan in plans for a in (held[plan], got[plan])]
    out, vectors = call(
        functools.partial(close_kernel, plans=plans),
        [
            ((plans[0].block * weights.shape[1] // LANES, LANES), F32),
            ((vec.size // LANES, LANES), F32),
        ],
        near(vec), near(other), *pairs, name="close", plain=(0, 1),
    )
    return out.reshape(-1), vectors.reshape(-1)


def make_plans(rows, width, slots):
    count = lax.axis_size("region") * lax.axis_size("patch")
    core_bit, first, second = halving_orders()
    if rows % (16 * count) or width % (4 * LANES) or slots % 32:
        return []
    high = [b for b in first if b > core_bit]
    low = [b for b in first if b < core_bit]
    turned = low[1:-1] + high + low[:1] + low[-1:]
    quarter = width // 4
    chunks = CHUNKS
    return [
        Halving(
            rows, slice(a * quarter, b * quarter),
            (turned, turned) if kind else (first, second), i == 0,
        )
        for i, (a, b, kind) in enumerate(chunks)
    ]


PICK = 20 << 30
CHUNKS = ((0, 2, 0), (2, 4, 0))


def per_device(
    nodes, edges, node_cotan, edge_cotan, edge_inner, edge_outer, node_inner, node_outer, edge_shift,
    edge_offset, edge_gain, node_shift, node_offset, node_gain, send_rows, senders, receivers,
):
    count, width = nodes.shape
    edge_count = edges.shape[0]
    hidden_width = edge_outer.shape[0]
    lists = send_rows.reshape(send_rows.shape[2:])
    half = lists.shape[1]
    slots = 2 * half
    devices_all = lax.axis_size("region") * lax.axis_size("patch")
    edge_norm = 1.0 / math.sqrt(edge_count * devices_all)
    node_norm = 1.0 / math.sqrt(count * devices_all)
    picked = 2 * count + -(-slots // LANES) * LANES
    edge_rows = 3 * width + hidden_width
    weight_rows = edge_rows + 2 * width + hidden_width
    plans = make_plans(weight_rows, hidden_width, slots)
    edge_shift, edge_offset, edge_gain, node_shift, node_offset, node_gain = (
        v.reshape(1, -1)
        for v in (edge_shift, edge_offset, edge_gain, node_shift, node_offset, node_gain)
    )

    out_low, out_high = call(
        pick_kernel, [((half, width), BF)] * 2, lists, nodes, name="pick", limit=4 << 20, hbm=(0, 1), flops=PICK,
        scratch=[
            pltpu.VMEM(lists.shape, jnp.int32), pltpu.VMEM(nodes.shape, BF),
            pltpu.SemaphoreType.DMA((2,)),
        ],
    )
    low = ring(out_high, 1)
    high = ring(out_low, -1)

    part, own, pick, turned = call(
        table_kernel,
        [
            ((edge_count, hidden_width), F32),
            ((2 * count, hidden_width), BF),
            ((edge_count, picked), BF),
            ((picked, edge_count), BF),
        ],
        senders.reshape(1, -1), receivers.reshape(1, -1), edge_shift, nodes, edge_inner, edges,
        name="table", flops=2 * (edge_count + 2 * count) * width * hidden_width,
    )
    hidden, slope, normed, invstd, pulled, partial, node_weights, node_sums = call(
        functools.partial(forward_kernel, scale=node_norm),
        [
            ((edge_count, hidden_width), BF),
            ((edge_count, hidden_width), F32),
            ((edge_count, width), F32),
            ((edge_count, 1), F32),
            ((count, width), BF),
            ((count, width), F32),
            ((weight_rows - edge_rows, hidden_width), F32),
            ((3, width), F32),
        ],
        near(part), near(own), near(pick), near(turned), near(low), near(high), edges, nodes,
        edge_inner, edge_outer, edge_offset, edge_gain, node_shift, node_offset, node_gain,
        node_inner, node_outer, node_cotan, name="forward", flops=5 << 30,
    )
    fresh, preact, spread, weights, sums = call(
        functools.partial(backward_kernel, scale=edge_norm),
        [
            ((edge_count, width), F32),
            ((edge_count, hidden_width), BF),
            ((2 * count + slots, hidden_width), BF),
            ((weight_rows, hidden_width), F32),
            ((6, width), F32),
        ],
        near(pick), near(turned), edges, edge_cotan, nodes, near(low),
        near(high), near(hidden), near(slope), near(normed), near(invstd), near(pulled),
        edge_outer, edge_gain, near(node_sums), near(node_weights),
        name="backward", flops=5 << 30,
        scratch=[pltpu.VMEM((edge_count, width), BF)],
    )
    results = {}

    def rim_side(marks):
        (spread_late,) = after(marks, spread)
        (rims,) = call(
            functools.partial(rim_kernel, count=count), [((slots, width), BF)],
            near(spread_late), edge_inner, name="rim", limit=4 << 20,
        )
        return rims

    def grads_side(marks):
        spread_late, fresh_late = after(marks, spread, fresh)
        results["nodes"], results["edges"] = call(
            grads_kernel,
            [((count, width), F32), ((edge_count, width), BF)],
            near(spread_late), edge_inner, near(partial), near(fresh_late), near(preact),
            name="grads", flops=2 << 30, plain=(1,),
        )
        return (results["nodes"],)

    def halo_side(back):
        (results["nodes"],) = call(
            rims_kernel, [((count, width), F32)], lists, near(results["nodes"]), near(back),
            name="rims", plain=(0,), limit=4 << 20,
        )

    if plans:
        sides = Sides(rim_side, grads_side, halo_side)
        grad_weights, grad_vectors = reduce_kernels(plans, weights, sums, sides)
    else:
        grad_weights, grad_vectors = reduce_all(weights, sums)
        rims = rim_side((sums,))
        back = jnp.concatenate([ring(rims[:half], 1), ring(rims[half:], -1)])
        grads_side((sums,))
        halo_side(back)
    return (results["nodes"], results["edges"], grad_weights, grad_vectors)


def solution(mesh):
    in_specs = (
        P(AXES, None), P(AXES, None), P(AXES, None), P(AXES, None),
        P(), P(), P(), P(), P(), P(), P(), P(), P(), P(),
        P("region", "patch", None, None), P(AXES), P(AXES),
    )
    out_specs = (P(AXES, None), P(AXES, None), P(AXES), P())
    return jax.shard_map(
        per_device, mesh=mesh, in_specs=in_specs, out_specs=out_specs, check_vma=False
    )
```

```python
import collections
import functools
import math

import jax
import jax.numpy as jnp
from jax import lax
from jax.experimental import pallas as pl
from jax.experimental.pallas import tpu as pltpu
from jax.sharding import PartitionSpec as P

BF = jnp.bfloat16
F32 = jnp.float32
LANES = 128
VMEM = pltpu.VMEM
AXES = ("region", "patch")


def pinned(shape, dtype):
    return pltpu.VMEM(shape, dtype)


def mm(a, b):
    return jnp.dot(a, b, preferred_element_type=F32)


def mm_nt(a, b):
    return lax.dot_general(a, b, (((1,), (1,)), ((), ())), preferred_element_type=F32)


def mm_tn(a, b):
    return lax.dot_general(a, b, (((0,), (0,)), ((), ())), preferred_element_type=F32)


def call(body, outs, *args, flops=0, limit=24 << 20, name=None, plain=(), hbm=(), scratch=()):
    vmem = pl.BlockSpec(memory_space=pltpu.VMEM)
    anywhere = pl.BlockSpec(memory_space=pltpu.HBM)
    shapes = [
        jax.ShapeDtypeStruct(s, d) if i in plain else pinned(s, d) for i, (s, d) in enumerate(outs)
    ]
    moved = sum(math.prod(s) * jnp.dtype(d).itemsize for s, d in outs)
    return pl.pallas_call(
        body,
        out_shape=shapes,
        in_specs=[anywhere if i in hbm else vmem for i in range(len(args))],
        out_specs=[vmem] * len(outs),
        scratch_shapes=list(scratch),
        compiler_params=pltpu.CompilerParams(vmem_limit_bytes=limit),
        cost_estimate=pl.CostEstimate(flops=flops, bytes_accessed=moved, transcendentals=0),
        name=name,
    )(*[far(a) if i in hbm else a for i, a in enumerate(args)])


def far(array):
    return pltpu.with_memory_space_constraint(array, pltpu.HBM)


def near(array):
    return pltpu.with_memory_space_constraint(array, pltpu.VMEM)


def start_copies(pairs, sems):
    copies = [pltpu.make_async_copy(a, b, sems.at[i]) for i, (a, b) in enumerate(pairs)]
    for copy in copies:
        copy.start()
    return copies


def layer_norm(values):
    centred = values - jnp.mean(values, axis=-1, keepdims=True)
    invstd = lax.rsqrt(jnp.mean(centred * centred, axis=-1, keepdims=True) + 1e-05)
    return centred * invstd, invstd


def norm_back(upstream, normed, invstd, gains):
    scaled = upstream * gains
    return invstd * (
        scaled
        - jnp.mean(scaled, axis=-1, keepdims=True)
        - normed * jnp.mean(scaled * normed, axis=-1, keepdims=True)
    )


def silu_and_slope(preact):
    gate = 1.0 / (1.0 + jnp.exp(-preact))
    hidden = preact * gate
    return hidden, gate + hidden * (1.0 - gate)


def column_sum(values):
    return jnp.sum(values, axis=0, keepdims=True)


def pick_kernel(lists_hbm, nodes_hbm, low_ref, high_ref, lists_ref, nodes_ref, sems):
    for copy in start_copies([(lists_hbm, lists_ref), (nodes_hbm, nodes_ref)], sems):
        copy.wait()
    slots, count = lists_ref.shape[1], nodes_ref.shape[0]
    rows = lax.broadcasted_iota(jnp.int32, (count, slots), 0)
    for k, out_ref in enumerate((low_ref, high_ref)):
        pick = jnp.where(rows == lists_ref[k : k + 1, :], 1.0, 0.0).astype(BF)
        out_ref[...] = mm_tn(pick, nodes_ref[...]).astype(BF)


def table_kernel(
    senders_ref, receivers_ref, shift_ref, nodes_ref, inner_ref, edges_ref, ninner_ref, nshift_ref,
    part_ref, npart_ref, pick_ref, turned_ref, own_ref,
):
    edge_count, width = edges_ref.shape
    count = nodes_ref.shape[0]
    senders = senders_ref[...]
    receivers = receivers_ref[...] + count
    senders = jnp.where(senders < count, senders, senders + count)
    wide_send = jnp.transpose(jnp.broadcast_to(senders, (LANES, edge_count)))
    wide_recv = jnp.transpose(jnp.broadcast_to(receivers, (LANES, edge_count)))
    lane = lax.broadcasted_iota(jnp.int32, (edge_count, LANES), 1)
    row = lax.broadcasted_iota(jnp.int32, (LANES, edge_count), 0)
    for start in range(0, pick_ref.shape[1], LANES):
        own_part = count <= start < 2 * count
        tall = wide_recv if own_part else wide_send
        flat = receivers if own_part else senders
        pick_ref[:, start : start + LANES] = jnp.where(tall == lane + start, 1.0, 0.0).astype(BF)
        turned_ref[start : start + LANES, :] = jnp.where(flat == row + start, 1.0, 0.0).astype(BF)
    nodes = nodes_ref[...]
    own_ref[:count, :] = mm(nodes, inner_ref[width : 2 * width, :]).astype(BF)
    own_ref[count:, :] = mm(nodes, inner_ref[2 * width :, :]).astype(BF)
    tile = edge_count // 2
    for start in range(0, edge_count, tile):
        rows = slice(start, start + tile)
        part_ref[rows, :] = (
            mm(edges_ref[rows, :], inner_ref[:width, :])
            + mm(pick_ref[rows, : 2 * count], own_ref[...])
            + shift_ref[...]
        )
    npart_ref[...] = mm(nodes, ninner_ref[:width, :]) + nshift_ref[...]


def forward_kernel(
    part_ref, npart_ref, pick_ref, turned_ref, low_ref, high_ref, edges_ref,
    einner_ref, eouter_ref, eoffset_ref, egain_ref, noffset_ref, ngain_ref,
    ninner_ref, nouter_ref, cotan_ref,
    hidden_ref, slope_ref, normed_ref, invstd_ref, pulled_ref, partial_ref, sums_ref,
    aggregate_ref, node_hidden_ref, node_preact_ref, node_linear_ref,
    *, scale,
):
    edge_count, width = edges_ref.shape
    count = cotan_ref.shape[0]
    rim = jnp.concatenate([low_ref[...], high_ref[...]], axis=0)
    far = mm(rim, einner_ref[width : 2 * width, :]).astype(BF)
    slots = rim.shape[0]
    tile = edge_count // 2
    tiles = [slice(start, start + tile) for start in range(0, edge_count, tile)]

    def first(rows):
        return part_ref[rows, :] + mm(pick_ref[rows, 2 * count : 2 * count + slots], far)

    def second(rows, preact):
        hidden, slope = silu_and_slope(preact)
        hidden = hidden.astype(BF)
        hidden_ref[rows, :] = hidden
        slope_ref[rows, :] = slope
        return mm(hidden, eouter_ref[...]) + eoffset_ref[...]

    def third(rows, linear):
        normed, invstd = layer_norm(linear)
        normed_ref[rows, :] = normed
        invstd_ref[rows, :] = invstd
        fresh = (edges_ref[rows, :].astype(F32) + egain_ref[...] * normed).astype(BF)
        return mm(turned_ref[count : 2 * count, rows], fresh)

    preacts = [first(rows) for rows in tiles]
    linears = [second(rows, preact) for rows, preact in zip(tiles, preacts)]
    total = sum(third(rows, linear) for rows, linear in zip(tiles, linears))
    aggregate = total.astype(BF)
    preact = npart_ref[...] + mm(aggregate, ninner_ref[width:, :])
    hidden, slope = silu_and_slope(preact)
    hidden = hidden.astype(BF)
    normed, invstd = layer_norm(mm(hidden, nouter_ref[...]) + noffset_ref[...])
    cotan = cotan_ref[...].astype(F32)
    linear_back = norm_back(cotan, normed, invstd, ngain_ref[...])
    linear_half = linear_back.astype(BF)
    preact_back = mm_nt(linear_half, nouter_ref[...]) * slope
    preact_half = preact_back.astype(BF)
    pulled_ref[...] = mm_nt(preact_half, ninner_ref[width:, :]).astype(BF)
    partial_ref[...] = cotan + mm_nt(preact_half, ninner_ref[:width, :])
    aggregate_ref[...] = aggregate
    node_hidden_ref[...] = hidden
    node_preact_ref[...] = preact_half
    node_linear_ref[...] = linear_half
    sums_ref[0:1, :] = column_sum(preact_back) * scale
    sums_ref[1:2, :] = column_sum(linear_back) * scale
    sums_ref[2:3, :] = column_sum(cotan * normed) * scale


def backward_kernel(
    pick_ref, turned_ref, ecotan_ref, normed_ref, invstd_ref, slope_ref, pulled_ref, eouter_ref,
    egain_ref, node_sums_ref,
    fresh_ref, preact_ref, spread_ref, sums_ref, linear_ref, *, scale,
):
    edge_count = ecotan_ref.shape[0]
    count = pulled_ref.shape[0]
    tile = edge_count // 2
    tiles = [slice(start, start + tile) for start in range(0, edge_count, tile)]
    sums = [0.0, 0.0, 0.0]

    def first(rows):
        return ecotan_ref[rows, :].astype(F32) + mm(
            pick_ref[rows, count : 2 * count], pulled_ref[...]
        )

    def second(rows, fresh_back):
        fresh_ref[rows, :] = fresh_back
        normed = normed_ref[rows, :]
        linear_back = norm_back(fresh_back, normed, invstd_ref[rows, :], egain_ref[...])
        linear_half = linear_back.astype(BF)
        linear_ref[rows, :] = linear_half
        sums[1] += column_sum(linear_back)
        sums[2] += column_sum(fresh_back * normed)
        return mm_nt(linear_half, eouter_ref[...])

    def third(rows, back):
        preact_back = back * slope_ref[rows, :]
        preact_ref[rows, :] = preact_back.astype(BF)
        sums[0] += column_sum(preact_back)

    fresh_backs = [first(rows) for rows in tiles]
    backs = [second(rows, fresh_back) for rows, fresh_back in zip(tiles, fresh_backs)]
    for rows, back in zip(tiles, backs):
        third(rows, back)
    for k in range(3):
        sums_ref[k : k + 1, :] = sums[k] * scale
    sums_ref[3:, :] = node_sums_ref[...]
    used = spread_ref.shape[0]
    spread_ref[...] = mm(turned_ref[:used, :], preact_ref[...]).astype(BF)


def weights_kernel(
    edges_ref, nodes_ref, low_ref, high_ref, hidden_ref, preact_ref, linear_ref, spread_ref,
    aggregate_ref, node_hidden_ref, node_preact_ref, node_linear_ref,
    weights_ref, *sends, columns, scales, plan,
):
    count = nodes_ref.shape[0]
    nodes = nodes_ref[...]
    rim = jnp.concatenate([low_ref[...], high_ref[...]], axis=0)
    node_preact = node_preact_ref[:, columns]
    start = 0
    for scale, terms in (
        (scales[0], [(edges_ref[...], preact_ref[:, columns])]),
        (scales[0], [(nodes, spread_ref[:count, columns]), (rim, spread_ref[2 * count :, columns])]),
        (scales[0], [(nodes, spread_ref[count : 2 * count, columns])]),
        (scales[0], [(hidden_ref[...], linear_ref[:, columns])]),
        (scales[1], [(nodes, node_preact)]),
        (scales[1], [(aggregate_ref[...], node_preact)]),
        (scales[1], [(node_hidden_ref[...], node_linear_ref[:, columns])]),
    ):
        value = sum(mm_tn(a, b) for a, b in terms) * scale
        weights_ref[start : start + value.shape[0], :] = value
        start += value.shape[0]
    for send_ref in sends:
        other = 1 - plan.core()
        for position in range(plan.count // 2):
            row = position * plan.block
            send_ref[row : row + plan.block, :] = weights_ref[
                pl.ds(plan.source(position, other), plan.block), :
            ].astype(BF)


def rim_kernel(spread_ref, inner_ref, out_ref, *, count):
    width, slots = spread_ref.shape[1], out_ref.shape[0]
    rows = mm_nt(spread_ref[2 * count :, :], inner_ref[width : 2 * width, :]).astype(BF)
    out_ref[: slots // 2, :] = rows[slots // 2 :]
    out_ref[slots // 2 :, :] = rows[: slots // 2]


def grads_kernel(spread_ref, inner_ref, partial_ref, fresh_ref, preact_ref, nodes_ref, edges_ref):
    count, width = partial_ref.shape
    nodes_ref[...] = (
        partial_ref[...]
        + mm_nt(spread_ref[:count, :], inner_ref[width : 2 * width, :])
        + mm_nt(spread_ref[count : 2 * count, :], inner_ref[2 * width :, :])
    )
    edge_count = preact_ref.shape[0]
    tile = edge_count // 2
    for start in range(0, edge_count, tile):
        rows = slice(start, start + tile)
        edges_ref[rows, :] = (
            fresh_ref[rows, :] + mm_nt(preact_ref[rows, :], inner_ref[:width, :])
        ).astype(BF)


def rims_kernel(lists_ref, partial_ref, back_ref, out_ref):
    count, half = partial_ref.shape[0], lists_ref.shape[1]
    rows = lax.broadcasted_iota(jnp.int32, (count, half), 0)
    total = partial_ref[...]
    for k in range(2):
        pick = jnp.where(rows == lists_ref[k : k + 1, :], 1.0, 0.0).astype(BF)
        total += mm(pick, back_ref[k * half : (k + 1) * half, :])
    out_ref[...] = total


def ring(values, step):
    count = lax.axis_size("patch")
    return lax.ppermute(values, "patch", [(i, (i + step) % count) for i in range(count)])


def halving_orders():
    core_bit = lax.axis_size("patch")
    high = [core_bit << k for k in range(1, lax.axis_size("region").bit_length() - 1)]
    low = [1 << k for k in range(core_bit.bit_length() - 1)]
    return core_bit, high + low, low[:-1] + high + low[-1:]


def permute_by(values, first, second, core_bit):
    count = lax.axis_size("region") * lax.axis_size("patch")
    pairs = [(i, i ^ (second if i & core_bit else first)) for i in range(count)]
    return lax.ppermute(values, AXES, pairs)


def reduce_all(flat, vectors):
    core_bit, first, second = halving_orders()
    count = lax.axis_size("region") * lax.axis_size("patch")
    me = lax.axis_index(AXES)
    core = (me & core_bit) // core_bit
    depth = count.bit_length() - 1
    flat = flat.reshape((2,) * depth + (-1, flat.shape[1]))

    def ordered(order):
        axes = [depth - bit.bit_length() for bit in [core_bit] + order]
        return jnp.transpose(flat, axes + [depth, depth + 1])

    blocks = jnp.stack([ordered(first)[0], ordered(second)[1]]).reshape(2, -1, flat.shape[-1])
    kept = lax.dynamic_index_in_dim(blocks, core, 0, keepdims=False)
    sent = lax.dynamic_index_in_dim(blocks, 1 - core, 0, keepdims=False).astype(BF)
    got = permute_by(sent, core_bit, core_bit, core_bit)
    total = kept + got
    for one, two in zip(first, second):
        bit = jnp.where(core == 1, (me & two) // two, (me & one) // one)
        halves = total.reshape(2, -1, flat.shape[-1])
        kept = lax.dynamic_index_in_dim(halves, bit, 0, keepdims=False)
        sent = lax.dynamic_index_in_dim(halves, 1 - bit, 0, keepdims=False).astype(BF)
        got = permute_by(sent, one, two, core_bit)
        vectors = vectors + permute_by(vectors, one, two, core_bit)
        total = kept + got
    vectors = vectors + permute_by(vectors, core_bit, core_bit, core_bit)
    return total.reshape(-1), vectors.reshape(-1)


Sides = collections.namedtuple("Sides", ("weights", "early", "late", "last"))


class Halving:
    def __init__(self, rows, columns, orders, carries):
        self.core_bit, (self.first, self.second) = lax.axis_size("patch"), orders
        self.count = lax.axis_size("region") * lax.axis_size("patch")
        self.block = rows // self.count
        self.rows = rows // 2
        self.columns = columns
        self.width = columns.stop - columns.start
        self.steps = len(self.first)
        self.carries = carries

    def place(self, order, core, position):
        block = self.core_bit if core else 0
        for k, bit in enumerate(order):
            if (position >> (self.steps - 1 - k)) & 1:
                block |= bit
        return block * self.block

    def me(self):
        return lax.axis_index("region") * self.core_bit + lax.axis_index("patch")

    def core(self):
        return lax.rem(self.me() // self.core_bit, 2)

    def bit(self, step):
        me = self.me()
        one, two = self.first[step], self.second[step]
        return jnp.where(self.core() == 1, lax.rem(me // two, 2), lax.rem(me // one, 2))

    def source(self, position, core):
        zero, one = self.place(self.first, 0, position), self.place(self.second, 1, position)
        return pl.multiple_of(jnp.where(core == 1, one, zero), 8)

    def pieces(self, full):
        return full // self.width

    def extra(self, full):
        return 16 * self.pieces(full) if self.carries else 0

    def slots(self, step, rows):
        if not self.carries:
            return 0
        bits = (self.first[step], self.second[step])
        return rows if 1 in bits else rows // 2 if min(bits) < self.core_bit else 0

    def taken(self, step):
        place = lax.rem(self.me(), self.core_bit)
        even = lax.rem(place, 2) == 0
        answers = []
        for bit in (self.first[step], self.second[step]):
            if bit == 1 or bit > self.core_bit:
                answers.append((bit == 1, bit == 1))
                continue
            between = lax.rem(place, bit) // 2
            up = jnp.logical_and(even, between == 0)
            down = jnp.logical_and(jnp.logical_not(even), between == bit // 2 - 1)
            answers.append((up, down))
        core = self.core() == 1
        return tuple(jnp.where(core, b, a) for a, b in zip(*answers))


def halve(src_ref, got_ref, out_ref, plan, step, side):
    half = plan.rows >> (step + 1)
    bit = plan.bit(step)
    chosen = 1 - bit if side else bit
    if step:
        start = pl.multiple_of(chosen * half, 16)
        held = src_ref[pl.ds(start, half), :]
        out_ref[:half, :] = (held + got_ref[pl.ds(start, half), :]).astype(out_ref.dtype)
        return
    core = plan.core()
    per_half = half // plan.block
    for k in range(per_half):
        low, high = plan.source(k, core), plan.source(k + per_half, core)
        row = pl.multiple_of(jnp.where(chosen == 1, high, low), 8)
        held = src_ref[pl.ds(row, plan.block), :]
        start = pl.multiple_of(chosen * half + k * plan.block, 16)
        got = got_ref[pl.ds(start, plan.block), :]
        out_ref[k * plan.block : (k + 1) * plan.block, :] = (held + got).astype(out_ref.dtype)


def keep_kernel(src_ref, got_ref, out_ref, *, plan, step):
    halve(src_ref, got_ref, out_ref, plan, step, 0)


def unpack(got_ref, start, rows, plan, full):
    parts = [
        got_ref[start + k * rows : start + (k + 1) * rows, :] for k in range(plan.pieces(full))
    ]
    return jnp.concatenate(parts, axis=1).astype(F32)


def pack(out_ref, start, values, plan):
    rows = values.shape[0]
    for k in range(plan.pieces(values.shape[1])):
        out_ref[start + k * rows : start + (k + 1) * rows, :] = values[
            :, k * plan.width : (k + 1) * plan.width
        ].astype(BF)


def add_vectors(vec_ref, got_ref, start, plan):
    count, full = vec_ref.shape
    both = unpack(got_ref, start, 16, plan, full)
    return vec_ref[...] + (both[:count] + both[8 : 8 + count])


def move_halo(state_ref, got_ref, start, plan, step):
    rows, full = state_ref.shape
    half = rows // 2
    slots = plan.slots(step, rows)
    state = state_ref[...].astype(F32)
    if not slots:
        return state
    came = unpack(got_ref, start, slots, plan, full)
    up, down = plan.taken(step)
    return jnp.concatenate(
        [
            jnp.where(up, came[:half], state[:half]),
            jnp.where(down, came[slots - half :], state[half:]),
        ],
        axis=0,
    )


def send_kernel(src_ref, got_ref, *refs, plan, step):
    if not plan.carries:
        halve(src_ref, got_ref, refs[0], plan, step, 1)
        return
    vec_ref, state_ref, out_ref, new_ref, moved_ref = refs
    halve(src_ref, got_ref, out_ref, plan, step, 1)
    half = plan.rows >> (step + 1)
    count, full = vec_ref.shape
    vec, state = vec_ref[...], state_ref[...].astype(F32)
    if step:
        vec = add_vectors(vec_ref, got_ref, 2 * half, plan)
        state = move_halo(state_ref, got_ref, 2 * half + plan.extra(full), plan, step - 1)
    upper = vec.astype(BF).astype(F32)
    lower = (vec - upper).astype(BF).astype(F32)
    gap = jnp.zeros((8 - count, full), F32)
    pack(out_ref, half, jnp.concatenate([upper, gap, lower, gap], axis=0), plan)
    new_ref[...] = upper + lower
    moved_ref[...] = state.astype(BF)
    rows = state.shape[0]
    slots = plan.slots(step, rows)
    if slots == rows:
        pack(out_ref, half + plan.extra(full), state, plan)
    elif slots:
        even = lax.rem(plan.me(), 2) == 0
        pack(
            out_ref, half + plan.extra(full),
            jnp.where(even, state[: rows // 2], state[rows // 2 :]), plan,
        )


def carried_kernel(vec_ref, state_ref, got_ref, new_ref, moved_ref, *, plan):
    new_ref[...] = add_vectors(vec_ref, got_ref, plan.block, plan)
    start = plan.block + plan.extra(vec_ref.shape[1])
    moved_ref[...] = move_halo(state_ref, got_ref, start, plan, plan.steps - 1).astype(BF)


def close_kernel(lists_ref, partial_ref, back_ref, vec_ref, other_ref, *refs, plans):
    *refs, out_ref, vectors_ref, nodes_ref = refs
    rims_kernel(lists_ref, partial_ref, back_ref, nodes_ref)
    pieces = out_ref.shape[0] // plans[0].block
    for plan, held_ref, got_ref in zip(plans, refs[0::2], refs[1::2]):
        total = held_ref[...] + got_ref[: plan.block, :]
        for k in range(0, plan.width, LANES):
            piece = (plan.columns.start + k) // LANES
            out_ref[pl.ds(piece, plan.block, stride=pieces), :] = total[:, k : k + LANES]
    vec = vec_ref[...] + other_ref[...]
    for k in range(pieces):
        vectors_ref[pl.ds(k, vec.shape[0], stride=pieces), :] = vec[:, k * LANES : (k + 1) * LANES]


def after(marks, *values):
    return lax.optimization_barrier((*values, *marks))[: len(values)]


def reduce_kernels(plans, sides, vec, width):
    full = vec.shape[1]
    held, got = {}, {}
    marks = ()
    for plan in plans:
        held[plan], sent = sides.weights(plan, marks)
        marks = (sent,)
        got[plan] = permute_by(sent, plan.core_bit, plan.core_bit, plan.core_bit)
    state = sides.early(marks)
    marks = (state,)
    shapes = [(vec.shape, F32), (state.shape, BF)]
    for step in range(plans[0].steps):
        if step == 1:
            (nodes,) = marks = sides.late(marks)
        for plan in plans:
            half = plan.rows >> (step + 1)
            source, came = after(marks, held[plan], got[plan])
            rows = half + plan.extra(full) + plan.slots(step, state.shape[0]) * plan.pieces(full)
            carried = [near(vec), near(state)] if plan.carries else []
            sent, *new = call(
                functools.partial(send_kernel, plan=plan, step=step),
                [((rows, plan.width), BF)] + (shapes if plan.carries else []),
                near(source), near(came), *carried, name=f"send{step}",
            )
            if plan.carries:
                vec, state = new
            marks = (sent,)
            source, came = after(marks, source, came)
            incoming = permute_by(sent, plan.first[step], plan.second[step], plan.core_bit)
            (held[plan],) = call(
                functools.partial(keep_kernel, plan=plan, step=step),
                [((half, plan.width), F32)], near(source), near(came), name=f"keep{step}",
            )
            got[plan] = incoming
    (carrier,) = [plan for plan in plans if plan.carries]
    vec, state = call(
        functools.partial(carried_kernel, plan=carrier), shapes, near(vec), near(state),
        near(got[carrier]), name="carried",
    )
    other = permute_by(vec, carrier.core_bit, carrier.core_bit, carrier.core_bit)
    pairs = [near(a) for plan in plans for a in (held[plan], got[plan])]
    out, vectors, nodes = call(
        functools.partial(close_kernel, plans=plans),
        [
            ((plans[0].block * width // LANES, LANES), F32),
            ((vec.size // LANES, LANES), F32),
            (nodes.shape, F32),
        ],
        sides.last, near(nodes), near(state), near(vec), near(other), *pairs, name="close",
        plain=(0, 1, 2),
    )
    return out.reshape(-1), vectors.reshape(-1), nodes


def make_plans(rows, width, slots):
    count = lax.axis_size("region") * lax.axis_size("patch")
    core_bit, first, second = halving_orders()
    if rows % (16 * count) or width % (4 * LANES) or slots % 32:
        return []
    high = [b for b in first if b > core_bit]
    low = [b for b in first if b < core_bit]
    turned = low[1:-1] + high + low[:1] + low[-1:]
    quarter = width // 4
    chunks = CHUNKS
    return [
        Halving(
            rows, slice(a * quarter, b * quarter),
            (turned, turned) if kind else (first, second), i == 0,
        )
        for i, (a, b, kind) in enumerate(chunks)
    ]


PICK = 20 << 30
CHUNKS = ((0, 2, 0), (2, 4, 0))


def per_device(
    nodes, edges, node_cotan, edge_cotan, edge_inner, edge_outer, node_inner, node_outer, edge_shift,
    edge_offset, edge_gain, node_shift, node_offset, node_gain, send_rows, senders, receivers,
):
    count, width = nodes.shape
    edge_count = edges.shape[0]
    hidden_width = edge_outer.shape[0]
    lists = send_rows.reshape(send_rows.shape[2:])
    half = lists.shape[1]
    slots = 2 * half
    devices_all = lax.axis_size("region") * lax.axis_size("patch")
    edge_norm = 1.0 / math.sqrt(edge_count * devices_all)
    node_norm = 1.0 / math.sqrt(count * devices_all)
    picked = 2 * count + -(-slots // LANES) * LANES
    edge_rows = 3 * width + hidden_width
    weight_rows = edge_rows + 2 * width + hidden_width
    plans = make_plans(weight_rows, hidden_width, slots)
    edge_shift, edge_offset, edge_gain, node_shift, node_offset, node_gain = (
        v.reshape(1, -1)
        for v in (edge_shift, edge_offset, edge_gain, node_shift, node_offset, node_gain)
    )

    out_low, out_high = call(
        pick_kernel, [((half, width), BF)] * 2, lists, nodes, name="pick", limit=4 << 20, hbm=(0, 1), flops=PICK,
        scratch=[
            pltpu.VMEM(lists.shape, jnp.int32), pltpu.VMEM(nodes.shape, BF),
            pltpu.SemaphoreType.DMA((2,)),
        ],
    )
    low = ring(out_high, 1)
    high = ring(out_low, -1)

    part, npart, pick, turned = call(
        table_kernel,
        [
            ((edge_count, hidden_width), F32),
            ((count, hidden_width), F32),
            ((edge_count, picked), BF),
            ((picked, edge_count), BF),
        ],
        senders.reshape(1, -1), receivers.reshape(1, -1), edge_shift, nodes, edge_inner, edges,
        node_inner, node_shift,
        name="table", flops=4 * edge_count * width * hidden_width,
        scratch=[pltpu.VMEM((2 * count, hidden_width), BF)],
    )
    hidden, slope, normed, invstd, pulled, partial, node_sums, *node_terms = call(
        functools.partial(forward_kernel, scale=node_norm),
        [
            ((edge_count, hidden_width), BF),
            ((edge_count, hidden_width), F32),
            ((edge_count, width), F32),
            ((edge_count, 1), F32),
            ((count, width), BF),
            ((count, width), F32),
            ((3, width), F32),
            ((count, width), BF),
            ((count, hidden_width), BF),
            ((count, hidden_width), BF),
            ((count, width), BF),
        ],
        near(part), near(npart), near(pick), near(turned), near(low), near(high), edges,
        edge_inner, edge_outer, edge_offset, edge_gain, node_offset, node_gain,
        node_inner, node_outer, node_cotan, name="forward", flops=5 << 30,
    )
    fresh, preact, spread, sums, linear = call(
        functools.partial(backward_kernel, scale=edge_norm),
        [
            ((edge_count, width), F32),
            ((edge_count, hidden_width), BF),
            ((2 * count + slots, hidden_width), BF),
            ((6, width), F32),
            ((edge_count, width), BF),
        ],
        near(pick), near(turned), edge_cotan, near(normed), near(invstd), near(slope), near(pulled),
        edge_outer, edge_gain, near(node_sums),
        name="backward", flops=3 << 30,
    )

    def weights_of(plan, marks):
        preact_late, linear_late = after(marks, preact, linear)
        columns = plan.columns if plan else slice(0, hidden_width)
        chunk = columns.stop - columns.start
        sends = [((plan.rows, chunk), BF)] if plan else []
        return call(
            functools.partial(
                weights_kernel, columns=columns, scales=(edge_norm, node_norm), plan=plan
            ),
            [((weight_rows, chunk), F32)] + sends,
            edges, nodes, near(low), near(high), near(hidden), near(preact_late), near(linear_late),
            near(spread), *[near(a) for a in node_terms],
            name="weights", flops=chunk << 22,
        )

    results = {}

    def rim_side(marks):
        (spread_late,) = after(marks, spread)
        (rims,) = call(
            functools.partial(rim_kernel, count=count), [((slots, width), BF)],
            near(spread_late), edge_inner, name="rim", limit=4 << 20,
        )
        return rims

    def grads_side(marks):
        spread_late, fresh_late = after(marks, spread, fresh)
        results["nodes"], results["edges"] = call(
            grads_kernel,
            [((count, width), F32), ((edge_count, width), BF)],
            near(spread_late), edge_inner, near(partial), near(fresh_late), near(preact),
            name="grads", flops=2 << 30, plain=(1,),
        )
        return (results["nodes"],)

    if plans:
        grad_weights, grad_vectors, grad_nodes = reduce_kernels(
            plans, Sides(weights_of, rim_side, grads_side, lists), sums, hidden_width
        )
    else:
        grad_weights, grad_vectors = reduce_all(weights_of(None, ())[0], sums)
        rims = rim_side((sums,))
        back = jnp.concatenate([ring(rims[:half], 1), ring(rims[half:], -1)])
        grads_side((sums,))
        (grad_nodes,) = call(
            rims_kernel, [((count, width), F32)], lists, near(results["nodes"]), near(back),
            name="rims", plain=(0,), limit=4 << 20,
        )
    return (grad_nodes, results["edges"], grad_weights, grad_vectors)


def solution(mesh):
    in_specs = (
        P(AXES, None), P(AXES, None), P(AXES, None), P(AXES, None),
        P(), P(), P(), P(), P(), P(), P(), P(), P(), P(),
        P("region", "patch", None, None), P(AXES), P(AXES),
    )
    out_specs = (P(AXES, None), P(AXES, None), P(AXES), P())
    return jax.shard_map(
        per_device, mesh=mesh, in_specs=in_specs, out_specs=out_specs, check_vma=False
    )
```

```python
import collections
import functools
import math

import jax
import jax.numpy as jnp
from jax import lax
from jax.experimental import pallas as pl
from jax.experimental.pallas import tpu as pltpu
from jax.sharding import PartitionSpec as P

BF = jnp.bfloat16
F32 = jnp.float32
LANES = 128
VMEM = pltpu.VMEM
AXES = ("region", "patch")


def pinned(shape, dtype):
    return pltpu.VMEM(shape, dtype)


def mm(a, b):
    return jnp.dot(a, b, preferred_element_type=F32)


def mm_nt(a, b):
    return lax.dot_general(a, b, (((1,), (1,)), ((), ())), preferred_element_type=F32)


def mm_tn(a, b):
    return lax.dot_general(a, b, (((0,), (0,)), ((), ())), preferred_element_type=F32)


def call(body, outs, *args, flops=0, limit=24 << 20, name=None, plain=(), hbm=(), scratch=()):
    vmem = pl.BlockSpec(memory_space=pltpu.VMEM)
    anywhere = pl.BlockSpec(memory_space=pltpu.HBM)
    shapes = [
        jax.ShapeDtypeStruct(s, d) if i in plain else pinned(s, d) for i, (s, d) in enumerate(outs)
    ]
    moved = sum(math.prod(s) * jnp.dtype(d).itemsize for s, d in outs)
    return pl.pallas_call(
        body,
        out_shape=shapes,
        in_specs=[anywhere if i in hbm else vmem for i in range(len(args))],
        out_specs=[vmem] * len(outs),
        scratch_shapes=list(scratch),
        compiler_params=pltpu.CompilerParams(vmem_limit_bytes=limit),
        cost_estimate=pl.CostEstimate(flops=flops, bytes_accessed=moved, transcendentals=0),
        name=name,
    )(*[far(a) if i in hbm else a for i, a in enumerate(args)])


def far(array):
    return pltpu.with_memory_space_constraint(array, pltpu.HBM)


def near(array):
    return pltpu.with_memory_space_constraint(array, pltpu.VMEM)


def start_copies(pairs, sems):
    copies = [pltpu.make_async_copy(a, b, sems.at[i]) for i, (a, b) in enumerate(pairs)]
    for copy in copies:
        copy.start()
    return copies


def layer_norm(values):
    centred = values - jnp.mean(values, axis=-1, keepdims=True)
    invstd = lax.rsqrt(jnp.mean(centred * centred, axis=-1, keepdims=True) + 1e-05)
    return centred * invstd, invstd


def norm_back(upstream, normed, invstd, gains):
    scaled = upstream * gains
    return invstd * (
        scaled
        - jnp.mean(scaled, axis=-1, keepdims=True)
        - normed * jnp.mean(scaled * normed, axis=-1, keepdims=True)
    )


def silu_and_slope(preact):
    gate = 1.0 / (1.0 + jnp.exp(-preact))
    hidden = preact * gate
    return hidden, gate + hidden * (1.0 - gate)


def column_sum(values):
    return jnp.sum(values, axis=0, keepdims=True)


def pick_kernel(lists_hbm, nodes_hbm, low_ref, high_ref, lists_ref, nodes_ref, sems):
    for copy in start_copies([(lists_hbm, lists_ref), (nodes_hbm, nodes_ref)], sems):
        copy.wait()
    slots, count = lists_ref.shape[1], nodes_ref.shape[0]
    rows = lax.broadcasted_iota(jnp.int32, (count, slots), 0)
    for k, out_ref in enumerate((low_ref, high_ref)):
        pick = jnp.where(rows == lists_ref[k : k + 1, :], 1.0, 0.0).astype(BF)
        out_ref[...] = mm_tn(pick, nodes_ref[...]).astype(BF)


def table_kernel(
    senders_ref, receivers_ref, shift_ref, nodes_ref, inner_ref, edges_ref, ninner_ref, nshift_ref,
    part_ref, npart_ref, pick_ref, turned_ref, own_ref,
):
    edge_count, width = edges_ref.shape
    count = nodes_ref.shape[0]
    senders = senders_ref[...]
    receivers = receivers_ref[...] + count
    senders = jnp.where(senders < count, senders, senders + count)
    wide_send = jnp.transpose(jnp.broadcast_to(senders, (LANES, edge_count)))
    wide_recv = jnp.transpose(jnp.broadcast_to(receivers, (LANES, edge_count)))
    lane = lax.broadcasted_iota(jnp.int32, (edge_count, LANES), 1)
    row = lax.broadcasted_iota(jnp.int32, (LANES, edge_count), 0)
    for start in range(0, pick_ref.shape[1], LANES):
        own_part = count <= start < 2 * count
        tall = wide_recv if own_part else wide_send
        flat = receivers if own_part else senders
        pick_ref[:, start : start + LANES] = jnp.where(tall == lane + start, 1.0, 0.0).astype(BF)
        turned_ref[start : start + LANES, :] = jnp.where(flat == row + start, 1.0, 0.0).astype(BF)
    nodes = nodes_ref[...]
    own_ref[:count, :] = mm(nodes, inner_ref[width : 2 * width, :]).astype(BF)
    own_ref[count:, :] = mm(nodes, inner_ref[2 * width :, :]).astype(BF)
    tile = edge_count // 2
    for start in range(0, edge_count, tile):
        rows = slice(start, start + tile)
        part_ref[rows, :] = (
            mm(edges_ref[rows, :], inner_ref[:width, :])
            + mm(pick_ref[rows, : 2 * count], own_ref[...])
            + shift_ref[...]
        )
    npart_ref[...] = mm(nodes, ninner_ref[:width, :]) + nshift_ref[...]


def forward_kernel(
    part_ref, npart_ref, pick_ref, turned_ref, low_ref, high_ref, edges_ref,
    einner_ref, eouter_ref, eoffset_ref, egain_ref, noffset_ref, ngain_ref,
    ninner_ref, nouter_ref, cotan_ref,
    hidden_ref, slope_ref, normed_ref, invstd_ref, pulled_ref, partial_ref, sums_ref,
    aggregate_ref, node_hidden_ref, node_preact_ref, node_linear_ref,
    *, scale,
):
    edge_count, width = edges_ref.shape
    count = cotan_ref.shape[0]
    rim = jnp.concatenate([low_ref[...], high_ref[...]], axis=0)
    far = mm(rim, einner_ref[width : 2 * width, :]).astype(BF)
    slots = rim.shape[0]
    tile = edge_count // 2
    tiles = [slice(start, start + tile) for start in range(0, edge_count, tile)]

    def first(rows):
        return part_ref[rows, :] + mm(pick_ref[rows, 2 * count : 2 * count + slots], far)

    def second(rows, preact):
        hidden, slope = silu_and_slope(preact)
        hidden = hidden.astype(BF)
        hidden_ref[rows, :] = hidden
        slope_ref[rows, :] = slope
        return mm(hidden, eouter_ref[...]) + eoffset_ref[...]

    def third(rows, linear):
        normed, invstd = layer_norm(linear)
        normed_ref[rows, :] = normed
        invstd_ref[rows, :] = invstd
        fresh = (edges_ref[rows, :].astype(F32) + egain_ref[...] * normed).astype(BF)
        return mm(turned_ref[count : 2 * count, rows], fresh)

    preacts = [first(rows) for rows in tiles]
    linears = [second(rows, preact) for rows, preact in zip(tiles, preacts)]
    total = sum(third(rows, linear) for rows, linear in zip(tiles, linears))
    aggregate = total.astype(BF)
    preact = npart_ref[...] + mm(aggregate, ninner_ref[width:, :])
    hidden, slope = silu_and_slope(preact)
    hidden = hidden.astype(BF)
    normed, invstd = layer_norm(mm(hidden, nouter_ref[...]) + noffset_ref[...])
    cotan = cotan_ref[...].astype(F32)
    linear_back = norm_back(cotan, normed, invstd, ngain_ref[...])
    linear_half = linear_back.astype(BF)
    preact_back = mm_nt(linear_half, nouter_ref[...]) * slope
    preact_half = preact_back.astype(BF)
    pulled_ref[...] = mm_nt(preact_half, ninner_ref[width:, :]).astype(BF)
    partial_ref[...] = cotan + mm_nt(preact_half, ninner_ref[:width, :])
    aggregate_ref[...] = aggregate
    node_hidden_ref[...] = hidden
    node_preact_ref[...] = preact_half
    node_linear_ref[...] = linear_half
    sums_ref[0:1, :] = column_sum(preact_back) * scale
    sums_ref[1:2, :] = column_sum(linear_back) * scale
    sums_ref[2:3, :] = column_sum(cotan * normed) * scale


def backward_kernel(
    pick_ref, turned_ref, ecotan_ref, normed_ref, invstd_ref, slope_ref, pulled_ref, eouter_ref,
    egain_ref, node_sums_ref,
    fresh_ref, preact_ref, spread_ref, sums_ref, linear_ref, *, scale,
):
    edge_count = ecotan_ref.shape[0]
    count = pulled_ref.shape[0]
    tile = edge_count // 2
    tiles = [slice(start, start + tile) for start in range(0, edge_count, tile)]
    sums = [0.0, 0.0, 0.0]

    def first(rows):
        return ecotan_ref[rows, :].astype(F32) + mm(
            pick_ref[rows, count : 2 * count], pulled_ref[...]
        )

    def second(rows, fresh_back):
        fresh_ref[rows, :] = fresh_back
        normed = normed_ref[rows, :]
        linear_back = norm_back(fresh_back, normed, invstd_ref[rows, :], egain_ref[...])
        linear_half = linear_back.astype(BF)
        linear_ref[rows, :] = linear_half
        sums[1] += column_sum(linear_back)
        sums[2] += column_sum(fresh_back * normed)
        return mm_nt(linear_half, eouter_ref[...])

    def third(rows, back):
        preact_back = back * slope_ref[rows, :]
        preact_ref[rows, :] = preact_back.astype(BF)
        sums[0] += column_sum(preact_back)

    fresh_backs = [first(rows) for rows in tiles]
    backs = [second(rows, fresh_back) for rows, fresh_back in zip(tiles, fresh_backs)]
    for rows, back in zip(tiles, backs):
        third(rows, back)
    for k in range(3):
        sums_ref[k : k + 1, :] = sums[k] * scale
    sums_ref[3:, :] = node_sums_ref[...]
    used = spread_ref.shape[0]
    spread_ref[...] = mm(turned_ref[:used, :], preact_ref[...]).astype(BF)


def weights_kernel(
    edges_ref, nodes_ref, low_ref, high_ref, hidden_ref, preact_ref, linear_ref, spread_ref,
    aggregate_ref, node_hidden_ref, node_preact_ref, node_linear_ref,
    weights_ref, *sends, columns, scales, plan,
):
    count = nodes_ref.shape[0]
    nodes = nodes_ref[...]
    rim = jnp.concatenate([low_ref[...], high_ref[...]], axis=0)
    node_preact = node_preact_ref[:, columns]
    start = 0
    for scale, terms in (
        (scales[0], [(edges_ref[...], preact_ref[:, columns])]),
        (scales[0], [(nodes, spread_ref[:count, columns]), (rim, spread_ref[2 * count :, columns])]),
        (scales[0], [(nodes, spread_ref[count : 2 * count, columns])]),
        (scales[0], [(hidden_ref[...], linear_ref[:, columns])]),
        (scales[1], [(nodes, node_preact)]),
        (scales[1], [(aggregate_ref[...], node_preact)]),
        (scales[1], [(node_hidden_ref[...], node_linear_ref[:, columns])]),
    ):
        value = sum(mm_tn(a, b) for a, b in terms) * scale
        weights_ref[start : start + value.shape[0], :] = value
        start += value.shape[0]
    for send_ref in sends:
        other = 1 - plan.core()
        for position in range(plan.count // 2):
            row = position * plan.block
            send_ref[row : row + plan.block, :] = weights_ref[
                pl.ds(plan.source(position, other), plan.block), :
            ].astype(BF)


def rim_kernel(spread_ref, inner_ref, out_ref, *, count):
    width, slots = spread_ref.shape[1], out_ref.shape[0]
    rows = mm_nt(spread_ref[2 * count :, :], inner_ref[width : 2 * width, :]).astype(BF)
    out_ref[: slots // 2, :] = rows[slots // 2 :]
    out_ref[slots // 2 :, :] = rows[: slots // 2]


def grads_kernel(spread_ref, inner_ref, partial_ref, fresh_ref, preact_ref, nodes_ref, edges_ref):
    count, width = partial_ref.shape
    nodes_ref[...] = (
        partial_ref[...]
        + mm_nt(spread_ref[:count, :], inner_ref[width : 2 * width, :])
        + mm_nt(spread_ref[count : 2 * count, :], inner_ref[2 * width :, :])
    )
    edge_count = preact_ref.shape[0]
    tile = edge_count // 2
    for start in range(0, edge_count, tile):
        rows = slice(start, start + tile)
        edges_ref[rows, :] = (
            fresh_ref[rows, :] + mm_nt(preact_ref[rows, :], inner_ref[:width, :])
        ).astype(BF)


def rims_kernel(lists_ref, partial_ref, back_ref, out_ref):
    count, half = partial_ref.shape[0], lists_ref.shape[1]
    rows = lax.broadcasted_iota(jnp.int32, (count, half), 0)
    total = partial_ref[...]
    for k in range(2):
        pick = jnp.where(rows == lists_ref[k : k + 1, :], 1.0, 0.0).astype(BF)
        total += mm(pick, back_ref[k * half : (k + 1) * half, :])
    out_ref[...] = total


def ring(values, step):
    count = lax.axis_size("patch")
    return lax.ppermute(values, "patch", [(i, (i + step) % count) for i in range(count)])


def halving_orders():
    core_bit = lax.axis_size("patch")
    high = [core_bit << k for k in range(1, lax.axis_size("region").bit_length() - 1)]
    low = [1 << k for k in range(core_bit.bit_length() - 1)]
    return core_bit, high + low, low + high


def permute_by(values, first, second, core_bit):
    count = lax.axis_size("region") * lax.axis_size("patch")
    pairs = [(i, i ^ (second if i & core_bit else first)) for i in range(count)]
    return lax.ppermute(values, AXES, pairs)


def reduce_all(flat, vectors):
    core_bit, first, second = halving_orders()
    count = lax.axis_size("region") * lax.axis_size("patch")
    me = lax.axis_index(AXES)
    core = (me & core_bit) // core_bit
    depth = count.bit_length() - 1
    flat = flat.reshape((2,) * depth + (-1, flat.shape[1]))

    def ordered(order):
        axes = [depth - bit.bit_length() for bit in [core_bit] + order]
        return jnp.transpose(flat, axes + [depth, depth + 1])

    blocks = jnp.stack([ordered(first)[0], ordered(second)[1]]).reshape(2, -1, flat.shape[-1])
    kept = lax.dynamic_index_in_dim(blocks, core, 0, keepdims=False)
    sent = lax.dynamic_index_in_dim(blocks, 1 - core, 0, keepdims=False).astype(BF)
    got = permute_by(sent, core_bit, core_bit, core_bit)
    total = kept + got
    for one, two in zip(first, second):
        bit = jnp.where(core == 1, (me & two) // two, (me & one) // one)
        halves = total.reshape(2, -1, flat.shape[-1])
        kept = lax.dynamic_index_in_dim(halves, bit, 0, keepdims=False)
        sent = lax.dynamic_index_in_dim(halves, 1 - bit, 0, keepdims=False).astype(BF)
        got = permute_by(sent, one, two, core_bit)
        vectors = vectors + permute_by(vectors, one, two, core_bit)
        total = kept + got
    vectors = vectors + permute_by(vectors, core_bit, core_bit, core_bit)
    return total.reshape(-1), vectors.reshape(-1)


Sides = collections.namedtuple("Sides", ("weights", "early", "late", "last"))


class Halving:
    def __init__(self, rows, columns, orders, carries):
        self.core_bit, (self.first, self.second) = lax.axis_size("patch"), orders
        self.count = lax.axis_size("region") * lax.axis_size("patch")
        self.block = rows // self.count
        self.rows = rows // 2
        self.columns = columns
        self.width = columns.stop - columns.start
        self.steps = len(self.first)
        self.carries = carries

    def place(self, order, core, position):
        block = self.core_bit if core else 0
        for k, bit in enumerate(order):
            if (position >> (self.steps - 1 - k)) & 1:
                block |= bit
        return block * self.block

    def me(self):
        return lax.axis_index("region") * self.core_bit + lax.axis_index("patch")

    def core(self):
        return lax.rem(self.me() // self.core_bit, 2)

    def bit(self, step):
        me = self.me()
        one, two = self.first[step], self.second[step]
        return jnp.where(self.core() == 1, lax.rem(me // two, 2), lax.rem(me // one, 2))

    def source(self, position, core):
        zero, one = self.place(self.first, 0, position), self.place(self.second, 1, position)
        return pl.multiple_of(jnp.where(core == 1, one, zero), 8)

    def pieces(self, full):
        return full // self.width

    def extra(self, full):
        return 16 * self.pieces(full) if self.carries else 0

    def slots(self, step, rows):
        if not self.carries:
            return 0
        bits = (self.first[step], self.second[step])
        return rows if 1 in bits else rows // 2 if min(bits) < self.core_bit else 0

    def taken(self, step):
        place = lax.rem(self.me(), self.core_bit)
        even = lax.rem(place, 2) == 0
        answers = []
        for bit in (self.first[step], self.second[step]):
            if bit == 1 or bit > self.core_bit:
                answers.append((bit == 1, bit == 1))
                continue
            between = lax.rem(place, bit) // 2
            up = jnp.logical_and(even, between == 0)
            down = jnp.logical_and(jnp.logical_not(even), between == bit // 2 - 1)
            answers.append((up, down))
        core = self.core() == 1
        return tuple(jnp.where(core, b, a) for a, b in zip(*answers))


def halve(src_ref, got_ref, out_ref, plan, step, side):
    half = plan.rows >> (step + 1)
    bit = plan.bit(step)
    chosen = 1 - bit if side else bit
    if step:
        start = pl.multiple_of(chosen * half, 16)
        held = src_ref[pl.ds(start, half), :]
        out_ref[:half, :] = (held + got_ref[pl.ds(start, half), :]).astype(out_ref.dtype)
        return
    core = plan.core()
    per_half = half // plan.block
    for k in range(per_half):
        low, high = plan.source(k, core), plan.source(k + per_half, core)
        row = pl.multiple_of(jnp.where(chosen == 1, high, low), 8)
        held = src_ref[pl.ds(row, plan.block), :]
        start = pl.multiple_of(chosen * half + k * plan.block, 16)
        got = got_ref[pl.ds(start, plan.block), :]
        out_ref[k * plan.block : (k + 1) * plan.block, :] = (held + got).astype(out_ref.dtype)


def keep_kernel(src_ref, got_ref, out_ref, *, plan, step):
    halve(src_ref, got_ref, out_ref, plan, step, 0)


def unpack(got_ref, start, rows, plan, full):
    parts = [
        got_ref[start + k * rows : start + (k + 1) * rows, :] for k in range(plan.pieces(full))
    ]
    return jnp.concatenate(parts, axis=1).astype(F32)


def pack(out_ref, start, values, plan):
    rows = values.shape[0]
    for k in range(plan.pieces(values.shape[1])):
        out_ref[start + k * rows : start + (k + 1) * rows, :] = values[
            :, k * plan.width : (k + 1) * plan.width
        ].astype(BF)


def add_vectors(vec_ref, got_ref, start, plan):
    count, full = vec_ref.shape
    both = unpack(got_ref, start, 16, plan, full)
    return vec_ref[...] + (both[:count] + both[8 : 8 + count])


def move_halo(state_ref, got_ref, start, plan, step):
    rows, full = state_ref.shape
    half = rows // 2
    slots = plan.slots(step, rows)
    state = state_ref[...].astype(F32)
    if not slots:
        return state
    came = unpack(got_ref, start, slots, plan, full)
    up, down = plan.taken(step)
    return jnp.concatenate(
        [
            jnp.where(up, came[:half], state[:half]),
            jnp.where(down, came[slots - half :], state[half:]),
        ],
        axis=0,
    )


def send_kernel(src_ref, got_ref, *refs, plan, step):
    if not plan.carries:
        halve(src_ref, got_ref, refs[0], plan, step, 1)
        return
    vec_ref, state_ref, out_ref, new_ref, moved_ref = refs
    halve(src_ref, got_ref, out_ref, plan, step, 1)
    half = plan.rows >> (step + 1)
    count, full = vec_ref.shape
    vec, state = vec_ref[...], state_ref[...].astype(F32)
    if step:
        vec = add_vectors(vec_ref, got_ref, 2 * half, plan)
        state = move_halo(state_ref, got_ref, 2 * half + plan.extra(full), plan, step - 1)
    upper = vec.astype(BF).astype(F32)
    lower = (vec - upper).astype(BF).astype(F32)
    gap = jnp.zeros((8 - count, full), F32)
    pack(out_ref, half, jnp.concatenate([upper, gap, lower, gap], axis=0), plan)
    new_ref[...] = upper + lower
    moved_ref[...] = state.astype(BF)
    rows = state.shape[0]
    slots = plan.slots(step, rows)
    if slots == rows:
        pack(out_ref, half + plan.extra(full), state, plan)
    elif slots:
        even = lax.rem(plan.me(), 2) == 0
        pack(
            out_ref, half + plan.extra(full),
            jnp.where(even, state[: rows // 2], state[rows // 2 :]), plan,
        )


def carried_kernel(vec_ref, state_ref, got_ref, new_ref, moved_ref, *, plan):
    new_ref[...] = add_vectors(vec_ref, got_ref, plan.block, plan)
    start = plan.block + plan.extra(vec_ref.shape[1])
    moved_ref[...] = move_halo(state_ref, got_ref, start, plan, plan.steps - 1).astype(BF)


def close_kernel(lists_ref, partial_ref, back_ref, vec_ref, other_ref, *refs, plans):
    *refs, out_ref, vectors_ref, nodes_ref = refs
    rims_kernel(lists_ref, partial_ref, back_ref, nodes_ref)
    pieces = out_ref.shape[0] // plans[0].block
    for plan, held_ref, got_ref in zip(plans, refs[0::2], refs[1::2]):
        total = held_ref[...] + got_ref[: plan.block, :]
        for k in range(0, plan.width, LANES):
            piece = (plan.columns.start + k) // LANES
            out_ref[pl.ds(piece, plan.block, stride=pieces), :] = total[:, k : k + LANES]
    vec = vec_ref[...] + other_ref[...]
    for k in range(pieces):
        vectors_ref[pl.ds(k, vec.shape[0], stride=pieces), :] = vec[:, k * LANES : (k + 1) * LANES]


def after(marks, *values):
    return lax.optimization_barrier((*values, *marks))[: len(values)]


def reduce_kernels(plans, sides, vec, width):
    full = vec.shape[1]
    held, got = {}, {}
    marks = ()
    for plan in plans:
        held[plan], sent = sides.weights(plan, marks)
        marks = (sent,)
        got[plan] = permute_by(sent, plan.core_bit, plan.core_bit, plan.core_bit)
    state = sides.early(marks)
    marks = (state,)
    shapes = [(vec.shape, F32), (state.shape, BF)]
    for step in range(plans[0].steps):
        if step == 1:
            (nodes,) = marks = sides.late(marks)
        for plan in plans:
            half = plan.rows >> (step + 1)
            source, came = after(marks, held[plan], got[plan])
            rows = half + plan.extra(full) + plan.slots(step, state.shape[0]) * plan.pieces(full)
            carried = [near(vec), near(state)] if plan.carries else []
            sent, *new = call(
                functools.partial(send_kernel, plan=plan, step=step),
                [((rows, plan.width), BF)] + (shapes if plan.carries else []),
                near(source), near(came), *carried, name=f"send{step}",
            )
            if plan.carries:
                vec, state = new
            marks = (sent,)
            source, came = after(marks, source, came)
            incoming = permute_by(sent, plan.first[step], plan.second[step], plan.core_bit)
            (held[plan],) = call(
                functools.partial(keep_kernel, plan=plan, step=step),
                [((half, plan.width), F32)], near(source), near(came), name=f"keep{step}",
            )
            got[plan] = incoming
    (carrier,) = [plan for plan in plans if plan.carries]
    vec, state = call(
        functools.partial(carried_kernel, plan=carrier), shapes, near(vec), near(state),
        near(got[carrier]), name="carried",
    )
    other = permute_by(vec, carrier.core_bit, carrier.core_bit, carrier.core_bit)
    pairs = [near(a) for plan in plans for a in (held[plan], got[plan])]
    out, vectors, nodes = call(
        functools.partial(close_kernel, plans=plans),
        [
            ((plans[0].block * width // LANES, LANES), F32),
            ((vec.size // LANES, LANES), F32),
            (nodes.shape, F32),
        ],
        sides.last, near(nodes), near(state), near(vec), near(other), *pairs, name="close",
        plain=(0, 1, 2),
    )
    return out.reshape(-1), vectors.reshape(-1), nodes


def make_plans(rows, width, slots):
    count = lax.axis_size("region") * lax.axis_size("patch")
    core_bit, first, second = halving_orders()
    if rows % (16 * count) or width % (4 * LANES) or slots % 32:
        return []
    high = [b for b in sorted(first) if b > core_bit]
    low = [b for b in sorted(first) if b < core_bit]
    turned = low[1:-1] + high + low[:1] + low[-1:]
    quarter = width // 4
    chunks = CHUNKS
    return [
        Halving(
            rows, slice(a * quarter, b * quarter),
            (turned, turned) if kind else (first, second), i == 0,
        )
        for i, (a, b, kind) in enumerate(chunks)
    ]


PICK = 20 << 30
CHUNKS = ((0, 2, 0), (2, 4, 0))


def per_device(
    nodes, edges, node_cotan, edge_cotan, edge_inner, edge_outer, node_inner, node_outer, edge_shift,
    edge_offset, edge_gain, node_shift, node_offset, node_gain, send_rows, senders, receivers,
):
    count, width = nodes.shape
    edge_count = edges.shape[0]
    hidden_width = edge_outer.shape[0]
    lists = send_rows.reshape(send_rows.shape[2:])
    half = lists.shape[1]
    slots = 2 * half
    devices_all = lax.axis_size("region") * lax.axis_size("patch")
    edge_norm = 1.0 / math.sqrt(edge_count * devices_all)
    node_norm = 1.0 / math.sqrt(count * devices_all)
    picked = 2 * count + -(-slots // LANES) * LANES
    edge_rows = 3 * width + hidden_width
    weight_rows = edge_rows + 2 * width + hidden_width
    plans = make_plans(weight_rows, hidden_width, slots)
    edge_shift, edge_offset, edge_gain, node_shift, node_offset, node_gain = (
        v.reshape(1, -1)
        for v in (edge_shift, edge_offset, edge_gain, node_shift, node_offset, node_gain)
    )

    out_low, out_high = call(
        pick_kernel, [((half, width), BF)] * 2, lists, nodes, name="pick", limit=4 << 20, hbm=(0, 1), flops=PICK,
        scratch=[
            pltpu.VMEM(lists.shape, jnp.int32), pltpu.VMEM(nodes.shape, BF),
            pltpu.SemaphoreType.DMA((2,)),
        ],
    )
    low = ring(out_high, 1)
    high = ring(out_low, -1)

    part, npart, pick, turned = call(
        table_kernel,
        [
            ((edge_count, hidden_width), F32),
            ((count, hidden_width), F32),
            ((edge_count, picked), BF),
            ((picked, edge_count), BF),
        ],
        senders.reshape(1, -1), receivers.reshape(1, -1), edge_shift, nodes, edge_inner, edges,
        node_inner, node_shift,
        name="table", flops=4 * edge_count * width * hidden_width,
        scratch=[pltpu.VMEM((2 * count, hidden_width), BF)],
    )
    hidden, slope, normed, invstd, pulled, partial, node_sums, *node_terms = call(
        functools.partial(forward_kernel, scale=node_norm),
        [
            ((edge_count, hidden_width), BF),
            ((edge_count, hidden_width), F32),
            ((edge_count, width), F32),
            ((edge_count, 1), F32),
            ((count, width), BF),
            ((count, width), F32),
            ((3, width), F32),
            ((count, width), BF),
            ((count, hidden_width), BF),
            ((count, hidden_width), BF),
            ((count, width), BF),
        ],
        near(part), near(npart), near(pick), near(turned), near(low), near(high), edges,
        edge_inner, edge_outer, edge_offset, edge_gain, node_offset, node_gain,
        node_inner, node_outer, node_cotan, name="forward", flops=5 << 30,
    )
    fresh, preact, spread, sums, linear = call(
        functools.partial(backward_kernel, scale=edge_norm),
        [
            ((edge_count, width), F32),
            ((edge_count, hidden_width), BF),
            ((2 * count + slots, hidden_width), BF),
            ((6, width), F32),
            ((edge_count, width), BF),
        ],
        near(pick), near(turned), edge_cotan, near(normed), near(invstd), near(slope), near(pulled),
        edge_outer, edge_gain, near(node_sums),
        name="backward", flops=3 << 30,
    )

    def weights_of(plan, marks):
        preact_late, linear_late = after(marks, preact, linear)
        columns = plan.columns if plan else slice(0, hidden_width)
        chunk = columns.stop - columns.start
        sends = [((plan.rows, chunk), BF)] if plan else []
        return call(
            functools.partial(
                weights_kernel, columns=columns, scales=(edge_norm, node_norm), plan=plan
            ),
            [((weight_rows, chunk), F32)] + sends,
            edges, nodes, near(low), near(high), near(hidden), near(preact_late), near(linear_late),
            near(spread), *[near(a) for a in node_terms],
            name="weights", flops=chunk << 22,
        )

    results = {}

    def rim_side(marks):
        (spread_late,) = after(marks, spread)
        (rims,) = call(
            functools.partial(rim_kernel, count=count), [((slots, width), BF)],
            near(spread_late), edge_inner, name="rim", limit=4 << 20,
        )
        return rims

    def grads_side(marks):
        spread_late, fresh_late = after(marks, spread, fresh)
        results["nodes"], results["edges"] = call(
            grads_kernel,
            [((count, width), F32), ((edge_count, width), BF)],
            near(spread_late), edge_inner, near(partial), near(fresh_late), near(preact),
            name="grads", flops=2 << 30, plain=(1,),
        )
        return (results["nodes"],)

    if plans:
        grad_weights, grad_vectors, grad_nodes = reduce_kernels(
            plans, Sides(weights_of, rim_side, grads_side, lists), sums, hidden_width
        )
    else:
        grad_weights, grad_vectors = reduce_all(weights_of(None, ())[0], sums)
        rims = rim_side((sums,))
        back = jnp.concatenate([ring(rims[:half], 1), ring(rims[half:], -1)])
        grads_side((sums,))
        (grad_nodes,) = call(
            rims_kernel, [((count, width), F32)], lists, near(results["nodes"]), near(back),
            name="rims", plain=(0,), limit=4 << 20,
        )
    return (grad_nodes, results["edges"], grad_weights, grad_vectors)


def solution(mesh):
    in_specs = (
        P(AXES, None), P(AXES, None), P(AXES, None), P(AXES, None),
        P(), P(), P(), P(), P(), P(), P(), P(), P(), P(),
        P("region", "patch", None, None), P(AXES), P(AXES),
    )
    out_specs = (P(AXES, None), P(AXES, None), P(AXES), P())
    return jax.shard_map(
        per_device, mesh=mesh, in_specs=in_specs, out_specs=out_specs, check_vma=False
    )
```

```python
import collections
import functools
import math

import jax
import jax.numpy as jnp
from jax import lax
from jax.experimental import pallas as pl
from jax.experimental.pallas import tpu as pltpu
from jax.sharding import PartitionSpec as P

BF = jnp.bfloat16
F32 = jnp.float32
LANES = 128
VMEM = pltpu.VMEM
AXES = ("region", "patch")


def pinned(shape, dtype):
    return pltpu.VMEM(shape, dtype)


def mm(a, b):
    return jnp.dot(a, b, preferred_element_type=F32)


def mm_nt(a, b):
    return lax.dot_general(a, b, (((1,), (1,)), ((), ())), preferred_element_type=F32)


def mm_tn(a, b):
    return lax.dot_general(a, b, (((0,), (0,)), ((), ())), preferred_element_type=F32)


def call(body, outs, *args, flops=0, limit=24 << 20, name=None, plain=(), hbm=(), scratch=()):
    vmem = pl.BlockSpec(memory_space=pltpu.VMEM)
    anywhere = pl.BlockSpec(memory_space=pltpu.HBM)
    shapes = [
        jax.ShapeDtypeStruct(s, d) if i in plain else pinned(s, d) for i, (s, d) in enumerate(outs)
    ]
    moved = sum(math.prod(s) * jnp.dtype(d).itemsize for s, d in outs)
    return pl.pallas_call(
        body,
        out_shape=shapes,
        in_specs=[anywhere if i in hbm else vmem for i in range(len(args))],
        out_specs=[vmem] * len(outs),
        scratch_shapes=list(scratch),
        compiler_params=pltpu.CompilerParams(vmem_limit_bytes=limit),
        cost_estimate=pl.CostEstimate(flops=flops, bytes_accessed=moved, transcendentals=0),
        name=name,
    )(*[far(a) if i in hbm else a for i, a in enumerate(args)])


def far(array):
    return pltpu.with_memory_space_constraint(array, pltpu.HBM)


def near(array):
    return pltpu.with_memory_space_constraint(array, pltpu.VMEM)


def start_copies(pairs, sems):
    copies = [pltpu.make_async_copy(a, b, sems.at[i]) for i, (a, b) in enumerate(pairs)]
    for copy in copies:
        copy.start()
    return copies


def layer_norm(values):
    centred = values - jnp.mean(values, axis=-1, keepdims=True)
    invstd = lax.rsqrt(jnp.mean(centred * centred, axis=-1, keepdims=True) + 1e-05)
    return centred * invstd, invstd


def norm_back(upstream, normed, invstd, gains):
    scaled = upstream * gains
    return invstd * (
        scaled
        - jnp.mean(scaled, axis=-1, keepdims=True)
        - normed * jnp.mean(scaled * normed, axis=-1, keepdims=True)
    )


def silu_and_slope(preact):
    gate = 1.0 / (1.0 + jnp.exp(-preact))
    hidden = preact * gate
    return hidden, gate + hidden * (1.0 - gate)


def column_sum(values):
    return jnp.sum(values, axis=0, keepdims=True)


def pick_kernel(lists_hbm, nodes_hbm, low_ref, high_ref, lists_ref, nodes_ref, sems):
    for copy in start_copies([(lists_hbm, lists_ref), (nodes_hbm, nodes_ref)], sems):
        copy.wait()
    slots, count = lists_ref.shape[1], nodes_ref.shape[0]
    rows = lax.broadcasted_iota(jnp.int32, (count, slots), 0)
    for k, out_ref in enumerate((low_ref, high_ref)):
        pick = jnp.where(rows == lists_ref[k : k + 1, :], 1.0, 0.0).astype(BF)
        out_ref[...] = mm_tn(pick, nodes_ref[...]).astype(BF)


def table_kernel(
    senders_ref, receivers_ref, shift_ref, nodes_ref, inner_ref, edges_ref, ninner_ref, nshift_ref,
    part_ref, npart_ref, pick_ref, turned_ref, edges_turned_ref, own_ref,
):
    edge_count, width = edges_ref.shape
    count = nodes_ref.shape[0]
    senders = senders_ref[...]
    receivers = receivers_ref[...] + count
    senders = jnp.where(senders < count, senders, senders + count)
    wide_send = jnp.transpose(jnp.broadcast_to(senders, (LANES, edge_count)))
    wide_recv = jnp.transpose(jnp.broadcast_to(receivers, (LANES, edge_count)))
    lane = lax.broadcasted_iota(jnp.int32, (edge_count, LANES), 1)
    row = lax.broadcasted_iota(jnp.int32, (LANES, edge_count), 0)
    for start in range(0, pick_ref.shape[1], LANES):
        own_part = count <= start < 2 * count
        tall = wide_recv if own_part else wide_send
        flat = receivers if own_part else senders
        pick_ref[:, start : start + LANES] = jnp.where(tall == lane + start, 1.0, 0.0).astype(BF)
        turned_ref[start : start + LANES, :] = jnp.where(flat == row + start, 1.0, 0.0).astype(BF)
    nodes = nodes_ref[...]
    own_ref[:count, :] = mm(nodes, inner_ref[width : 2 * width, :]).astype(BF)
    own_ref[count:, :] = mm(nodes, inner_ref[2 * width :, :]).astype(BF)
    tile = edge_count // 2
    for start in range(0, edge_count, tile):
        rows = slice(start, start + tile)
        part_ref[rows, :] = (
            mm(edges_ref[rows, :], inner_ref[:width, :])
            + mm(pick_ref[rows, : 2 * count], own_ref[...])
            + shift_ref[...]
        )
    npart_ref[...] = mm(nodes, ninner_ref[:width, :]) + nshift_ref[...]
    edges_turned_ref[...] = edges_ref[...].T


def forward_kernel(
    part_ref, npart_ref, pick_ref, turned_ref, low_ref, high_ref, edges_ref,
    einner_ref, eouter_ref, eoffset_ref, egain_ref, noffset_ref, ngain_ref,
    ninner_ref, nouter_ref, cotan_ref,
    hidden_ref, slope_ref, normed_ref, invstd_ref, pulled_ref, partial_ref, sums_ref,
    aggregate_ref, node_hidden_ref, node_preact_ref, node_linear_ref,
    *, scale,
):
    edge_count, width = edges_ref.shape
    count = cotan_ref.shape[0]
    rim = jnp.concatenate([low_ref[...], high_ref[...]], axis=0)
    far = mm(rim, einner_ref[width : 2 * width, :]).astype(BF)
    slots = rim.shape[0]
    tile = edge_count // 2
    tiles = [slice(start, start + tile) for start in range(0, edge_count, tile)]

    def first(rows):
        return part_ref[rows, :] + mm(pick_ref[rows, 2 * count : 2 * count + slots], far)

    def second(rows, preact):
        hidden, slope = silu_and_slope(preact)
        hidden = hidden.astype(BF)
        hidden_ref[rows, :] = hidden
        slope_ref[rows, :] = slope
        return mm(hidden, eouter_ref[...]) + eoffset_ref[...]

    def third(rows, linear):
        normed, invstd = layer_norm(linear)
        normed_ref[rows, :] = normed
        invstd_ref[rows, :] = invstd
        fresh = (edges_ref[rows, :].astype(F32) + egain_ref[...] * normed).astype(BF)
        return mm(turned_ref[count : 2 * count, rows], fresh)

    preacts = [first(rows) for rows in tiles]
    linears = [second(rows, preact) for rows, preact in zip(tiles, preacts)]
    total = sum(third(rows, linear) for rows, linear in zip(tiles, linears))
    aggregate = total.astype(BF)
    preact = npart_ref[...] + mm(aggregate, ninner_ref[width:, :])
    hidden, slope = silu_and_slope(preact)
    hidden = hidden.astype(BF)
    normed, invstd = layer_norm(mm(hidden, nouter_ref[...]) + noffset_ref[...])
    cotan = cotan_ref[...].astype(F32)
    linear_back = norm_back(cotan, normed, invstd, ngain_ref[...])
    linear_half = linear_back.astype(BF)
    preact_back = mm_nt(linear_half, nouter_ref[...]) * slope
    preact_half = preact_back.astype(BF)
    pulled_ref[...] = mm_nt(preact_half, ninner_ref[width:, :]).astype(BF)
    partial_ref[...] = cotan + mm_nt(preact_half, ninner_ref[:width, :])
    aggregate_ref[...] = aggregate
    node_hidden_ref[...] = hidden
    node_preact_ref[...] = preact_half
    node_linear_ref[...] = linear_half
    sums_ref[0:1, :] = column_sum(preact_back) * scale
    sums_ref[1:2, :] = column_sum(linear_back) * scale
    sums_ref[2:3, :] = column_sum(cotan * normed) * scale


def backward_kernel(
    pick_ref, turned_ref, ecotan_ref, normed_ref, invstd_ref, slope_ref, pulled_ref, eouter_ref,
    egain_ref, node_sums_ref,
    fresh_ref, preact_ref, spread_ref, sums_ref, linear_ref, *, scale,
):
    edge_count = ecotan_ref.shape[0]
    count = pulled_ref.shape[0]
    tile = edge_count // 2
    tiles = [slice(start, start + tile) for start in range(0, edge_count, tile)]
    sums = [0.0, 0.0, 0.0]

    def first(rows):
        return ecotan_ref[rows, :].astype(F32) + mm(
            pick_ref[rows, count : 2 * count], pulled_ref[...]
        )

    def second(rows, fresh_back):
        fresh_ref[rows, :] = fresh_back
        normed = normed_ref[rows, :]
        linear_back = norm_back(fresh_back, normed, invstd_ref[rows, :], egain_ref[...])
        linear_half = linear_back.astype(BF)
        linear_ref[rows, :] = linear_half
        sums[1] += column_sum(linear_back)
        sums[2] += column_sum(fresh_back * normed)
        return mm_nt(linear_half, eouter_ref[...])

    def third(rows, back):
        preact_back = back * slope_ref[rows, :]
        preact_ref[rows, :] = preact_back.astype(BF)
        sums[0] += column_sum(preact_back)

    fresh_backs = [first(rows) for rows in tiles]
    backs = [second(rows, fresh_back) for rows, fresh_back in zip(tiles, fresh_backs)]
    for rows, back in zip(tiles, backs):
        third(rows, back)
    for k in range(3):
        sums_ref[k : k + 1, :] = sums[k] * scale
    sums_ref[3:, :] = node_sums_ref[...]
    used = spread_ref.shape[0]
    spread_ref[...] = mm(turned_ref[:used, :], preact_ref[...]).astype(BF)


def weights_kernel(
    edges_turned_ref, nodes_ref, low_ref, high_ref, hidden_ref, preact_ref, linear_ref, spread_ref,
    aggregate_ref, node_hidden_ref, node_preact_ref, node_linear_ref,
    weights_ref, *sends, columns, scales, plan,
):
    count = nodes_ref.shape[0]
    nodes = nodes_ref[...]
    rim = jnp.concatenate([low_ref[...], high_ref[...]], axis=0)
    node_preact = node_preact_ref[:, columns]
    chunk = columns.stop - columns.start
    by_nodes = mm_tn(
        nodes,
        jnp.concatenate(
            [spread_ref[:count, columns], spread_ref[count : 2 * count, columns], node_preact], axis=1
        ),
    )
    start = 0
    for scale, term in (
        (scales[0], mm(edges_turned_ref[...], preact_ref[:, columns])),
        (scales[0], by_nodes[:, :chunk] + mm_tn(rim, spread_ref[2 * count :, columns])),
        (scales[0], by_nodes[:, chunk : 2 * chunk]),
        (scales[0], mm_tn(hidden_ref[...], linear_ref[:, columns])),
        (scales[1], by_nodes[:, 2 * chunk :]),
        (scales[1], mm_tn(aggregate_ref[...], node_preact)),
        (scales[1], mm_tn(node_hidden_ref[...], node_linear_ref[:, columns])),
    ):
        value = term * scale
        weights_ref[start : start + value.shape[0], :] = value
        start += value.shape[0]
    for send_ref in sends:
        other = 1 - plan.core()
        for position in range(plan.count // 2):
            row = position * plan.block
            send_ref[row : row + plan.block, :] = weights_ref[
                pl.ds(plan.source(position, other), plan.block), :
            ].astype(BF)


def rim_kernel(spread_ref, inner_ref, out_ref, *, count):
    width, slots = spread_ref.shape[1], out_ref.shape[0]
    rows = mm_nt(spread_ref[2 * count :, :], inner_ref[width : 2 * width, :]).astype(BF)
    out_ref[: slots // 2, :] = rows[slots // 2 :]
    out_ref[slots // 2 :, :] = rows[: slots // 2]


def grads_kernel(spread_ref, inner_ref, partial_ref, fresh_ref, preact_ref, nodes_ref, edges_ref):
    count, width = partial_ref.shape
    nodes_ref[...] = (
        partial_ref[...]
        + mm_nt(spread_ref[:count, :], inner_ref[width : 2 * width, :])
        + mm_nt(spread_ref[count : 2 * count, :], inner_ref[2 * width :, :])
    )
    edge_count = preact_ref.shape[0]
    tile = edge_count // 2
    for start in range(0, edge_count, tile):
        rows = slice(start, start + tile)
        edges_ref[rows, :] = (
            fresh_ref[rows, :] + mm_nt(preact_ref[rows, :], inner_ref[:width, :])
        ).astype(BF)


def rims_kernel(lists_ref, partial_ref, back_ref, out_ref):
    count, half = partial_ref.shape[0], lists_ref.shape[1]
    rows = lax.broadcasted_iota(jnp.int32, (count, half), 0)
    total = partial_ref[...]
    for k in range(2):
        pick = jnp.where(rows == lists_ref[k : k + 1, :], 1.0, 0.0).astype(BF)
        total += mm(pick, back_ref[k * half : (k + 1) * half, :])
    out_ref[...] = total


def ring(values, step):
    count = lax.axis_size("patch")
    return lax.ppermute(values, "patch", [(i, (i + step) % count) for i in range(count)])


def halving_orders():
    core_bit = lax.axis_size("patch")
    high = [core_bit << k for k in range(1, lax.axis_size("region").bit_length() - 1)]
    low = [1 << k for k in range(core_bit.bit_length() - 1)]
    return core_bit, high + low, low + high


def permute_by(values, first, second, core_bit):
    count = lax.axis_size("region") * lax.axis_size("patch")
    pairs = [(i, i ^ (second if i & core_bit else first)) for i in range(count)]
    return lax.ppermute(values, AXES, pairs)


def reduce_all(flat, vectors):
    core_bit, first, second = halving_orders()
    count = lax.axis_size("region") * lax.axis_size("patch")
    me = lax.axis_index(AXES)
    core = (me & core_bit) // core_bit
    depth = count.bit_length() - 1
    flat = flat.reshape((2,) * depth + (-1, flat.shape[1]))

    def ordered(order):
        axes = [depth - bit.bit_length() for bit in [core_bit] + order]
        return jnp.transpose(flat, axes + [depth, depth + 1])

    blocks = jnp.stack([ordered(first)[0], ordered(second)[1]]).reshape(2, -1, flat.shape[-1])
    kept = lax.dynamic_index_in_dim(blocks, core, 0, keepdims=False)
    sent = lax.dynamic_index_in_dim(blocks, 1 - core, 0, keepdims=False).astype(BF)
    got = permute_by(sent, core_bit, core_bit, core_bit)
    total = kept + got
    for one, two in zip(first, second):
        bit = jnp.where(core == 1, (me & two) // two, (me & one) // one)
        halves = total.reshape(2, -1, flat.shape[-1])
        kept = lax.dynamic_index_in_dim(halves, bit, 0, keepdims=False)
        sent = lax.dynamic_index_in_dim(halves, 1 - bit, 0, keepdims=False).astype(BF)
        got = permute_by(sent, one, two, core_bit)
        vectors = vectors + permute_by(vectors, one, two, core_bit)
        total = kept + got
    vectors = vectors + permute_by(vectors, core_bit, core_bit, core_bit)
    return total.reshape(-1), vectors.reshape(-1)


Sides = collections.namedtuple("Sides", ("weights", "early", "late", "last"))


class Halving:
    def __init__(self, rows, columns, orders, carries):
        self.core_bit, (self.first, self.second) = lax.axis_size("patch"), orders
        self.count = lax.axis_size("region") * lax.axis_size("patch")
        self.block = rows // self.count
        self.rows = rows // 2
        self.columns = columns
        self.width = columns.stop - columns.start
        self.steps = len(self.first)
        self.carries = carries

    def place(self, order, core, position):
        block = self.core_bit if core else 0
        for k, bit in enumerate(order):
            if (position >> (self.steps - 1 - k)) & 1:
                block |= bit
        return block * self.block

    def me(self):
        return lax.axis_index("region") * self.core_bit + lax.axis_index("patch")

    def core(self):
        return lax.rem(self.me() // self.core_bit, 2)

    def bit(self, step):
        me = self.me()
        one, two = self.first[step], self.second[step]
        return jnp.where(self.core() == 1, lax.rem(me // two, 2), lax.rem(me // one, 2))

    def source(self, position, core):
        zero, one = self.place(self.first, 0, position), self.place(self.second, 1, position)
        return pl.multiple_of(jnp.where(core == 1, one, zero), 8)

    def pieces(self, full):
        return full // self.width

    def extra(self, full):
        return 16 * self.pieces(full) if self.carries else 0

    def slots(self, step, rows):
        if not self.carries:
            return 0
        bits = (self.first[step], self.second[step])
        return rows if 1 in bits else rows // 2 if min(bits) < self.core_bit else 0

    def taken(self, step):
        place = lax.rem(self.me(), self.core_bit)
        even = lax.rem(place, 2) == 0
        answers = []
        for bit in (self.first[step], self.second[step]):
            if bit == 1 or bit > self.core_bit:
                answers.append((bit == 1, bit == 1))
                continue
            between = lax.rem(place, bit) // 2
            up = jnp.logical_and(even, between == 0)
            down = jnp.logical_and(jnp.logical_not(even), between == bit // 2 - 1)
            answers.append((up, down))
        core = self.core() == 1
        return tuple(jnp.where(core, b, a) for a, b in zip(*answers))


def halve(src_ref, got_ref, out_ref, plan, step, side):
    half = plan.rows >> (step + 1)
    bit = plan.bit(step)
    chosen = 1 - bit if side else bit
    if step:
        start = pl.multiple_of(chosen * half, 16)
        held = src_ref[pl.ds(start, half), :]
        out_ref[:half, :] = (held + got_ref[pl.ds(start, half), :]).astype(out_ref.dtype)
        return
    core = plan.core()
    per_half = half // plan.block
    for k in range(per_half):
        low, high = plan.source(k, core), plan.source(k + per_half, core)
        row = pl.multiple_of(jnp.where(chosen == 1, high, low), 8)
        held = src_ref[pl.ds(row, plan.block), :]
        start = pl.multiple_of(chosen * half + k * plan.block, 16)
        got = got_ref[pl.ds(start, plan.block), :]
        out_ref[k * plan.block : (k + 1) * plan.block, :] = (held + got).astype(out_ref.dtype)


def keep_kernel(src_ref, got_ref, out_ref, *, plan, step):
    halve(src_ref, got_ref, out_ref, plan, step, 0)


def unpack(got_ref, start, rows, plan, full):
    parts = [
        got_ref[start + k * rows : start + (k + 1) * rows, :] for k in range(plan.pieces(full))
    ]
    return jnp.concatenate(parts, axis=1).astype(F32)


def pack(out_ref, start, values, plan):
    rows = values.shape[0]
    for k in range(plan.pieces(values.shape[1])):
        out_ref[start + k * rows : start + (k + 1) * rows, :] = values[
            :, k * plan.width : (k + 1) * plan.width
        ].astype(BF)


def add_vectors(vec_ref, got_ref, start, plan):
    count, full = vec_ref.shape
    both = unpack(got_ref, start, 16, plan, full)
    return vec_ref[...] + (both[:count] + both[8 : 8 + count])


def move_halo(state_ref, got_ref, start, plan, step):
    rows, full = state_ref.shape
    half = rows // 2
    slots = plan.slots(step, rows)
    state = state_ref[...].astype(F32)
    if not slots:
        return state
    came = unpack(got_ref, start, slots, plan, full)
    up, down = plan.taken(step)
    return jnp.concatenate(
        [
            jnp.where(up, came[:half], state[:half]),
            jnp.where(down, came[slots - half :], state[half:]),
        ],
        axis=0,
    )


def send_kernel(src_ref, got_ref, *refs, plan, step):
    if not plan.carries:
        halve(src_ref, got_ref, refs[0], plan, step, 1)
        return
    vec_ref, state_ref, out_ref, new_ref, moved_ref = refs
    halve(src_ref, got_ref, out_ref, plan, step, 1)
    half = plan.rows >> (step + 1)
    count, full = vec_ref.shape
    vec, state = vec_ref[...], state_ref[...].astype(F32)
    if step:
        vec = add_vectors(vec_ref, got_ref, 2 * half, plan)
        state = move_halo(state_ref, got_ref, 2 * half + plan.extra(full), plan, step - 1)
    upper = vec.astype(BF).astype(F32)
    lower = (vec - upper).astype(BF).astype(F32)
    gap = jnp.zeros((8 - count, full), F32)
    pack(out_ref, half, jnp.concatenate([upper, gap, lower, gap], axis=0), plan)
    new_ref[...] = upper + lower
    moved_ref[...] = state.astype(BF)
    rows = state.shape[0]
    slots = plan.slots(step, rows)
    if slots == rows:
        pack(out_ref, half + plan.extra(full), state, plan)
    elif slots:
        even = lax.rem(plan.me(), 2) == 0
        pack(
            out_ref, half + plan.extra(full),
            jnp.where(even, state[: rows // 2], state[rows // 2 :]), plan,
        )


def carried_kernel(vec_ref, state_ref, got_ref, new_ref, moved_ref, *, plan):
    new_ref[...] = add_vectors(vec_ref, got_ref, plan.block, plan)
    start = plan.block + plan.extra(vec_ref.shape[1])
    moved_ref[...] = move_halo(state_ref, got_ref, start, plan, plan.steps - 1).astype(BF)


def close_kernel(vec_ref, other_ref, *refs, plans):
    *refs, out_ref, vectors_ref = refs
    pieces = out_ref.shape[0] // plans[0].block
    for plan, held_ref, got_ref in zip(plans, refs[0::2], refs[1::2]):
        total = held_ref[...] + got_ref[: plan.block, :]
        for k in range(0, plan.width, LANES):
            piece = (plan.columns.start + k) // LANES
            out_ref[pl.ds(piece, plan.block, stride=pieces), :] = total[:, k : k + LANES]
    vec = vec_ref[...] + other_ref[...]
    for k in range(pieces):
        vectors_ref[pl.ds(k, vec.shape[0], stride=pieces), :] = vec[:, k * LANES : (k + 1) * LANES]


def after(marks, *values):
    return lax.optimization_barrier((*values, *marks))[: len(values)]


def reduce_kernels(plans, sides, vec, width):
    full = vec.shape[1]
    held, got = {}, {}
    marks, state = (), None
    for plan in plans:
        held[plan], sent = sides.weights(plan, marks)
        marks = (sent,)
        got[plan] = permute_by(sent, plan.core_bit, plan.core_bit, plan.core_bit)
        if state is None:
            state = sides.early(marks)
            marks = (state,)
    shapes = [(vec.shape, F32), (state.shape, BF)]
    for step in range(plans[0].steps):
        if step == 1:
            (nodes,) = marks = sides.late(marks)
        for plan in plans:
            half = plan.rows >> (step + 1)
            source, came = after(marks, held[plan], got[plan])
            rows = half + plan.extra(full) + plan.slots(step, state.shape[0]) * plan.pieces(full)
            carried = [near(vec), near(state)] if plan.carries else []
            sent, *new = call(
                functools.partial(send_kernel, plan=plan, step=step),
                [((rows, plan.width), BF)] + (shapes if plan.carries else []),
                near(source), near(came), *carried, name=f"send{step}",
            )
            if plan.carries:
                vec, state = new
            marks = (sent,)
            source, came = after(marks, source, came)
            incoming = permute_by(sent, plan.first[step], plan.second[step], plan.core_bit)
            (held[plan],) = call(
                functools.partial(keep_kernel, plan=plan, step=step),
                [((half, plan.width), F32)], near(source), near(came), name=f"keep{step}",
            )
            got[plan] = incoming
    (carrier,) = [plan for plan in plans if plan.carries]
    vec, state = call(
        functools.partial(carried_kernel, plan=carrier), shapes, near(vec), near(state),
        near(got[carrier]), name="carried",
    )
    other = permute_by(vec, carrier.core_bit, carrier.core_bit, carrier.core_bit)
    pairs = [near(a) for plan in plans for a in (held[plan], got[plan])]
    (nodes,) = call(
        rims_kernel, [(nodes.shape, F32)], sides.last, near(nodes), near(state), name="rims",
        plain=(0,), limit=4 << 20,
    )
    out, vectors = call(
        functools.partial(close_kernel, plans=plans),
        [
            ((plans[0].block * width // LANES, LANES), F32),
            ((vec.size // LANES, LANES), F32),
        ],
        near(vec), near(other), *pairs, name="close", plain=(0, 1),
    )
    return out.reshape(-1), vectors.reshape(-1), nodes


def make_plans(rows, width, slots):
    count = lax.axis_size("region") * lax.axis_size("patch")
    core_bit, first, second = halving_orders()
    if rows % (16 * count) or width % (4 * LANES) or slots % 32:
        return []
    high = [b for b in sorted(first) if b > core_bit]
    low = [b for b in sorted(first) if b < core_bit]
    turned = low[1:-1] + high + low[:1] + low[-1:]
    quarter = width // 4
    chunks = CHUNKS
    return [
        Halving(
            rows, slice(a * quarter, b * quarter),
            (turned, turned) if kind else (first, second), i == 0,
        )
        for i, (a, b, kind) in enumerate(chunks)
    ]


PICK = 20 << 30
CHUNKS = ((0, 2, 0), (2, 4, 0))


def per_device(
    nodes, edges, node_cotan, edge_cotan, edge_inner, edge_outer, node_inner, node_outer, edge_shift,
    edge_offset, edge_gain, node_shift, node_offset, node_gain, send_rows, senders, receivers,
):
    count, width = nodes.shape
    edge_count = edges.shape[0]
    hidden_width = edge_outer.shape[0]
    lists = send_rows.reshape(send_rows.shape[2:])
    half = lists.shape[1]
    slots = 2 * half
    devices_all = lax.axis_size("region") * lax.axis_size("patch")
    edge_norm = 1.0 / math.sqrt(edge_count * devices_all)
    node_norm = 1.0 / math.sqrt(count * devices_all)
    picked = 2 * count + -(-slots // LANES) * LANES
    edge_rows = 3 * width + hidden_width
    weight_rows = edge_rows + 2 * width + hidden_width
    plans = make_plans(weight_rows, hidden_width, slots)
    edge_shift, edge_offset, edge_gain, node_shift, node_offset, node_gain = (
        v.reshape(1, -1)
        for v in (edge_shift, edge_offset, edge_gain, node_shift, node_offset, node_gain)
    )

    out_low, out_high = call(
        pick_kernel, [((half, width), BF)] * 2, lists, nodes, name="pick", limit=4 << 20, hbm=(0, 1), flops=PICK,
        scratch=[
            pltpu.VMEM(lists.shape, jnp.int32), pltpu.VMEM(nodes.shape, BF),
            pltpu.SemaphoreType.DMA((2,)),
        ],
    )
    low = ring(out_high, 1)
    high = ring(out_low, -1)

    part, npart, pick, turned, edges_turned = call(
        table_kernel,
        [
            ((edge_count, hidden_width), F32),
            ((count, hidden_width), F32),
            ((edge_count, picked), BF),
            ((picked, edge_count), BF),
            ((width, edge_count), BF),
        ],
        senders.reshape(1, -1), receivers.reshape(1, -1), edge_shift, nodes, edge_inner, edges,
        node_inner, node_shift,
        name="table", flops=4 * edge_count * width * hidden_width,
        scratch=[pltpu.VMEM((2 * count, hidden_width), BF)],
    )
    hidden, slope, normed, invstd, pulled, partial, node_sums, *node_terms = call(
        functools.partial(forward_kernel, scale=node_norm),
        [
            ((edge_count, hidden_width), BF),
            ((edge_count, hidden_width), F32),
            ((edge_count, width), F32),
            ((edge_count, 1), F32),
            ((count, width), BF),
            ((count, width), F32),
            ((3, width), F32),
            ((count, width), BF),
            ((count, hidden_width), BF),
            ((count, hidden_width), BF),
            ((count, width), BF),
        ],
        near(part), near(npart), near(pick), near(turned), near(low), near(high), edges,
        edge_inner, edge_outer, edge_offset, edge_gain, node_offset, node_gain,
        node_inner, node_outer, node_cotan, name="forward", flops=5 << 30,
    )
    fresh, preact, spread, sums, linear = call(
        functools.partial(backward_kernel, scale=edge_norm),
        [
            ((edge_count, width), F32),
            ((edge_count, hidden_width), BF),
            ((2 * count + slots, hidden_width), BF),
            ((6, width), F32),
            ((edge_count, width), BF),
        ],
        near(pick), near(turned), edge_cotan, near(normed), near(invstd), near(slope), near(pulled),
        edge_outer, edge_gain, near(node_sums),
        name="backward", flops=3 << 30,
    )

    def weights_of(plan, marks):
        preact_late, linear_late = after(marks, preact, linear)
        columns = plan.columns if plan else slice(0, hidden_width)
        chunk = columns.stop - columns.start
        sends = [((plan.rows, chunk), BF)] if plan else []
        return call(
            functools.partial(
                weights_kernel, columns=columns, scales=(edge_norm, node_norm), plan=plan
            ),
            [((weight_rows, chunk), F32)] + sends,
            near(edges_turned), nodes, near(low), near(high), near(hidden), near(preact_late), near(linear_late),
            near(spread), *[near(a) for a in node_terms],
            name="weights", flops=chunk << 22,
        )

    results = {}

    def rim_side(marks):
        (spread_late,) = after(marks, spread)
        (rims,) = call(
            functools.partial(rim_kernel, count=count), [((slots, width), BF)],
            near(spread_late), edge_inner, name="rim", limit=4 << 20,
        )
        return rims

    def grads_side(marks):
        spread_late, fresh_late = after(marks, spread, fresh)
        results["nodes"], results["edges"] = call(
            grads_kernel,
            [((count, width), F32), ((edge_count, width), BF)],
            near(spread_late), edge_inner, near(partial), near(fresh_late), near(preact),
            name="grads", flops=2 << 30, plain=(1,),
        )
        return (results["nodes"],)

    if plans:
        grad_weights, grad_vectors, grad_nodes = reduce_kernels(
            plans, Sides(weights_of, rim_side, grads_side, lists), sums, hidden_width
        )
    else:
        grad_weights, grad_vectors = reduce_all(weights_of(None, ())[0], sums)
        rims = rim_side((sums,))
        back = jnp.concatenate([ring(rims[:half], 1), ring(rims[half:], -1)])
        grads_side((sums,))
        (grad_nodes,) = call(
            rims_kernel, [((count, width), F32)], lists, near(results["nodes"]), near(back),
            name="rims", plain=(0,), limit=4 << 20,
        )
    return (grad_nodes, results["edges"], grad_weights, grad_vectors)


def solution(mesh):
    in_specs = (
        P(AXES, None), P(AXES, None), P(AXES, None), P(AXES, None),
        P(), P(), P(), P(), P(), P(), P(), P(), P(), P(),
        P("region", "patch", None, None), P(AXES), P(AXES),
    )
    out_specs = (P(AXES, None), P(AXES, None), P(AXES), P())
    return jax.shard_map(
        per_device, mesh=mesh, in_specs=in_specs, out_specs=out_specs, check_vma=False
    )
```

```python
import collections
import functools
import math

import jax
import jax.numpy as jnp
from jax import lax
from jax.experimental import pallas as pl
from jax.experimental.pallas import tpu as pltpu
from jax.sharding import PartitionSpec as P

BF = jnp.bfloat16
F32 = jnp.float32
LANES = 128
VMEM = pltpu.VMEM
AXES = ("region", "patch")


def pinned(shape, dtype):
    return pltpu.VMEM(shape, dtype)


def mm(a, b):
    return jnp.dot(a, b, preferred_element_type=F32)


def mm_nt(a, b):
    return lax.dot_general(a, b, (((1,), (1,)), ((), ())), preferred_element_type=F32)


def mm_tn(a, b):
    return lax.dot_general(a, b, (((0,), (0,)), ((), ())), preferred_element_type=F32)


def call(body, outs, *args, flops=0, limit=24 << 20, name=None, plain=(), hbm=(), scratch=()):
    vmem = pl.BlockSpec(memory_space=pltpu.VMEM)
    anywhere = pl.BlockSpec(memory_space=pltpu.HBM)
    shapes = [
        jax.ShapeDtypeStruct(s, d) if i in plain else pinned(s, d) for i, (s, d) in enumerate(outs)
    ]
    moved = sum(math.prod(s) * jnp.dtype(d).itemsize for s, d in outs)
    return pl.pallas_call(
        body,
        out_shape=shapes,
        in_specs=[anywhere if i in hbm else vmem for i in range(len(args))],
        out_specs=[vmem] * len(outs),
        scratch_shapes=list(scratch),
        compiler_params=pltpu.CompilerParams(vmem_limit_bytes=limit),
        cost_estimate=pl.CostEstimate(flops=flops, bytes_accessed=moved, transcendentals=0),
        name=name,
    )(*[far(a) if i in hbm else a for i, a in enumerate(args)])


def far(array):
    return pltpu.with_memory_space_constraint(array, pltpu.HBM)


def near(array):
    return pltpu.with_memory_space_constraint(array, pltpu.VMEM)


def start_copies(pairs, sems):
    copies = [pltpu.make_async_copy(a, b, sems.at[i]) for i, (a, b) in enumerate(pairs)]
    for copy in copies:
        copy.start()
    return copies


def layer_norm(values):
    centred = values - jnp.mean(values, axis=-1, keepdims=True)
    invstd = lax.rsqrt(jnp.mean(centred * centred, axis=-1, keepdims=True) + 1e-05)
    return centred * invstd, invstd


def norm_back(upstream, normed, invstd, gains):
    scaled = upstream * gains
    return invstd * (
        scaled
        - jnp.mean(scaled, axis=-1, keepdims=True)
        - normed * jnp.mean(scaled * normed, axis=-1, keepdims=True)
    )


def silu_and_slope(preact):
    gate = 1.0 / (1.0 + jnp.exp(-preact))
    hidden = preact * gate
    return hidden, gate + hidden * (1.0 - gate)


def column_sum(values):
    return jnp.sum(values, axis=0, keepdims=True)


def pick_kernel(lists_hbm, nodes_hbm, low_ref, high_ref, lists_ref, nodes_ref, sems):
    for copy in start_copies([(lists_hbm, lists_ref), (nodes_hbm, nodes_ref)], sems):
        copy.wait()
    slots, count = lists_ref.shape[1], nodes_ref.shape[0]
    rows = lax.broadcasted_iota(jnp.int32, (count, slots), 0)
    for k, out_ref in enumerate((low_ref, high_ref)):
        pick = jnp.where(rows == lists_ref[k : k + 1, :], 1.0, 0.0).astype(BF)
        out_ref[...] = mm_tn(pick, nodes_ref[...]).astype(BF)


def table_kernel(
    senders_ref, receivers_ref, shift_ref, nodes_ref, inner_ref, edges_ref, ninner_ref, nshift_ref,
    part_ref, npart_ref, pick_ref, turned_ref, edges_turned_ref, own_ref,
):
    edge_count, width = edges_ref.shape
    count = nodes_ref.shape[0]
    senders = senders_ref[...]
    receivers = receivers_ref[...] + count
    senders = jnp.where(senders < count, senders, senders + count)
    wide_send = jnp.transpose(jnp.broadcast_to(senders, (LANES, edge_count)))
    wide_recv = jnp.transpose(jnp.broadcast_to(receivers, (LANES, edge_count)))
    lane = lax.broadcasted_iota(jnp.int32, (edge_count, LANES), 1)
    row = lax.broadcasted_iota(jnp.int32, (LANES, edge_count), 0)
    for start in range(0, pick_ref.shape[1], LANES):
        own_part = count <= start < 2 * count
        tall = wide_recv if own_part else wide_send
        flat = receivers if own_part else senders
        pick_ref[:, start : start + LANES] = jnp.where(tall == lane + start, 1.0, 0.0).astype(BF)
        turned_ref[start : start + LANES, :] = jnp.where(flat == row + start, 1.0, 0.0).astype(BF)
    nodes = nodes_ref[...]
    own_ref[:count, :] = mm(nodes, inner_ref[width : 2 * width, :]).astype(BF)
    own_ref[count:, :] = mm(nodes, inner_ref[2 * width :, :]).astype(BF)
    tile = edge_count // 2
    for start in range(0, edge_count, tile):
        rows = slice(start, start + tile)
        part_ref[rows, :] = (
            mm(edges_ref[rows, :], inner_ref[:width, :])
            + mm(pick_ref[rows, : 2 * count], own_ref[...])
            + shift_ref[...]
        )
    npart_ref[...] = mm(nodes, ninner_ref[:width, :]) + nshift_ref[...]
    edges_turned_ref[...] = edges_ref[...].T


def forward_kernel(
    part_ref, npart_ref, pick_ref, turned_ref, low_ref, high_ref, edges_ref,
    einner_ref, eouter_ref, eoffset_ref, egain_ref, noffset_ref, ngain_ref,
    ninner_ref, nouter_ref, cotan_ref,
    hidden_ref, slope_ref, normed_ref, invstd_ref, pulled_ref, partial_ref, sums_ref,
    aggregate_ref, node_hidden_ref, node_preact_ref, node_linear_ref,
    *, scale,
):
    edge_count, width = edges_ref.shape
    count = cotan_ref.shape[0]
    rim = jnp.concatenate([low_ref[...], high_ref[...]], axis=0)
    far = mm(rim, einner_ref[width : 2 * width, :]).astype(BF)
    slots = rim.shape[0]
    tile = edge_count // 1
    tiles = [slice(start, start + tile) for start in range(0, edge_count, tile)]

    def first(rows):
        return part_ref[rows, :] + mm(pick_ref[rows, 2 * count : 2 * count + slots], far)

    def second(rows, preact):
        hidden, slope = silu_and_slope(preact)
        hidden = hidden.astype(BF)
        hidden_ref[rows, :] = hidden
        slope_ref[rows, :] = slope
        return mm(hidden, eouter_ref[...]) + eoffset_ref[...]

    def third(rows, linear):
        normed, invstd = layer_norm(linear)
        normed_ref[rows, :] = normed
        invstd_ref[rows, :] = invstd
        fresh = (edges_ref[rows, :].astype(F32) + egain_ref[...] * normed).astype(BF)
        return mm(turned_ref[count : 2 * count, rows], fresh)

    preacts = [first(rows) for rows in tiles]
    linears = [second(rows, preact) for rows, preact in zip(tiles, preacts)]
    total = sum(third(rows, linear) for rows, linear in zip(tiles, linears))
    aggregate = total.astype(BF)
    preact = npart_ref[...] + mm(aggregate, ninner_ref[width:, :])
    hidden, slope = silu_and_slope(preact)
    hidden = hidden.astype(BF)
    normed, invstd = layer_norm(mm(hidden, nouter_ref[...]) + noffset_ref[...])
    cotan = cotan_ref[...].astype(F32)
    linear_back = norm_back(cotan, normed, invstd, ngain_ref[...])
    linear_half = linear_back.astype(BF)
    preact_back = mm_nt(linear_half, nouter_ref[...]) * slope
    preact_half = preact_back.astype(BF)
    pulled_ref[...] = mm_nt(preact_half, ninner_ref[width:, :]).astype(BF)
    partial_ref[...] = cotan + mm_nt(preact_half, ninner_ref[:width, :])
    aggregate_ref[...] = aggregate
    node_hidden_ref[...] = hidden
    node_preact_ref[...] = preact_half
    node_linear_ref[...] = linear_half
    sums_ref[0:1, :] = column_sum(preact_back) * scale
    sums_ref[1:2, :] = column_sum(linear_back) * scale
    sums_ref[2:3, :] = column_sum(cotan * normed) * scale


def backward_kernel(
    pick_ref, turned_ref, ecotan_ref, normed_ref, invstd_ref, slope_ref, pulled_ref, eouter_ref,
    egain_ref, node_sums_ref,
    fresh_ref, preact_ref, spread_ref, sums_ref, linear_ref, *, scale,
):
    edge_count = ecotan_ref.shape[0]
    count = pulled_ref.shape[0]
    tile = edge_count // 1
    tiles = [slice(start, start + tile) for start in range(0, edge_count, tile)]
    sums = [0.0, 0.0, 0.0]

    def first(rows):
        return ecotan_ref[rows, :].astype(F32) + mm(
            pick_ref[rows, count : 2 * count], pulled_ref[...]
        )

    def second(rows, fresh_back):
        fresh_ref[rows, :] = fresh_back
        normed = normed_ref[rows, :]
        linear_back = norm_back(fresh_back, normed, invstd_ref[rows, :], egain_ref[...])
        linear_half = linear_back.astype(BF)
        linear_ref[rows, :] = linear_half
        sums[1] += column_sum(linear_back)
        sums[2] += column_sum(fresh_back * normed)
        return mm_nt(linear_half, eouter_ref[...])

    def third(rows, back):
        preact_back = back * slope_ref[rows, :]
        preact_ref[rows, :] = preact_back.astype(BF)
        sums[0] += column_sum(preact_back)

    fresh_backs = [first(rows) for rows in tiles]
    backs = [second(rows, fresh_back) for rows, fresh_back in zip(tiles, fresh_backs)]
    for rows, back in zip(tiles, backs):
        third(rows, back)
    for k in range(3):
        sums_ref[k : k + 1, :] = sums[k] * scale
    sums_ref[3:, :] = node_sums_ref[...]
    used = spread_ref.shape[0]
    spread_ref[...] = mm(turned_ref[:used, :], preact_ref[...]).astype(BF)


def weights_kernel(
    edges_turned_ref, nodes_ref, low_ref, high_ref, hidden_ref, preact_ref, linear_ref, spread_ref,
    aggregate_ref, node_hidden_ref, node_preact_ref, node_linear_ref,
    weights_ref, *sends, columns, scales, plan,
):
    count = nodes_ref.shape[0]
    nodes = nodes_ref[...]
    rim = jnp.concatenate([low_ref[...], high_ref[...]], axis=0)
    node_preact = node_preact_ref[:, columns]
    chunk = columns.stop - columns.start
    by_nodes = mm_tn(
        nodes,
        jnp.concatenate(
            [spread_ref[:count, columns], spread_ref[count : 2 * count, columns], node_preact], axis=1
        ),
    )
    start = 0
    for scale, term in (
        (scales[0], mm(edges_turned_ref[...], preact_ref[:, columns])),
        (scales[0], by_nodes[:, :chunk] + mm_tn(rim, spread_ref[2 * count :, columns])),
        (scales[0], by_nodes[:, chunk : 2 * chunk]),
        (scales[0], mm_tn(hidden_ref[...], linear_ref[:, columns])),
        (scales[1], by_nodes[:, 2 * chunk :]),
        (scales[1], mm_tn(aggregate_ref[...], node_preact)),
        (scales[1], mm_tn(node_hidden_ref[...], node_linear_ref[:, columns])),
    ):
        value = term * scale
        weights_ref[start : start + value.shape[0], :] = value
        start += value.shape[0]
    for send_ref in sends:
        other = 1 - plan.core()
        for position in range(plan.count // 2):
            row = position * plan.block
            send_ref[row : row + plan.block, :] = weights_ref[
                pl.ds(plan.source(position, other), plan.block), :
            ].astype(BF)


def rim_kernel(spread_ref, inner_ref, out_ref, *, count):
    width, slots = spread_ref.shape[1], out_ref.shape[0]
    rows = mm_nt(spread_ref[2 * count :, :], inner_ref[width : 2 * width, :]).astype(BF)
    out_ref[: slots // 2, :] = rows[slots // 2 :]
    out_ref[slots // 2 :, :] = rows[: slots // 2]


def grads_kernel(spread_ref, inner_ref, partial_ref, fresh_ref, preact_ref, nodes_ref, edges_ref):
    count, width = partial_ref.shape
    nodes_ref[...] = (
        partial_ref[...]
        + mm_nt(spread_ref[:count, :], inner_ref[width : 2 * width, :])
        + mm_nt(spread_ref[count : 2 * count, :], inner_ref[2 * width :, :])
    )
    edge_count = preact_ref.shape[0]
    tile = edge_count // 2
    for start in range(0, edge_count, tile):
        rows = slice(start, start + tile)
        edges_ref[rows, :] = (
            fresh_ref[rows, :] + mm_nt(preact_ref[rows, :], inner_ref[:width, :])
        ).astype(BF)


def rims_kernel(lists_ref, partial_ref, back_ref, out_ref):
    count, half = partial_ref.shape[0], lists_ref.shape[1]
    rows = lax.broadcasted_iota(jnp.int32, (count, half), 0)
    total = partial_ref[...]
    for k in range(2):
        pick = jnp.where(rows == lists_ref[k : k + 1, :], 1.0, 0.0).astype(BF)
        total += mm(pick, back_ref[k * half : (k + 1) * half, :])
    out_ref[...] = total


def ring(values, step):
    count = lax.axis_size("patch")
    return lax.ppermute(values, "patch", [(i, (i + step) % count) for i in range(count)])


def halving_orders():
    core_bit = lax.axis_size("patch")
    high = [core_bit << k for k in range(1, lax.axis_size("region").bit_length() - 1)]
    low = [1 << k for k in range(core_bit.bit_length() - 1)]
    return core_bit, high + low, low + high


def permute_by(values, first, second, core_bit):
    count = lax.axis_size("region") * lax.axis_size("patch")
    pairs = [(i, i ^ (second if i & core_bit else first)) for i in range(count)]
    return lax.ppermute(values, AXES, pairs)


def reduce_all(flat, vectors):
    core_bit, first, second = halving_orders()
    count = lax.axis_size("region") * lax.axis_size("patch")
    me = lax.axis_index(AXES)
    core = (me & core_bit) // core_bit
    depth = count.bit_length() - 1
    flat = flat.reshape((2,) * depth + (-1, flat.shape[1]))

    def ordered(order):
        axes = [depth - bit.bit_length() for bit in [core_bit] + order]
        return jnp.transpose(flat, axes + [depth, depth + 1])

    blocks = jnp.stack([ordered(first)[0], ordered(second)[1]]).reshape(2, -1, flat.shape[-1])
    kept = lax.dynamic_index_in_dim(blocks, core, 0, keepdims=False)
    sent = lax.dynamic_index_in_dim(blocks, 1 - core, 0, keepdims=False).astype(BF)
    got = permute_by(sent, core_bit, core_bit, core_bit)
    total = kept + got
    for one, two in zip(first, second):
        bit = jnp.where(core == 1, (me & two) // two, (me & one) // one)
        halves = total.reshape(2, -1, flat.shape[-1])
        kept = lax.dynamic_index_in_dim(halves, bit, 0, keepdims=False)
        sent = lax.dynamic_index_in_dim(halves, 1 - bit, 0, keepdims=False).astype(BF)
        got = permute_by(sent, one, two, core_bit)
        vectors = vectors + permute_by(vectors, one, two, core_bit)
        total = kept + got
    vectors = vectors + permute_by(vectors, core_bit, core_bit, core_bit)
    return total.reshape(-1), vectors.reshape(-1)


Sides = collections.namedtuple("Sides", ("weights", "early", "late", "last"))


class Halving:
    def __init__(self, rows, columns, orders, carries):
        self.core_bit, (self.first, self.second) = lax.axis_size("patch"), orders
        self.count = lax.axis_size("region") * lax.axis_size("patch")
        self.block = rows // self.count
        self.rows = rows // 2
        self.columns = columns
        self.width = columns.stop - columns.start
        self.steps = len(self.first)
        self.carries = carries

    def place(self, order, core, position):
        block = self.core_bit if core else 0
        for k, bit in enumerate(order):
            if (position >> (self.steps - 1 - k)) & 1:
                block |= bit
        return block * self.block

    def me(self):
        return lax.axis_index("region") * self.core_bit + lax.axis_index("patch")

    def core(self):
        return lax.rem(self.me() // self.core_bit, 2)

    def bit(self, step):
        me = self.me()
        one, two = self.first[step], self.second[step]
        return jnp.where(self.core() == 1, lax.rem(me // two, 2), lax.rem(me // one, 2))

    def source(self, position, core):
        zero, one = self.place(self.first, 0, position), self.place(self.second, 1, position)
        return pl.multiple_of(jnp.where(core == 1, one, zero), 8)

    def pieces(self, full):
        return full // self.width

    def extra(self, full):
        return 16 * self.pieces(full) if self.carries else 0

    def slots(self, step, rows):
        if not self.carries:
            return 0
        bits = (self.first[step], self.second[step])
        return rows if 1 in bits else rows // 2 if min(bits) < self.core_bit else 0

    def taken(self, step):
        place = lax.rem(self.me(), self.core_bit)
        even = lax.rem(place, 2) == 0
        answers = []
        for bit in (self.first[step], self.second[step]):
            if bit == 1 or bit > self.core_bit:
                answers.append((bit == 1, bit == 1))
                continue
            between = lax.rem(place, bit) // 2
            up = jnp.logical_and(even, between == 0)
            down = jnp.logical_and(jnp.logical_not(even), between == bit // 2 - 1)
            answers.append((up, down))
        core = self.core() == 1
        return tuple(jnp.where(core, b, a) for a, b in zip(*answers))


def halve(src_ref, got_ref, out_ref, plan, step, side):
    half = plan.rows >> (step + 1)
    bit = plan.bit(step)
    chosen = 1 - bit if side else bit
    if step:
        start = pl.multiple_of(chosen * half, 16)
        held = src_ref[pl.ds(start, half), :]
        out_ref[:half, :] = (held + got_ref[pl.ds(start, half), :]).astype(out_ref.dtype)
        return
    core = plan.core()
    per_half = half // plan.block
    for k in range(per_half):
        low, high = plan.source(k, core), plan.source(k + per_half, core)
        row = pl.multiple_of(jnp.where(chosen == 1, high, low), 8)
        held = src_ref[pl.ds(row, plan.block), :]
        start = pl.multiple_of(chosen * half + k * plan.block, 16)
        got = got_ref[pl.ds(start, plan.block), :]
        out_ref[k * plan.block : (k + 1) * plan.block, :] = (held + got).astype(out_ref.dtype)


def keep_kernel(src_ref, got_ref, out_ref, *, plan, step):
    halve(src_ref, got_ref, out_ref, plan, step, 0)


def unpack(got_ref, start, rows, plan, full):
    parts = [
        got_ref[start + k * rows : start + (k + 1) * rows, :] for k in range(plan.pieces(full))
    ]
    return jnp.concatenate(parts, axis=1).astype(F32)


def pack(out_ref, start, values, plan):
    rows = values.shape[0]
    for k in range(plan.pieces(values.shape[1])):
        out_ref[start + k * rows : start + (k + 1) * rows, :] = values[
            :, k * plan.width : (k + 1) * plan.width
        ].astype(BF)


def add_vectors(vec_ref, got_ref, start, plan):
    count, full = vec_ref.shape
    both = unpack(got_ref, start, 16, plan, full)
    return vec_ref[...] + (both[:count] + both[8 : 8 + count])


def move_halo(state_ref, got_ref, start, plan, step):
    rows, full = state_ref.shape
    half = rows // 2
    slots = plan.slots(step, rows)
    state = state_ref[...].astype(F32)
    if not slots:
        return state
    came = unpack(got_ref, start, slots, plan, full)
    up, down = plan.taken(step)
    return jnp.concatenate(
        [
            jnp.where(up, came[:half], state[:half]),
            jnp.where(down, came[slots - half :], state[half:]),
        ],
        axis=0,
    )


def send_kernel(src_ref, got_ref, *refs, plan, step):
    if not plan.carries:
        halve(src_ref, got_ref, refs[0], plan, step, 1)
        return
    vec_ref, state_ref, out_ref, new_ref, moved_ref = refs
    halve(src_ref, got_ref, out_ref, plan, step, 1)
    half = plan.rows >> (step + 1)
    count, full = vec_ref.shape
    vec, state = vec_ref[...], state_ref[...].astype(F32)
    if step:
        vec = add_vectors(vec_ref, got_ref, 2 * half, plan)
        state = move_halo(state_ref, got_ref, 2 * half + plan.extra(full), plan, step - 1)
    upper = vec.astype(BF).astype(F32)
    lower = (vec - upper).astype(BF).astype(F32)
    gap = jnp.zeros((8 - count, full), F32)
    pack(out_ref, half, jnp.concatenate([upper, gap, lower, gap], axis=0), plan)
    new_ref[...] = upper + lower
    moved_ref[...] = state.astype(BF)
    rows = state.shape[0]
    slots = plan.slots(step, rows)
    if slots == rows:
        pack(out_ref, half + plan.extra(full), state, plan)
    elif slots:
        even = lax.rem(plan.me(), 2) == 0
        pack(
            out_ref, half + plan.extra(full),
            jnp.where(even, state[: rows // 2], state[rows // 2 :]), plan,
        )


def carried_kernel(vec_ref, state_ref, got_ref, new_ref, moved_ref, *, plan):
    new_ref[...] = add_vectors(vec_ref, got_ref, plan.block, plan)
    start = plan.block + plan.extra(vec_ref.shape[1])
    moved_ref[...] = move_halo(state_ref, got_ref, start, plan, plan.steps - 1).astype(BF)


def close_kernel(vec_ref, other_ref, *refs, plans):
    *refs, out_ref, vectors_ref = refs
    pieces = out_ref.shape[0] // plans[0].block
    for plan, held_ref, got_ref in zip(plans, refs[0::2], refs[1::2]):
        total = held_ref[...] + got_ref[: plan.block, :]
        for k in range(0, plan.width, LANES):
            piece = (plan.columns.start + k) // LANES
            out_ref[pl.ds(piece, plan.block, stride=pieces), :] = total[:, k : k + LANES]
    vec = vec_ref[...] + other_ref[...]
    for k in range(pieces):
        vectors_ref[pl.ds(k, vec.shape[0], stride=pieces), :] = vec[:, k * LANES : (k + 1) * LANES]


def after(marks, *values):
    return lax.optimization_barrier((*values, *marks))[: len(values)]


def reduce_kernels(plans, sides, vec, width):
    full = vec.shape[1]
    held, got = {}, {}
    marks, state = (), None
    for plan in plans:
        held[plan], sent = sides.weights(plan, marks)
        marks = (sent,)
        got[plan] = permute_by(sent, plan.core_bit, plan.core_bit, plan.core_bit)
        if state is None:
            state = sides.early(marks)
            marks = (state,)
    shapes = [(vec.shape, F32), (state.shape, BF)]
    for step in range(plans[0].steps):
        if step == 1:
            (nodes,) = marks = sides.late(marks)
        for plan in plans:
            half = plan.rows >> (step + 1)
            source, came = after(marks, held[plan], got[plan])
            rows = half + plan.extra(full) + plan.slots(step, state.shape[0]) * plan.pieces(full)
            carried = [near(vec), near(state)] if plan.carries else []
            sent, *new = call(
                functools.partial(send_kernel, plan=plan, step=step),
                [((rows, plan.width), BF)] + (shapes if plan.carries else []),
                near(source), near(came), *carried, name=f"send{step}",
            )
            if plan.carries:
                vec, state = new
            marks = (sent,)
            source, came = after(marks, source, came)
            incoming = permute_by(sent, plan.first[step], plan.second[step], plan.core_bit)
            (held[plan],) = call(
                functools.partial(keep_kernel, plan=plan, step=step),
                [((half, plan.width), F32)], near(source), near(came), name=f"keep{step}",
            )
            got[plan] = incoming
    (carrier,) = [plan for plan in plans if plan.carries]
    vec, state = call(
        functools.partial(carried_kernel, plan=carrier), shapes, near(vec), near(state),
        near(got[carrier]), name="carried",
    )
    other = permute_by(vec, carrier.core_bit, carrier.core_bit, carrier.core_bit)
    pairs = [near(a) for plan in plans for a in (held[plan], got[plan])]
    (nodes,) = call(
        rims_kernel, [(nodes.shape, F32)], sides.last, near(nodes), near(state), name="rims",
        plain=(0,), limit=4 << 20,
    )
    out, vectors = call(
        functools.partial(close_kernel, plans=plans),
        [
            ((plans[0].block * width // LANES, LANES), F32),
            ((vec.size // LANES, LANES), F32),
        ],
        near(vec), near(other), *pairs, name="close", plain=(0, 1),
    )
    return out.reshape(-1), vectors.reshape(-1), nodes


def make_plans(rows, width, slots):
    count = lax.axis_size("region") * lax.axis_size("patch")
    core_bit, first, second = halving_orders()
    if rows % (16 * count) or width % (4 * LANES) or slots % 32:
        return []
    high = [b for b in sorted(first) if b > core_bit]
    low = [b for b in sorted(first) if b < core_bit]
    turned = low[1:-1] + high + low[:1] + low[-1:]
    quarter = width // 4
    chunks = CHUNKS
    return [
        Halving(
            rows, slice(a * quarter, b * quarter),
            (turned, turned) if kind else (first, second), i == 0,
        )
        for i, (a, b, kind) in enumerate(chunks)
    ]


PICK = 20 << 30
CHUNKS = ((0, 2, 0), (2, 4, 0))


def per_device(
    nodes, edges, node_cotan, edge_cotan, edge_inner, edge_outer, node_inner, node_outer, edge_shift,
    edge_offset, edge_gain, node_shift, node_offset, node_gain, send_rows, senders, receivers,
):
    count, width = nodes.shape
    edge_count = edges.shape[0]
    hidden_width = edge_outer.shape[0]
    lists = send_rows.reshape(send_rows.shape[2:])
    half = lists.shape[1]
    slots = 2 * half
    devices_all = lax.axis_size("region") * lax.axis_size("patch")
    edge_norm = 1.0 / math.sqrt(edge_count * devices_all)
    node_norm = 1.0 / math.sqrt(count * devices_all)
    picked = 2 * count + -(-slots // LANES) * LANES
    edge_rows = 3 * width + hidden_width
    weight_rows = edge_rows + 2 * width + hidden_width
    plans = make_plans(weight_rows, hidden_width, slots)
    edge_shift, edge_offset, edge_gain, node_shift, node_offset, node_gain = (
        v.reshape(1, -1)
        for v in (edge_shift, edge_offset, edge_gain, node_shift, node_offset, node_gain)
    )

    out_low, out_high = call(
        pick_kernel, [((half, width), BF)] * 2, lists, nodes, name="pick", limit=4 << 20, hbm=(0, 1), flops=PICK,
        scratch=[
            pltpu.VMEM(lists.shape, jnp.int32), pltpu.VMEM(nodes.shape, BF),
            pltpu.SemaphoreType.DMA((2,)),
        ],
    )
    low = ring(out_high, 1)
    high = ring(out_low, -1)

    part, npart, pick, turned, edges_turned = call(
        table_kernel,
        [
            ((edge_count, hidden_width), F32),
            ((count, hidden_width), F32),
            ((edge_count, picked), BF),
            ((picked, edge_count), BF),
            ((width, edge_count), BF),
        ],
        senders.reshape(1, -1), receivers.reshape(1, -1), edge_shift, nodes, edge_inner, edges,
        node_inner, node_shift,
        name="table", flops=4 * edge_count * width * hidden_width,
        scratch=[pltpu.VMEM((2 * count, hidden_width), BF)],
    )
    hidden, slope, normed, invstd, pulled, partial, node_sums, *node_terms = call(
        functools.partial(forward_kernel, scale=node_norm),
        [
            ((edge_count, hidden_width), BF),
            ((edge_count, hidden_width), F32),
            ((edge_count, width), F32),
            ((edge_count, 1), F32),
            ((count, width), BF),
            ((count, width), F32),
            ((3, width), F32),
            ((count, width), BF),
            ((count, hidden_width), BF),
            ((count, hidden_width), BF),
            ((count, width), BF),
        ],
        near(part), near(npart), near(pick), near(turned), near(low), near(high), edges,
        edge_inner, edge_outer, edge_offset, edge_gain, node_offset, node_gain,
        node_inner, node_outer, node_cotan, name="forward", flops=5 << 30,
    )
    fresh, preact, spread, sums, linear = call(
        functools.partial(backward_kernel, scale=edge_norm),
        [
            ((edge_count, width), F32),
            ((edge_count, hidden_width), BF),
            ((2 * count + slots, hidden_width), BF),
            ((6, width), F32),
            ((edge_count, width), BF),
        ],
        near(pick), near(turned), edge_cotan, near(normed), near(invstd), near(slope), near(pulled),
        edge_outer, edge_gain, near(node_sums),
        name="backward", flops=3 << 30,
    )

    def weights_of(plan, marks):
        preact_late, linear_late = after(marks, preact, linear)
        columns = plan.columns if plan else slice(0, hidden_width)
        chunk = columns.stop - columns.start
        sends = [((plan.rows, chunk), BF)] if plan else []
        return call(
            functools.partial(
                weights_kernel, columns=columns, scales=(edge_norm, node_norm), plan=plan
            ),
            [((weight_rows, chunk), F32)] + sends,
            near(edges_turned), nodes, near(low), near(high), near(hidden), near(preact_late), near(linear_late),
            near(spread), *[near(a) for a in node_terms],
            name="weights", flops=chunk << 22,
        )

    results = {}

    def rim_side(marks):
        (spread_late,) = after(marks, spread)
        (rims,) = call(
            functools.partial(rim_kernel, count=count), [((slots, width), BF)],
            near(spread_late), edge_inner, name="rim", limit=4 << 20,
        )
        return rims

    def grads_side(marks):
        spread_late, fresh_late = after(marks, spread, fresh)
        results["nodes"], results["edges"] = call(
            grads_kernel,
            [((count, width), F32), ((edge_count, width), BF)],
            near(spread_late), edge_inner, near(partial), near(fresh_late), near(preact),
            name="grads", flops=2 << 30, plain=(1,),
        )
        return (results["nodes"],)

    if plans:
        grad_weights, grad_vectors, grad_nodes = reduce_kernels(
            plans, Sides(weights_of, rim_side, grads_side, lists), sums, hidden_width
        )
    else:
        grad_weights, grad_vectors = reduce_all(weights_of(None, ())[0], sums)
        rims = rim_side((sums,))
        back = jnp.concatenate([ring(rims[:half], 1), ring(rims[half:], -1)])
        grads_side((sums,))
        (grad_nodes,) = call(
            rims_kernel, [((count, width), F32)], lists, near(results["nodes"]), near(back),
            name="rims", plain=(0,), limit=4 << 20,
        )
    return (grad_nodes, results["edges"], grad_weights, grad_vectors)


def solution(mesh):
    in_specs = (
        P(AXES, None), P(AXES, None), P(AXES, None), P(AXES, None),
        P(), P(), P(), P(), P(), P(), P(), P(), P(), P(),
        P("region", "patch", None, None), P(AXES), P(AXES),
    )
    out_specs = (P(AXES, None), P(AXES, None), P(AXES), P())
    return jax.shard_map(
        per_device, mesh=mesh, in_specs=in_specs, out_specs=out_specs, check_vma=False
    )
```

```python
import collections
import functools
import math

import jax
import jax.numpy as jnp
from jax import lax
from jax.experimental import pallas as pl
from jax.experimental.pallas import tpu as pltpu
from jax.sharding import PartitionSpec as P

BF = jnp.bfloat16
F32 = jnp.float32
LANES = 128
VMEM = pltpu.VMEM
AXES = ("region", "patch")


def pinned(shape, dtype):
    return pltpu.VMEM(shape, dtype)


def mm(a, b):
    return jnp.dot(a, b, preferred_element_type=F32)


def mm_nt(a, b):
    return lax.dot_general(a, b, (((1,), (1,)), ((), ())), preferred_element_type=F32)


def mm_tn(a, b):
    return lax.dot_general(a, b, (((0,), (0,)), ((), ())), preferred_element_type=F32)


def call(body, outs, *args, flops=0, limit=24 << 20, name=None, plain=(), hbm=(), scratch=()):
    vmem = pl.BlockSpec(memory_space=pltpu.VMEM)
    anywhere = pl.BlockSpec(memory_space=pltpu.HBM)
    shapes = [
        jax.ShapeDtypeStruct(s, d) if i in plain else pinned(s, d) for i, (s, d) in enumerate(outs)
    ]
    moved = sum(math.prod(s) * jnp.dtype(d).itemsize for s, d in outs)
    return pl.pallas_call(
        body,
        out_shape=shapes,
        in_specs=[anywhere if i in hbm else vmem for i in range(len(args))],
        out_specs=[vmem] * len(outs),
        scratch_shapes=list(scratch),
        compiler_params=pltpu.CompilerParams(vmem_limit_bytes=limit),
        cost_estimate=pl.CostEstimate(flops=flops, bytes_accessed=moved, transcendentals=0),
        name=name,
    )(*[far(a) if i in hbm else a for i, a in enumerate(args)])


def far(array):
    return pltpu.with_memory_space_constraint(array, pltpu.HBM)


def near(array):
    return pltpu.with_memory_space_constraint(array, pltpu.VMEM)


def start_copies(pairs, sems):
    copies = [pltpu.make_async_copy(a, b, sems.at[i]) for i, (a, b) in enumerate(pairs)]
    for copy in copies:
        copy.start()
    return copies


def layer_norm(values):
    centred = values - jnp.mean(values, axis=-1, keepdims=True)
    invstd = lax.rsqrt(jnp.mean(centred * centred, axis=-1, keepdims=True) + 1e-05)
    return centred * invstd, invstd


def norm_back(upstream, normed, invstd, gains):
    scaled = upstream * gains
    return invstd * (
        scaled
        - jnp.mean(scaled, axis=-1, keepdims=True)
        - normed * jnp.mean(scaled * normed, axis=-1, keepdims=True)
    )


def silu_and_slope(preact):
    gate = 1.0 / (1.0 + jnp.exp(-preact))
    hidden = preact * gate
    return hidden, gate + hidden * (1.0 - gate)


def column_sum(values):
    return jnp.sum(values, axis=0, keepdims=True)


def pick_kernel(lists_hbm, nodes_hbm, low_ref, high_ref, lists_ref, nodes_ref, sems):
    for copy in start_copies([(lists_hbm, lists_ref), (nodes_hbm, nodes_ref)], sems):
        copy.wait()
    slots, count = lists_ref.shape[1], nodes_ref.shape[0]
    rows = lax.broadcasted_iota(jnp.int32, (count, slots), 0)
    for k, out_ref in enumerate((low_ref, high_ref)):
        pick = jnp.where(rows == lists_ref[k : k + 1, :], 1.0, 0.0).astype(BF)
        out_ref[...] = mm_tn(pick, nodes_ref[...]).astype(BF)


def table_kernel(
    senders_ref, receivers_ref, shift_ref, nodes_ref, inner_ref, edges_ref, ninner_ref, nshift_ref,
    part_ref, npart_ref, pick_ref, turned_ref, edges_turned_ref, own_ref,
):
    edge_count, width = edges_ref.shape
    count = nodes_ref.shape[0]
    senders = senders_ref[...]
    receivers = receivers_ref[...] + count
    senders = jnp.where(senders < count, senders, senders + count)
    wide_send = jnp.transpose(jnp.broadcast_to(senders, (LANES, edge_count)))
    wide_recv = jnp.transpose(jnp.broadcast_to(receivers, (LANES, edge_count)))
    lane = lax.broadcasted_iota(jnp.int32, (edge_count, LANES), 1)
    row = lax.broadcasted_iota(jnp.int32, (LANES, edge_count), 0)
    for start in range(0, pick_ref.shape[1], LANES):
        own_part = count <= start < 2 * count
        tall = wide_recv if own_part else wide_send
        flat = receivers if own_part else senders
        pick_ref[:, start : start + LANES] = jnp.where(tall == lane + start, 1.0, 0.0).astype(BF)
        turned_ref[start : start + LANES, :] = jnp.where(flat == row + start, 1.0, 0.0).astype(BF)
    nodes = nodes_ref[...]
    own_ref[:count, :] = mm(nodes, inner_ref[width : 2 * width, :]).astype(BF)
    own_ref[count:, :] = mm(nodes, inner_ref[2 * width :, :]).astype(BF)
    tile = edge_count // 2
    for start in range(0, edge_count, tile):
        rows = slice(start, start + tile)
        part_ref[rows, :] = (
            mm(edges_ref[rows, :], inner_ref[:width, :])
            + mm(pick_ref[rows, : 2 * count], own_ref[...])
            + shift_ref[...]
        )
    npart_ref[...] = mm(nodes, ninner_ref[:width, :]) + nshift_ref[...]
    edges_turned_ref[...] = edges_ref[...].T


def forward_kernel(
    part_ref, npart_ref, pick_ref, turned_ref, low_ref, high_ref, edges_ref,
    einner_ref, eouter_ref, eoffset_ref, egain_ref, noffset_ref, ngain_ref,
    ninner_ref, nouter_ref, cotan_ref,
    hidden_ref, slope_ref, normed_ref, invstd_ref, pulled_ref, partial_ref, sums_ref,
    aggregate_ref, node_hidden_ref, node_preact_ref, node_linear_ref,
    *, scale,
):
    edge_count, width = edges_ref.shape
    count = cotan_ref.shape[0]
    rim = jnp.concatenate([low_ref[...], high_ref[...]], axis=0)
    far = mm(rim, einner_ref[width : 2 * width, :]).astype(BF)
    slots = rim.shape[0]
    tile = edge_count // 1
    tiles = [slice(start, start + tile) for start in range(0, edge_count, tile)]

    def first(rows):
        return part_ref[rows, :] + mm(pick_ref[rows, 2 * count : 2 * count + slots], far)

    def second(rows, preact):
        hidden, slope = silu_and_slope(preact)
        hidden = hidden.astype(BF)
        hidden_ref[rows, :] = hidden
        slope_ref[rows, :] = slope
        return mm(hidden, eouter_ref[...]) + eoffset_ref[...]

    def third(rows, linear):
        normed, invstd = layer_norm(linear)
        normed_ref[rows, :] = normed
        invstd_ref[rows, :] = invstd
        fresh = (edges_ref[rows, :].astype(F32) + egain_ref[...] * normed).astype(BF)
        return mm(turned_ref[count : 2 * count, rows], fresh)

    preacts = [first(rows) for rows in tiles]
    linears = [second(rows, preact) for rows, preact in zip(tiles, preacts)]
    total = sum(third(rows, linear) for rows, linear in zip(tiles, linears))
    aggregate = total.astype(BF)
    preact = npart_ref[...] + mm(aggregate, ninner_ref[width:, :])
    hidden, slope = silu_and_slope(preact)
    hidden = hidden.astype(BF)
    normed, invstd = layer_norm(mm(hidden, nouter_ref[...]) + noffset_ref[...])
    cotan = cotan_ref[...].astype(F32)
    linear_back = norm_back(cotan, normed, invstd, ngain_ref[...])
    linear_half = linear_back.astype(BF)
    preact_back = mm_nt(linear_half, nouter_ref[...]) * slope
    preact_half = preact_back.astype(BF)
    pulled_ref[...] = mm_nt(preact_half, ninner_ref[width:, :]).astype(BF)
    partial_ref[...] = cotan + mm_nt(preact_half, ninner_ref[:width, :])
    aggregate_ref[...] = aggregate
    node_hidden_ref[...] = hidden
    node_preact_ref[...] = preact_half
    node_linear_ref[...] = linear_half
    sums_ref[0:1, :] = column_sum(preact_back) * scale
    sums_ref[1:2, :] = column_sum(linear_back) * scale
    sums_ref[2:3, :] = column_sum(cotan * normed) * scale


def backward_kernel(
    pick_ref, turned_ref, ecotan_ref, normed_ref, invstd_ref, slope_ref, pulled_ref, eouter_ref,
    egain_ref, node_sums_ref, einner_ref,
    fresh_ref, preact_ref, spread_ref, sums_ref, linear_ref, rim_ref, *, scale,
):
    edge_count = ecotan_ref.shape[0]
    count = pulled_ref.shape[0]
    tile = edge_count // 1
    tiles = [slice(start, start + tile) for start in range(0, edge_count, tile)]
    sums = [0.0, 0.0, 0.0]

    def first(rows):
        return ecotan_ref[rows, :].astype(F32) + mm(
            pick_ref[rows, count : 2 * count], pulled_ref[...]
        )

    def second(rows, fresh_back):
        fresh_ref[rows, :] = fresh_back
        normed = normed_ref[rows, :]
        linear_back = norm_back(fresh_back, normed, invstd_ref[rows, :], egain_ref[...])
        linear_half = linear_back.astype(BF)
        linear_ref[rows, :] = linear_half
        sums[1] += column_sum(linear_back)
        sums[2] += column_sum(fresh_back * normed)
        return mm_nt(linear_half, eouter_ref[...])

    def third(rows, back):
        preact_back = back * slope_ref[rows, :]
        preact_ref[rows, :] = preact_back.astype(BF)
        sums[0] += column_sum(preact_back)

    fresh_backs = [first(rows) for rows in tiles]
    backs = [second(rows, fresh_back) for rows, fresh_back in zip(tiles, fresh_backs)]
    for rows, back in zip(tiles, backs):
        third(rows, back)
    for k in range(3):
        sums_ref[k : k + 1, :] = sums[k] * scale
    sums_ref[3:, :] = node_sums_ref[...]
    used = spread_ref.shape[0]
    spread_ref[...] = mm(turned_ref[:used, :], preact_ref[...]).astype(BF)
    rim_kernel(spread_ref, einner_ref, rim_ref, count=count)


def weights_kernel(
    edges_turned_ref, nodes_ref, low_ref, high_ref, hidden_ref, preact_ref, linear_ref, spread_ref,
    aggregate_ref, node_hidden_ref, node_preact_ref, node_linear_ref,
    weights_ref, *sends, columns, scales, plan,
):
    count = nodes_ref.shape[0]
    nodes = nodes_ref[...]
    rim = jnp.concatenate([low_ref[...], high_ref[...]], axis=0)
    node_preact = node_preact_ref[:, columns]
    chunk = columns.stop - columns.start
    by_nodes = mm_tn(
        nodes,
        jnp.concatenate(
            [spread_ref[:count, columns], spread_ref[count : 2 * count, columns], node_preact], axis=1
        ),
    )
    start = 0
    for scale, term in (
        (scales[0], mm(edges_turned_ref[...], preact_ref[:, columns])),
        (scales[0], by_nodes[:, :chunk] + mm_tn(rim, spread_ref[2 * count :, columns])),
        (scales[0], by_nodes[:, chunk : 2 * chunk]),
        (scales[0], mm_tn(hidden_ref[...], linear_ref[:, columns])),
        (scales[1], by_nodes[:, 2 * chunk :]),
        (scales[1], mm_tn(aggregate_ref[...], node_preact)),
        (scales[1], mm_tn(node_hidden_ref[...], node_linear_ref[:, columns])),
    ):
        value = term * scale
        weights_ref[start : start + value.shape[0], :] = value
        start += value.shape[0]
    for send_ref in sends:
        other = 1 - plan.core()
        for position in range(plan.count // 2):
            row = position * plan.block
            send_ref[row : row + plan.block, :] = weights_ref[
                pl.ds(plan.source(position, other), plan.block), :
            ].astype(BF)


def rim_kernel(spread_ref, inner_ref, out_ref, *, count):
    width, slots = spread_ref.shape[1], out_ref.shape[0]
    rows = mm_nt(spread_ref[2 * count :, :], inner_ref[width : 2 * width, :]).astype(BF)
    out_ref[: slots // 2, :] = rows[slots // 2 :]
    out_ref[slots // 2 :, :] = rows[: slots // 2]


def grads_kernel(spread_ref, inner_ref, partial_ref, fresh_ref, preact_ref, nodes_ref, edges_ref):
    count, width = partial_ref.shape
    nodes_ref[...] = (
        partial_ref[...]
        + mm_nt(spread_ref[:count, :], inner_ref[width : 2 * width, :])
        + mm_nt(spread_ref[count : 2 * count, :], inner_ref[2 * width :, :])
    )
    edge_count = preact_ref.shape[0]
    tile = edge_count // 2
    for start in range(0, edge_count, tile):
        rows = slice(start, start + tile)
        edges_ref[rows, :] = (
            fresh_ref[rows, :] + mm_nt(preact_ref[rows, :], inner_ref[:width, :])
        ).astype(BF)


def rims_kernel(lists_ref, partial_ref, back_ref, out_ref):
    count, half = partial_ref.shape[0], lists_ref.shape[1]
    rows = lax.broadcasted_iota(jnp.int32, (count, half), 0)
    total = partial_ref[...]
    for k in range(2):
        pick = jnp.where(rows == lists_ref[k : k + 1, :], 1.0, 0.0).astype(BF)
        total += mm(pick, back_ref[k * half : (k + 1) * half, :])
    out_ref[...] = total


def ring(values, step):
    count = lax.axis_size("patch")
    return lax.ppermute(values, "patch", [(i, (i + step) % count) for i in range(count)])


def halving_orders():
    core_bit = lax.axis_size("patch")
    high = [core_bit << k for k in range(1, lax.axis_size("region").bit_length() - 1)]
    low = [1 << k for k in range(core_bit.bit_length() - 1)]
    return core_bit, high + low, low + high


def permute_by(values, first, second, core_bit):
    count = lax.axis_size("region") * lax.axis_size("patch")
    pairs = [(i, i ^ (second if i & core_bit else first)) for i in range(count)]
    return lax.ppermute(values, AXES, pairs)


def reduce_all(flat, vectors):
    core_bit, first, second = halving_orders()
    count = lax.axis_size("region") * lax.axis_size("patch")
    me = lax.axis_index(AXES)
    core = (me & core_bit) // core_bit
    depth = count.bit_length() - 1
    flat = flat.reshape((2,) * depth + (-1, flat.shape[1]))

    def ordered(order):
        axes = [depth - bit.bit_length() for bit in [core_bit] + order]
        return jnp.transpose(flat, axes + [depth, depth + 1])

    blocks = jnp.stack([ordered(first)[0], ordered(second)[1]]).reshape(2, -1, flat.shape[-1])
    kept = lax.dynamic_index_in_dim(blocks, core, 0, keepdims=False)
    sent = lax.dynamic_index_in_dim(blocks, 1 - core, 0, keepdims=False).astype(BF)
    got = permute_by(sent, core_bit, core_bit, core_bit)
    total = kept + got
    for one, two in zip(first, second):
        bit = jnp.where(core == 1, (me & two) // two, (me & one) // one)
        halves = total.reshape(2, -1, flat.shape[-1])
        kept = lax.dynamic_index_in_dim(halves, bit, 0, keepdims=False)
        sent = lax.dynamic_index_in_dim(halves, 1 - bit, 0, keepdims=False).astype(BF)
        got = permute_by(sent, one, two, core_bit)
        vectors = vectors + permute_by(vectors, one, two, core_bit)
        total = kept + got
    vectors = vectors + permute_by(vectors, core_bit, core_bit, core_bit)
    return total.reshape(-1), vectors.reshape(-1)


Sides = collections.namedtuple("Sides", ("weights", "early", "late", "last"))


class Halving:
    def __init__(self, rows, columns, orders, carries):
        self.core_bit, (self.first, self.second) = lax.axis_size("patch"), orders
        self.count = lax.axis_size("region") * lax.axis_size("patch")
        self.block = rows // self.count
        self.rows = rows // 2
        self.columns = columns
        self.width = columns.stop - columns.start
        self.steps = len(self.first)
        self.carries = carries

    def place(self, order, core, position):
        block = self.core_bit if core else 0
        for k, bit in enumerate(order):
            if (position >> (self.steps - 1 - k)) & 1:
                block |= bit
        return block * self.block

    def me(self):
        return lax.axis_index("region") * self.core_bit + lax.axis_index("patch")

    def core(self):
        return lax.rem(self.me() // self.core_bit, 2)

    def bit(self, step):
        me = self.me()
        one, two = self.first[step], self.second[step]
        return jnp.where(self.core() == 1, lax.rem(me // two, 2), lax.rem(me // one, 2))

    def source(self, position, core):
        zero, one = self.place(self.first, 0, position), self.place(self.second, 1, position)
        return pl.multiple_of(jnp.where(core == 1, one, zero), 8)

    def pieces(self, full):
        return full // self.width

    def extra(self, full):
        return 16 * self.pieces(full) if self.carries else 0

    def slots(self, step, rows):
        if not self.carries:
            return 0
        bits = (self.first[step], self.second[step])
        return rows if 1 in bits else rows // 2 if min(bits) < self.core_bit else 0

    def taken(self, step):
        place = lax.rem(self.me(), self.core_bit)
        even = lax.rem(place, 2) == 0
        answers = []
        for bit in (self.first[step], self.second[step]):
            if bit == 1 or bit > self.core_bit:
                answers.append((bit == 1, bit == 1))
                continue
            between = lax.rem(place, bit) // 2
            up = jnp.logical_and(even, between == 0)
            down = jnp.logical_and(jnp.logical_not(even), between == bit // 2 - 1)
            answers.append((up, down))
        core = self.core() == 1
        return tuple(jnp.where(core, b, a) for a, b in zip(*answers))


def halve(src_ref, got_ref, out_ref, plan, step, side):
    half = plan.rows >> (step + 1)
    bit = plan.bit(step)
    chosen = 1 - bit if side else bit
    if step:
        start = pl.multiple_of(chosen * half, 16)
        held = src_ref[pl.ds(start, half), :]
        out_ref[:half, :] = (held + got_ref[pl.ds(start, half), :]).astype(out_ref.dtype)
        return
    core = plan.core()
    per_half = half // plan.block
    for k in range(per_half):
        low, high = plan.source(k, core), plan.source(k + per_half, core)
        row = pl.multiple_of(jnp.where(chosen == 1, high, low), 8)
        held = src_ref[pl.ds(row, plan.block), :]
        start = pl.multiple_of(chosen * half + k * plan.block, 16)
        got = got_ref[pl.ds(start, plan.block), :]
        out_ref[k * plan.block : (k + 1) * plan.block, :] = (held + got).astype(out_ref.dtype)


def keep_kernel(src_ref, got_ref, out_ref, *, plan, step):
    halve(src_ref, got_ref, out_ref, plan, step, 0)


def unpack(got_ref, start, rows, plan, full):
    parts = [
        got_ref[start + k * rows : start + (k + 1) * rows, :] for k in range(plan.pieces(full))
    ]
    return jnp.concatenate(parts, axis=1).astype(F32)


def pack(out_ref, start, values, plan):
    rows = values.shape[0]
    for k in range(plan.pieces(values.shape[1])):
        out_ref[start + k * rows : start + (k + 1) * rows, :] = values[
            :, k * plan.width : (k + 1) * plan.width
        ].astype(BF)


def add_vectors(vec_ref, got_ref, start, plan):
    count, full = vec_ref.shape
    both = unpack(got_ref, start, 16, plan, full)
    return vec_ref[...] + (both[:count] + both[8 : 8 + count])


def move_halo(state_ref, got_ref, start, plan, step):
    rows, full = state_ref.shape
    half = rows // 2
    slots = plan.slots(step, rows)
    state = state_ref[...].astype(F32)
    if not slots:
        return state
    came = unpack(got_ref, start, slots, plan, full)
    up, down = plan.taken(step)
    return jnp.concatenate(
        [
            jnp.where(up, came[:half], state[:half]),
            jnp.where(down, came[slots - half :], state[half:]),
        ],
        axis=0,
    )


def send_kernel(src_ref, got_ref, *refs, plan, step):
    if not plan.carries:
        halve(src_ref, got_ref, refs[0], plan, step, 1)
        return
    vec_ref, state_ref, out_ref, new_ref, moved_ref = refs
    halve(src_ref, got_ref, out_ref, plan, step, 1)
    half = plan.rows >> (step + 1)
    count, full = vec_ref.shape
    vec, state = vec_ref[...], state_ref[...].astype(F32)
    if step:
        vec = add_vectors(vec_ref, got_ref, 2 * half, plan)
        state = move_halo(state_ref, got_ref, 2 * half + plan.extra(full), plan, step - 1)
    upper = vec.astype(BF).astype(F32)
    lower = (vec - upper).astype(BF).astype(F32)
    gap = jnp.zeros((8 - count, full), F32)
    pack(out_ref, half, jnp.concatenate([upper, gap, lower, gap], axis=0), plan)
    new_ref[...] = upper + lower
    moved_ref[...] = state.astype(BF)
    rows = state.shape[0]
    slots = plan.slots(step, rows)
    if slots == rows:
        pack(out_ref, half + plan.extra(full), state, plan)
    elif slots:
        even = lax.rem(plan.me(), 2) == 0
        pack(
            out_ref, half + plan.extra(full),
            jnp.where(even, state[: rows // 2], state[rows // 2 :]), plan,
        )


def carried_kernel(vec_ref, state_ref, got_ref, new_ref, moved_ref, *, plan):
    new_ref[...] = add_vectors(vec_ref, got_ref, plan.block, plan)
    start = plan.block + plan.extra(vec_ref.shape[1])
    moved_ref[...] = move_halo(state_ref, got_ref, start, plan, plan.steps - 1).astype(BF)


def close_kernel(vec_ref, other_ref, *refs, plans):
    *refs, out_ref, vectors_ref = refs
    pieces = out_ref.shape[0] // plans[0].block
    for plan, held_ref, got_ref in zip(plans, refs[0::2], refs[1::2]):
        total = held_ref[...] + got_ref[: plan.block, :]
        for k in range(0, plan.width, LANES):
            piece = (plan.columns.start + k) // LANES
            out_ref[pl.ds(piece, plan.block, stride=pieces), :] = total[:, k : k + LANES]
    vec = vec_ref[...] + other_ref[...]
    for k in range(pieces):
        vectors_ref[pl.ds(k, vec.shape[0], stride=pieces), :] = vec[:, k * LANES : (k + 1) * LANES]


def after(marks, *values):
    return lax.optimization_barrier((*values, *marks))[: len(values)]


def reduce_kernels(plans, sides, vec, width):
    full = vec.shape[1]
    held, got = {}, {}
    marks, state = (), None
    for plan in plans:
        held[plan], sent = sides.weights(plan, marks)
        marks = (sent,)
        got[plan] = permute_by(sent, plan.core_bit, plan.core_bit, plan.core_bit)
        if state is None:
            state = sides.early
    shapes = [(vec.shape, F32), (state.shape, BF)]
    for step in range(plans[0].steps):
        if step == 1:
            (nodes,) = marks = sides.late(marks)
        for plan in plans:
            half = plan.rows >> (step + 1)
            source, came = after(marks, held[plan], got[plan])
            rows = half + plan.extra(full) + plan.slots(step, state.shape[0]) * plan.pieces(full)
            carried = [near(vec), near(state)] if plan.carries else []
            sent, *new = call(
                functools.partial(send_kernel, plan=plan, step=step),
                [((rows, plan.width), BF)] + (shapes if plan.carries else []),
                near(source), near(came), *carried, name=f"send{step}",
            )
            if plan.carries:
                vec, state = new
            marks = (sent,)
            source, came = after(marks, source, came)
            incoming = permute_by(sent, plan.first[step], plan.second[step], plan.core_bit)
            (held[plan],) = call(
                functools.partial(keep_kernel, plan=plan, step=step),
                [((half, plan.width), F32)], near(source), near(came), name=f"keep{step}",
            )
            got[plan] = incoming
    (carrier,) = [plan for plan in plans if plan.carries]
    vec, state = call(
        functools.partial(carried_kernel, plan=carrier), shapes, near(vec), near(state),
        near(got[carrier]), name="carried",
    )
    other = permute_by(vec, carrier.core_bit, carrier.core_bit, carrier.core_bit)
    pairs = [near(a) for plan in plans for a in (held[plan], got[plan])]
    (nodes,) = call(
        rims_kernel, [(nodes.shape, F32)], sides.last, near(nodes), near(state), name="rims",
        plain=(0,), limit=4 << 20,
    )
    out, vectors = call(
        functools.partial(close_kernel, plans=plans),
        [
            ((plans[0].block * width // LANES, LANES), F32),
            ((vec.size // LANES, LANES), F32),
        ],
        near(vec), near(other), *pairs, name="close", plain=(0, 1),
    )
    return out.reshape(-1), vectors.reshape(-1), nodes


def make_plans(rows, width, slots):
    count = lax.axis_size("region") * lax.axis_size("patch")
    core_bit, first, second = halving_orders()
    if rows % (16 * count) or width % (4 * LANES) or slots % 32:
        return []
    high = [b for b in sorted(first) if b > core_bit]
    low = [b for b in sorted(first) if b < core_bit]
    turned = low[1:-1] + high + low[:1] + low[-1:]
    quarter = width // 4
    chunks = CHUNKS
    return [
        Halving(
            rows, slice(a * quarter, b * quarter),
            (turned, turned) if kind else (first, second), i == 0,
        )
        for i, (a, b, kind) in enumerate(chunks)
    ]


PICK = 20 << 30
CHUNKS = ((0, 2, 0), (2, 4, 0))


def per_device(
    nodes, edges, node_cotan, edge_cotan, edge_inner, edge_outer, node_inner, node_outer, edge_shift,
    edge_offset, edge_gain, node_shift, node_offset, node_gain, send_rows, senders, receivers,
):
    count, width = nodes.shape
    edge_count = edges.shape[0]
    hidden_width = edge_outer.shape[0]
    lists = send_rows.reshape(send_rows.shape[2:])
    half = lists.shape[1]
    slots = 2 * half
    devices_all = lax.axis_size("region") * lax.axis_size("patch")
    edge_norm = 1.0 / math.sqrt(edge_count * devices_all)
    node_norm = 1.0 / math.sqrt(count * devices_all)
    picked = 2 * count + -(-slots // LANES) * LANES
    edge_rows = 3 * width + hidden_width
    weight_rows = edge_rows + 2 * width + hidden_width
    plans = make_plans(weight_rows, hidden_width, slots)
    edge_shift, edge_offset, edge_gain, node_shift, node_offset, node_gain = (
        v.reshape(1, -1)
        for v in (edge_shift, edge_offset, edge_gain, node_shift, node_offset, node_gain)
    )

    out_low, out_high = call(
        pick_kernel, [((half, width), BF)] * 2, lists, nodes, name="pick", limit=4 << 20, hbm=(0, 1), flops=PICK,
        scratch=[
            pltpu.VMEM(lists.shape, jnp.int32), pltpu.VMEM(nodes.shape, BF),
            pltpu.SemaphoreType.DMA((2,)),
        ],
    )
    low = ring(out_high, 1)
    high = ring(out_low, -1)

    part, npart, pick, turned, edges_turned = call(
        table_kernel,
        [
            ((edge_count, hidden_width), F32),
            ((count, hidden_width), F32),
            ((edge_count, picked), BF),
            ((picked, edge_count), BF),
            ((width, edge_count), BF),
        ],
        senders.reshape(1, -1), receivers.reshape(1, -1), edge_shift, nodes, edge_inner, edges,
        node_inner, node_shift,
        name="table", flops=4 * edge_count * width * hidden_width,
        scratch=[pltpu.VMEM((2 * count, hidden_width), BF)],
    )
    hidden, slope, normed, invstd, pulled, partial, node_sums, *node_terms = call(
        functools.partial(forward_kernel, scale=node_norm),
        [
            ((edge_count, hidden_width), BF),
            ((edge_count, hidden_width), F32),
            ((edge_count, width), F32),
            ((edge_count, 1), F32),
            ((count, width), BF),
            ((count, width), F32),
            ((3, width), F32),
            ((count, width), BF),
            ((count, hidden_width), BF),
            ((count, hidden_width), BF),
            ((count, width), BF),
        ],
        near(part), near(npart), near(pick), near(turned), near(low), near(high), edges,
        edge_inner, edge_outer, edge_offset, edge_gain, node_offset, node_gain,
        node_inner, node_outer, node_cotan, name="forward", flops=5 << 30,
    )
    fresh, preact, spread, sums, linear, rims = call(
        functools.partial(backward_kernel, scale=edge_norm),
        [
            ((edge_count, width), F32),
            ((edge_count, hidden_width), BF),
            ((2 * count + slots, hidden_width), BF),
            ((6, width), F32),
            ((edge_count, width), BF),
            ((slots, width), BF),
        ],
        near(pick), near(turned), edge_cotan, near(normed), near(invstd), near(slope), near(pulled),
        edge_outer, edge_gain, near(node_sums), edge_inner,
        name="backward", flops=3 << 30,
    )

    def weights_of(plan, marks):
        preact_late, linear_late = after(marks, preact, linear)
        columns = plan.columns if plan else slice(0, hidden_width)
        chunk = columns.stop - columns.start
        sends = [((plan.rows, chunk), BF)] if plan else []
        return call(
            functools.partial(
                weights_kernel, columns=columns, scales=(edge_norm, node_norm), plan=plan
            ),
            [((weight_rows, chunk), F32)] + sends,
            near(edges_turned), nodes, near(low), near(high), near(hidden), near(preact_late), near(linear_late),
            near(spread), *[near(a) for a in node_terms],
            name="weights", flops=chunk << 22,
        )

    results = {}

    def grads_side(marks):
        spread_late, fresh_late = after(marks, spread, fresh)
        results["nodes"], results["edges"] = call(
            grads_kernel,
            [((count, width), F32), ((edge_count, width), BF)],
            near(spread_late), edge_inner, near(partial), near(fresh_late), near(preact),
            name="grads", flops=2 << 30, plain=(1,),
        )
        return (results["nodes"],)

    if plans:
        grad_weights, grad_vectors, grad_nodes = reduce_kernels(
            plans, Sides(weights_of, rims, grads_side, lists), sums, hidden_width
        )
    else:
        grad_weights, grad_vectors = reduce_all(weights_of(None, ())[0], sums)
        back = jnp.concatenate([ring(rims[:half], 1), ring(rims[half:], -1)])
        grads_side((sums,))
        (grad_nodes,) = call(
            rims_kernel, [((count, width), F32)], lists, near(results["nodes"]), near(back),
            name="rims", plain=(0,), limit=4 << 20,
        )
    return (grad_nodes, results["edges"], grad_weights, grad_vectors)


def solution(mesh):
    in_specs = (
        P(AXES, None), P(AXES, None), P(AXES, None), P(AXES, None),
        P(), P(), P(), P(), P(), P(), P(), P(), P(), P(),
        P("region", "patch", None, None), P(AXES), P(AXES),
    )
    out_specs = (P(AXES, None), P(AXES, None), P(AXES), P())
    return jax.shard_map(
        per_device, mesh=mesh, in_specs=in_specs, out_specs=out_specs, check_vma=False
    )
```

```python
import collections
import functools
import math

import jax
import jax.numpy as jnp
from jax import lax
from jax.experimental import pallas as pl
from jax.experimental.pallas import tpu as pltpu
from jax.sharding import PartitionSpec as P

BF = jnp.bfloat16
F32 = jnp.float32
LANES = 128
VMEM = pltpu.VMEM
AXES = ("region", "patch")


def pinned(shape, dtype):
    return pltpu.VMEM(shape, dtype)


def mm(a, b):
    return jnp.dot(a, b, preferred_element_type=F32)


def mm_nt(a, b):
    return lax.dot_general(a, b, (((1,), (1,)), ((), ())), preferred_element_type=F32)


def mm_tn(a, b):
    return lax.dot_general(a, b, (((0,), (0,)), ((), ())), preferred_element_type=F32)


def call(body, outs, *args, flops=0, limit=24 << 20, name=None, plain=(), hbm=(), scratch=()):
    vmem = pl.BlockSpec(memory_space=pltpu.VMEM)
    anywhere = pl.BlockSpec(memory_space=pltpu.HBM)
    shapes = [
        jax.ShapeDtypeStruct(s, d) if i in plain else pinned(s, d) for i, (s, d) in enumerate(outs)
    ]
    moved = sum(math.prod(s) * jnp.dtype(d).itemsize for s, d in outs)
    return pl.pallas_call(
        body,
        out_shape=shapes,
        in_specs=[anywhere if i in hbm else vmem for i in range(len(args))],
        out_specs=[vmem] * len(outs),
        scratch_shapes=list(scratch),
        compiler_params=pltpu.CompilerParams(vmem_limit_bytes=limit),
        cost_estimate=pl.CostEstimate(flops=flops, bytes_accessed=moved, transcendentals=0),
        name=name,
    )(*[far(a) if i in hbm else a for i, a in enumerate(args)])


def far(array):
    return pltpu.with_memory_space_constraint(array, pltpu.HBM)


def near(array):
    return pltpu.with_memory_space_constraint(array, pltpu.VMEM)


def start_copies(pairs, sems):
    copies = [pltpu.make_async_copy(a, b, sems.at[i]) for i, (a, b) in enumerate(pairs)]
    for copy in copies:
        copy.start()
    return copies


def layer_norm(values):
    centred = values - jnp.mean(values, axis=-1, keepdims=True)
    invstd = lax.rsqrt(jnp.mean(centred * centred, axis=-1, keepdims=True) + 1e-05)
    return centred * invstd, invstd


def norm_back(upstream, normed, invstd, gains):
    scaled = upstream * gains
    return invstd * (
        scaled
        - jnp.mean(scaled, axis=-1, keepdims=True)
        - normed * jnp.mean(scaled * normed, axis=-1, keepdims=True)
    )


def silu_and_slope(preact):
    gate = 0.5 * jnp.tanh(0.5 * preact) + 0.5
    hidden = preact * gate
    return hidden, gate + hidden * (1.0 - gate)


def column_sum(values):
    return jnp.sum(values, axis=0, keepdims=True)


def pick_kernel(lists_hbm, nodes_hbm, low_ref, high_ref, lists_ref, nodes_ref, sems):
    for copy in start_copies([(lists_hbm, lists_ref), (nodes_hbm, nodes_ref)], sems):
        copy.wait()
    slots, count = lists_ref.shape[1], nodes_ref.shape[0]
    rows = lax.broadcasted_iota(jnp.int32, (count, slots), 0)
    for k, out_ref in enumerate((low_ref, high_ref)):
        pick = jnp.where(rows == lists_ref[k : k + 1, :], 1.0, 0.0).astype(BF)
        out_ref[...] = mm_tn(pick, nodes_ref[...]).astype(BF)


def table_kernel(
    senders_ref, receivers_ref, shift_ref, nodes_ref, inner_ref, edges_ref, ninner_ref, nshift_ref,
    part_ref, npart_ref, pick_ref, turned_ref, edges_turned_ref, own_ref,
):
    edge_count, width = edges_ref.shape
    count = nodes_ref.shape[0]
    senders = senders_ref[...]
    receivers = receivers_ref[...] + count
    senders = jnp.where(senders < count, senders, senders + count)
    wide_send = jnp.transpose(jnp.broadcast_to(senders, (LANES, edge_count)))
    wide_recv = jnp.transpose(jnp.broadcast_to(receivers, (LANES, edge_count)))
    lane = lax.broadcasted_iota(jnp.int32, (edge_count, LANES), 1)
    row = lax.broadcasted_iota(jnp.int32, (LANES, edge_count), 0)
    for start in range(0, pick_ref.shape[1], LANES):
        own_part = count <= start < 2 * count
        tall = wide_recv if own_part else wide_send
        flat = receivers if own_part else senders
        pick_ref[:, start : start + LANES] = jnp.where(tall == lane + start, 1.0, 0.0).astype(BF)
        turned_ref[start : start + LANES, :] = jnp.where(flat == row + start, 1.0, 0.0).astype(BF)
    nodes = nodes_ref[...]
    own_ref[:count, :] = mm(nodes, inner_ref[width : 2 * width, :]).astype(BF)
    own_ref[count:, :] = mm(nodes, inner_ref[2 * width :, :]).astype(BF)
    tile = edge_count // 2
    for start in range(0, edge_count, tile):
        rows = slice(start, start + tile)
        part_ref[rows, :] = (
            mm(edges_ref[rows, :], inner_ref[:width, :])
            + mm(pick_ref[rows, : 2 * count], own_ref[...])
            + shift_ref[...]
        )
    npart_ref[...] = mm(nodes, ninner_ref[:width, :]) + nshift_ref[...]
    edges_turned_ref[...] = edges_ref[...].T


def forward_kernel(
    part_ref, npart_ref, pick_ref, turned_ref, low_ref, high_ref, edges_ref,
    einner_ref, eouter_ref, eoffset_ref, egain_ref, noffset_ref, ngain_ref,
    ninner_ref, nouter_ref, cotan_ref,
    hidden_ref, slope_ref, normed_ref, invstd_ref, pulled_ref, partial_ref, sums_ref,
    aggregate_ref, node_hidden_ref, node_preact_ref, node_linear_ref,
    *, scale,
):
    edge_count, width = edges_ref.shape
    count = cotan_ref.shape[0]
    rim = jnp.concatenate([low_ref[...], high_ref[...]], axis=0)
    far = mm(rim, einner_ref[width : 2 * width, :]).astype(BF)
    slots = rim.shape[0]
    tile = edge_count // 1
    tiles = [slice(start, start + tile) for start in range(0, edge_count, tile)]

    def first(rows):
        return part_ref[rows, :] + mm(pick_ref[rows, 2 * count : 2 * count + slots], far)

    def second(rows, preact):
        hidden, slope = silu_and_slope(preact)
        hidden = hidden.astype(BF)
        hidden_ref[rows, :] = hidden
        slope_ref[rows, :] = slope
        return mm(hidden, eouter_ref[...]) + eoffset_ref[...]

    def third(rows, linear):
        normed, invstd = layer_norm(linear)
        normed_ref[rows, :] = normed
        invstd_ref[rows, :] = invstd
        fresh = (edges_ref[rows, :].astype(F32) + egain_ref[...] * normed).astype(BF)
        return mm(turned_ref[count : 2 * count, rows], fresh)

    preacts = [first(rows) for rows in tiles]
    linears = [second(rows, preact) for rows, preact in zip(tiles, preacts)]
    total = sum(third(rows, linear) for rows, linear in zip(tiles, linears))
    aggregate = total.astype(BF)
    preact = npart_ref[...] + mm(aggregate, ninner_ref[width:, :])
    hidden, slope = silu_and_slope(preact)
    hidden = hidden.astype(BF)
    normed, invstd = layer_norm(mm(hidden, nouter_ref[...]) + noffset_ref[...])
    cotan = cotan_ref[...].astype(F32)
    linear_back = norm_back(cotan, normed, invstd, ngain_ref[...])
    linear_half = linear_back.astype(BF)
    preact_back = mm_nt(linear_half, nouter_ref[...]) * slope
    preact_half = preact_back.astype(BF)
    pulled_ref[...] = mm_nt(preact_half, ninner_ref[width:, :]).astype(BF)
    partial_ref[...] = cotan + mm_nt(preact_half, ninner_ref[:width, :])
    aggregate_ref[...] = aggregate
    node_hidden_ref[...] = hidden
    node_preact_ref[...] = preact_half
    node_linear_ref[...] = linear_half
    sums_ref[0:1, :] = column_sum(preact_back) * scale
    sums_ref[1:2, :] = column_sum(linear_back) * scale
    sums_ref[2:3, :] = column_sum(cotan * normed) * scale


def backward_kernel(
    pick_ref, turned_ref, ecotan_ref, normed_ref, invstd_ref, slope_ref, pulled_ref, eouter_ref,
    egain_ref, node_sums_ref,
    fresh_ref, preact_ref, spread_ref, sums_ref, linear_ref, *, scale,
):
    edge_count = ecotan_ref.shape[0]
    count = pulled_ref.shape[0]
    tile = edge_count // 1
    tiles = [slice(start, start + tile) for start in range(0, edge_count, tile)]
    sums = [0.0, 0.0, 0.0]

    def first(rows):
        return ecotan_ref[rows, :].astype(F32) + mm(
            pick_ref[rows, count : 2 * count], pulled_ref[...]
        )

    def second(rows, fresh_back):
        fresh_ref[rows, :] = fresh_back
        normed = normed_ref[rows, :]
        linear_back = norm_back(fresh_back, normed, invstd_ref[rows, :], egain_ref[...])
        linear_half = linear_back.astype(BF)
        linear_ref[rows, :] = linear_half
        sums[1] += column_sum(linear_back)
        sums[2] += column_sum(fresh_back * normed)
        return mm_nt(linear_half, eouter_ref[...])

    def third(rows, back):
        preact_back = back * slope_ref[rows, :]
        preact_ref[rows, :] = preact_back.astype(BF)
        sums[0] += column_sum(preact_back)

    fresh_backs = [first(rows) for rows in tiles]
    backs = [second(rows, fresh_back) for rows, fresh_back in zip(tiles, fresh_backs)]
    for rows, back in zip(tiles, backs):
        third(rows, back)
    for k in range(3):
        sums_ref[k : k + 1, :] = sums[k] * scale
    sums_ref[3:, :] = node_sums_ref[...]
    used = spread_ref.shape[0]
    spread_ref[...] = mm(turned_ref[:used, :], preact_ref[...]).astype(BF)


def weights_kernel(
    edges_turned_ref, nodes_ref, low_ref, high_ref, hidden_ref, preact_ref, linear_ref, spread_ref,
    aggregate_ref, node_hidden_ref, node_preact_ref, node_linear_ref,
    weights_ref, *sends, columns, scales, plan,
):
    count = nodes_ref.shape[0]
    nodes = nodes_ref[...]
    rim = jnp.concatenate([low_ref[...], high_ref[...]], axis=0)
    node_preact = node_preact_ref[:, columns]
    chunk = columns.stop - columns.start
    by_nodes = mm_tn(
        nodes,
        jnp.concatenate(
            [spread_ref[:count, columns], spread_ref[count : 2 * count, columns], node_preact], axis=1
        ),
    )
    start = 0
    for scale, term in (
        (scales[0], mm(edges_turned_ref[...], preact_ref[:, columns])),
        (scales[0], by_nodes[:, :chunk] + mm_tn(rim, spread_ref[2 * count :, columns])),
        (scales[0], by_nodes[:, chunk : 2 * chunk]),
        (scales[0], mm_tn(hidden_ref[...], linear_ref[:, columns])),
        (scales[1], by_nodes[:, 2 * chunk :]),
        (scales[1], mm_tn(aggregate_ref[...], node_preact)),
        (scales[1], mm_tn(node_hidden_ref[...], node_linear_ref[:, columns])),
    ):
        value = term * scale
        weights_ref[start : start + value.shape[0], :] = value
        start += value.shape[0]
    for send_ref in sends:
        other = 1 - plan.core()
        for position in range(plan.count // 2):
            row = position * plan.block
            send_ref[row : row + plan.block, :] = weights_ref[
                pl.ds(plan.source(position, other), plan.block), :
            ].astype(BF)


def rim_kernel(spread_ref, inner_ref, out_ref, *, count):
    width, slots = spread_ref.shape[1], out_ref.shape[0]
    rows = mm_nt(spread_ref[2 * count :, :], inner_ref[width : 2 * width, :]).astype(BF)
    out_ref[: slots // 2, :] = rows[slots // 2 :]
    out_ref[slots // 2 :, :] = rows[: slots // 2]


def grads_kernel(spread_ref, inner_ref, partial_ref, fresh_ref, preact_ref, nodes_ref, edges_ref):
    count, width = partial_ref.shape
    nodes_ref[...] = (
        partial_ref[...]
        + mm_nt(spread_ref[:count, :], inner_ref[width : 2 * width, :])
        + mm_nt(spread_ref[count : 2 * count, :], inner_ref[2 * width :, :])
    )
    edge_count = preact_ref.shape[0]
    tile = edge_count // 2
    for start in range(0, edge_count, tile):
        rows = slice(start, start + tile)
        edges_ref[rows, :] = (
            fresh_ref[rows, :] + mm_nt(preact_ref[rows, :], inner_ref[:width, :])
        ).astype(BF)


def rims_kernel(lists_ref, partial_ref, back_ref, out_ref):
    count, half = partial_ref.shape[0], lists_ref.shape[1]
    rows = lax.broadcasted_iota(jnp.int32, (count, half), 0)
    total = partial_ref[...]
    for k in range(2):
        pick = jnp.where(rows == lists_ref[k : k + 1, :], 1.0, 0.0).astype(BF)
        total += mm(pick, back_ref[k * half : (k + 1) * half, :])
    out_ref[...] = total


def ring(values, step):
    count = lax.axis_size("patch")
    return lax.ppermute(values, "patch", [(i, (i + step) % count) for i in range(count)])


def halving_orders():
    core_bit = lax.axis_size("patch")
    high = [core_bit << k for k in range(1, lax.axis_size("region").bit_length() - 1)]
    low = [1 << k for k in range(core_bit.bit_length() - 1)]
    return core_bit, high + low, low + high


def permute_by(values, first, second, core_bit):
    count = lax.axis_size("region") * lax.axis_size("patch")
    pairs = [(i, i ^ (second if i & core_bit else first)) for i in range(count)]
    return lax.ppermute(values, AXES, pairs)


def reduce_all(flat, vectors):
    core_bit, first, second = halving_orders()
    count = lax.axis_size("region") * lax.axis_size("patch")
    me = lax.axis_index(AXES)
    core = (me & core_bit) // core_bit
    depth = count.bit_length() - 1
    flat = flat.reshape((2,) * depth + (-1, flat.shape[1]))

    def ordered(order):
        axes = [depth - bit.bit_length() for bit in [core_bit] + order]
        return jnp.transpose(flat, axes + [depth, depth + 1])

    blocks = jnp.stack([ordered(first)[0], ordered(second)[1]]).reshape(2, -1, flat.shape[-1])
    kept = lax.dynamic_index_in_dim(blocks, core, 0, keepdims=False)
    sent = lax.dynamic_index_in_dim(blocks, 1 - core, 0, keepdims=False).astype(BF)
    got = permute_by(sent, core_bit, core_bit, core_bit)
    total = kept + got
    for one, two in zip(first, second):
        bit = jnp.where(core == 1, (me & two) // two, (me & one) // one)
        halves = total.reshape(2, -1, flat.shape[-1])
        kept = lax.dynamic_index_in_dim(halves, bit, 0, keepdims=False)
        sent = lax.dynamic_index_in_dim(halves, 1 - bit, 0, keepdims=False).astype(BF)
        got = permute_by(sent, one, two, core_bit)
        vectors = vectors + permute_by(vectors, one, two, core_bit)
        total = kept + got
    vectors = vectors + permute_by(vectors, core_bit, core_bit, core_bit)
    return total.reshape(-1), vectors.reshape(-1)


Sides = collections.namedtuple("Sides", ("weights", "early", "late", "last"))


class Halving:
    def __init__(self, rows, columns, orders, carries):
        self.core_bit, (self.first, self.second) = lax.axis_size("patch"), orders
        self.count = lax.axis_size("region") * lax.axis_size("patch")
        self.block = rows // self.count
        self.rows = rows // 2
        self.columns = columns
        self.width = columns.stop - columns.start
        self.steps = len(self.first)
        self.carries = carries

    def place(self, order, core, position):
        block = self.core_bit if core else 0
        for k, bit in enumerate(order):
            if (position >> (self.steps - 1 - k)) & 1:
                block |= bit
        return block * self.block

    def me(self):
        return lax.axis_index("region") * self.core_bit + lax.axis_index("patch")

    def core(self):
        return lax.rem(self.me() // self.core_bit, 2)

    def bit(self, step):
        me = self.me()
        one, two = self.first[step], self.second[step]
        return jnp.where(self.core() == 1, lax.rem(me // two, 2), lax.rem(me // one, 2))

    def source(self, position, core):
        zero, one = self.place(self.first, 0, position), self.place(self.second, 1, position)
        return pl.multiple_of(jnp.where(core == 1, one, zero), 8)

    def pieces(self, full):
        return full // self.width

    def extra(self, full):
        return 16 * self.pieces(full) if self.carries else 0

    def slots(self, step, rows):
        if not self.carries:
            return 0
        bits = (self.first[step], self.second[step])
        return rows if 1 in bits else rows // 2 if min(bits) < self.core_bit else 0

    def taken(self, step):
        place = lax.rem(self.me(), self.core_bit)
        even = lax.rem(place, 2) == 0
        answers = []
        for bit in (self.first[step], self.second[step]):
            if bit == 1 or bit > self.core_bit:
                answers.append((bit == 1, bit == 1))
                continue
            between = lax.rem(place, bit) // 2
            up = jnp.logical_and(even, between == 0)
            down = jnp.logical_and(jnp.logical_not(even), between == bit // 2 - 1)
            answers.append((up, down))
        core = self.core() == 1
        return tuple(jnp.where(core, b, a) for a, b in zip(*answers))


def halve(src_ref, got_ref, out_ref, plan, step, side):
    half = plan.rows >> (step + 1)
    bit = plan.bit(step)
    chosen = 1 - bit if side else bit
    if step:
        start = pl.multiple_of(chosen * half, 16)
        held = src_ref[pl.ds(start, half), :]
        out_ref[:half, :] = (held + got_ref[pl.ds(start, half), :]).astype(out_ref.dtype)
        return
    core = plan.core()
    per_half = half // plan.block
    for k in range(per_half):
        low, high = plan.source(k, core), plan.source(k + per_half, core)
        row = pl.multiple_of(jnp.where(chosen == 1, high, low), 8)
        held = src_ref[pl.ds(row, plan.block), :]
        start = pl.multiple_of(chosen * half + k * plan.block, 16)
        got = got_ref[pl.ds(start, plan.block), :]
        out_ref[k * plan.block : (k + 1) * plan.block, :] = (held + got).astype(out_ref.dtype)


def keep_kernel(src_ref, got_ref, out_ref, *, plan, step):
    halve(src_ref, got_ref, out_ref, plan, step, 0)


def unpack(got_ref, start, rows, plan, full):
    parts = [
        got_ref[start + k * rows : start + (k + 1) * rows, :] for k in range(plan.pieces(full))
    ]
    return jnp.concatenate(parts, axis=1).astype(F32)


def pack(out_ref, start, values, plan):
    rows = values.shape[0]
    for k in range(plan.pieces(values.shape[1])):
        out_ref[start + k * rows : start + (k + 1) * rows, :] = values[
            :, k * plan.width : (k + 1) * plan.width
        ].astype(BF)


def add_vectors(vec_ref, got_ref, start, plan):
    count, full = vec_ref.shape
    both = unpack(got_ref, start, 16, plan, full)
    return vec_ref[...] + (both[:count] + both[8 : 8 + count])


def move_halo(state_ref, got_ref, start, plan, step):
    rows, full = state_ref.shape
    half = rows // 2
    slots = plan.slots(step, rows)
    state = state_ref[...].astype(F32)
    if not slots:
        return state
    came = unpack(got_ref, start, slots, plan, full)
    up, down = plan.taken(step)
    return jnp.concatenate(
        [
            jnp.where(up, came[:half], state[:half]),
            jnp.where(down, came[slots - half :], state[half:]),
        ],
        axis=0,
    )


def send_kernel(src_ref, got_ref, *refs, plan, step):
    if not plan.carries:
        halve(src_ref, got_ref, refs[0], plan, step, 1)
        return
    vec_ref, state_ref, out_ref, new_ref, moved_ref = refs
    halve(src_ref, got_ref, out_ref, plan, step, 1)
    half = plan.rows >> (step + 1)
    count, full = vec_ref.shape
    vec, state = vec_ref[...], state_ref[...].astype(F32)
    if step:
        vec = add_vectors(vec_ref, got_ref, 2 * half, plan)
        state = move_halo(state_ref, got_ref, 2 * half + plan.extra(full), plan, step - 1)
    upper = vec.astype(BF).astype(F32)
    lower = (vec - upper).astype(BF).astype(F32)
    gap = jnp.zeros((8 - count, full), F32)
    pack(out_ref, half, jnp.concatenate([upper, gap, lower, gap], axis=0), plan)
    new_ref[...] = upper + lower
    moved_ref[...] = state.astype(BF)
    rows = state.shape[0]
    slots = plan.slots(step, rows)
    if slots == rows:
        pack(out_ref, half + plan.extra(full), state, plan)
    elif slots:
        even = lax.rem(plan.me(), 2) == 0
        pack(
            out_ref, half + plan.extra(full),
            jnp.where(even, state[: rows // 2], state[rows // 2 :]), plan,
        )


def carried_kernel(vec_ref, state_ref, got_ref, new_ref, moved_ref, *, plan):
    new_ref[...] = add_vectors(vec_ref, got_ref, plan.block, plan)
    start = plan.block + plan.extra(vec_ref.shape[1])
    moved_ref[...] = move_halo(state_ref, got_ref, start, plan, plan.steps - 1).astype(BF)


def close_kernel(vec_ref, other_ref, *refs, plans):
    *refs, out_ref, vectors_ref = refs
    pieces = out_ref.shape[0] // plans[0].block
    for plan, held_ref, got_ref in zip(plans, refs[0::2], refs[1::2]):
        total = held_ref[...] + got_ref[: plan.block, :]
        for k in range(0, plan.width, LANES):
            piece = (plan.columns.start + k) // LANES
            out_ref[pl.ds(piece, plan.block, stride=pieces), :] = total[:, k : k + LANES]
    vec = vec_ref[...] + other_ref[...]
    for k in range(pieces):
        vectors_ref[pl.ds(k, vec.shape[0], stride=pieces), :] = vec[:, k * LANES : (k + 1) * LANES]


def after(marks, *values):
    return lax.optimization_barrier((*values, *marks))[: len(values)]


def reduce_kernels(plans, sides, vec, width):
    full = vec.shape[1]
    held, got = {}, {}
    marks, state = (), None
    for plan in plans:
        held[plan], sent = sides.weights(plan, marks)
        marks = (sent,)
        got[plan] = permute_by(sent, plan.core_bit, plan.core_bit, plan.core_bit)
        if state is None:
            state = sides.early(marks)
            marks = (state,)
    shapes = [(vec.shape, F32), (state.shape, BF)]
    for step in range(plans[0].steps):
        if step == 1:
            (nodes,) = marks = sides.late(marks)
        for plan in plans:
            half = plan.rows >> (step + 1)
            source, came = after(marks, held[plan], got[plan])
            rows = half + plan.extra(full) + plan.slots(step, state.shape[0]) * plan.pieces(full)
            carried = [near(vec), near(state)] if plan.carries else []
            sent, *new = call(
                functools.partial(send_kernel, plan=plan, step=step),
                [((rows, plan.width), BF)] + (shapes if plan.carries else []),
                near(source), near(came), *carried, name=f"send{step}",
            )
            if plan.carries:
                vec, state = new
            marks = (sent,)
            source, came = after(marks, source, came)
            incoming = permute_by(sent, plan.first[step], plan.second[step], plan.core_bit)
            (held[plan],) = call(
                functools.partial(keep_kernel, plan=plan, step=step),
                [((half, plan.width), F32)], near(source), near(came), name=f"keep{step}",
            )
            got[plan] = incoming
    (carrier,) = [plan for plan in plans if plan.carries]
    vec, state = call(
        functools.partial(carried_kernel, plan=carrier), shapes, near(vec), near(state),
        near(got[carrier]), name="carried",
    )
    other = permute_by(vec, carrier.core_bit, carrier.core_bit, carrier.core_bit)
    pairs = [near(a) for plan in plans for a in (held[plan], got[plan])]
    (nodes,) = call(
        rims_kernel, [(nodes.shape, F32)], sides.last, near(nodes), near(state), name="rims",
        plain=(0,), limit=4 << 20,
    )
    out, vectors = call(
        functools.partial(close_kernel, plans=plans),
        [
            ((plans[0].block * width // LANES, LANES), F32),
            ((vec.size // LANES, LANES), F32),
        ],
        near(vec), near(other), *pairs, name="close", plain=(0, 1),
    )
    return out.reshape(-1), vectors.reshape(-1), nodes


def make_plans(rows, width, slots):
    count = lax.axis_size("region") * lax.axis_size("patch")
    core_bit, first, second = halving_orders()
    if rows % (16 * count) or width % (4 * LANES) or slots % 32:
        return []
    high = [b for b in sorted(first) if b > core_bit]
    low = [b for b in sorted(first) if b < core_bit]
    turned = low[1:-1] + high + low[:1] + low[-1:]
    quarter = width // 4
    chunks = CHUNKS
    return [
        Halving(
            rows, slice(a * quarter, b * quarter),
            (turned, turned) if kind else (first, second), i == 0,
        )
        for i, (a, b, kind) in enumerate(chunks)
    ]


PICK = 20 << 30
CHUNKS = ((0, 2, 0), (2, 4, 0))


def per_device(
    nodes, edges, node_cotan, edge_cotan, edge_inner, edge_outer, node_inner, node_outer, edge_shift,
    edge_offset, edge_gain, node_shift, node_offset, node_gain, send_rows, senders, receivers,
):
    count, width = nodes.shape
    edge_count = edges.shape[0]
    hidden_width = edge_outer.shape[0]
    lists = send_rows.reshape(send_rows.shape[2:])
    half = lists.shape[1]
    slots = 2 * half
    devices_all = lax.axis_size("region") * lax.axis_size("patch")
    edge_norm = 1.0 / math.sqrt(edge_count * devices_all)
    node_norm = 1.0 / math.sqrt(count * devices_all)
    picked = 2 * count + -(-slots // LANES) * LANES
    edge_rows = 3 * width + hidden_width
    weight_rows = edge_rows + 2 * width + hidden_width
    plans = make_plans(weight_rows, hidden_width, slots)
    edge_shift, edge_offset, edge_gain, node_shift, node_offset, node_gain = (
        v.reshape(1, -1)
        for v in (edge_shift, edge_offset, edge_gain, node_shift, node_offset, node_gain)
    )

    out_low, out_high = call(
        pick_kernel, [((half, width), BF)] * 2, lists, nodes, name="pick", limit=4 << 20, hbm=(0, 1), flops=PICK,
        scratch=[
            pltpu.VMEM(lists.shape, jnp.int32), pltpu.VMEM(nodes.shape, BF),
            pltpu.SemaphoreType.DMA((2,)),
        ],
    )
    low = ring(out_high, 1)
    high = ring(out_low, -1)

    part, npart, pick, turned, edges_turned = call(
        table_kernel,
        [
            ((edge_count, hidden_width), F32),
            ((count, hidden_width), F32),
            ((edge_count, picked), BF),
            ((picked, edge_count), BF),
            ((width, edge_count), BF),
        ],
        senders.reshape(1, -1), receivers.reshape(1, -1), edge_shift, nodes, edge_inner, edges,
        node_inner, node_shift,
        name="table", flops=4 * edge_count * width * hidden_width,
        scratch=[pltpu.VMEM((2 * count, hidden_width), BF)],
    )
    hidden, slope, normed, invstd, pulled, partial, node_sums, *node_terms = call(
        functools.partial(forward_kernel, scale=node_norm),
        [
            ((edge_count, hidden_width), BF),
            ((edge_count, hidden_width), F32),
            ((edge_count, width), F32),
            ((edge_count, 1), F32),
            ((count, width), BF),
            ((count, width), F32),
            ((3, width), F32),
            ((count, width), BF),
            ((count, hidden_width), BF),
            ((count, hidden_width), BF),
            ((count, width), BF),
        ],
        near(part), near(npart), near(pick), near(turned), near(low), near(high), edges,
        edge_inner, edge_outer, edge_offset, edge_gain, node_offset, node_gain,
        node_inner, node_outer, node_cotan, name="forward", flops=5 << 30,
    )
    fresh, preact, spread, sums, linear = call(
        functools.partial(backward_kernel, scale=edge_norm),
        [
            ((edge_count, width), F32),
            ((edge_count, hidden_width), BF),
            ((2 * count + slots, hidden_width), BF),
            ((6, width), F32),
            ((edge_count, width), BF),
        ],
        near(pick), near(turned), edge_cotan, near(normed), near(invstd), near(slope), near(pulled),
        edge_outer, edge_gain, near(node_sums),
        name="backward", flops=3 << 30,
    )

    def weights_of(plan, marks):
        preact_late, linear_late = after(marks, preact, linear)
        columns = plan.columns if plan else slice(0, hidden_width)
        chunk = columns.stop - columns.start
        sends = [((plan.rows, chunk), BF)] if plan else []
        return call(
            functools.partial(
                weights_kernel, columns=columns, scales=(edge_norm, node_norm), plan=plan
            ),
            [((weight_rows, chunk), F32)] + sends,
            near(edges_turned), nodes, near(low), near(high), near(hidden), near(preact_late), near(linear_late),
            near(spread), *[near(a) for a in node_terms],
            name="weights", flops=chunk << 22,
        )

    results = {}

    def rim_side(marks):
        (spread_late,) = after(marks, spread)
        (rims,) = call(
            functools.partial(rim_kernel, count=count), [((slots, width), BF)],
            near(spread_late), edge_inner, name="rim", limit=4 << 20,
        )
        return rims

    def grads_side(marks):
        spread_late, fresh_late = after(marks, spread, fresh)
        results["nodes"], results["edges"] = call(
            grads_kernel,
            [((count, width), F32), ((edge_count, width), BF)],
            near(spread_late), edge_inner, near(partial), near(fresh_late), near(preact),
            name="grads", flops=2 << 30, plain=(1,),
        )
        return (results["nodes"],)

    if plans:
        grad_weights, grad_vectors, grad_nodes = reduce_kernels(
            plans, Sides(weights_of, rim_side, grads_side, lists), sums, hidden_width
        )
    else:
        grad_weights, grad_vectors = reduce_all(weights_of(None, ())[0], sums)
        rims = rim_side((sums,))
        back = jnp.concatenate([ring(rims[:half], 1), ring(rims[half:], -1)])
        grads_side((sums,))
        (grad_nodes,) = call(
            rims_kernel, [((count, width), F32)], lists, near(results["nodes"]), near(back),
            name="rims", plain=(0,), limit=4 << 20,
        )
    return (grad_nodes, results["edges"], grad_weights, grad_vectors)


def solution(mesh):
    in_specs = (
        P(AXES, None), P(AXES, None), P(AXES, None), P(AXES, None),
        P(), P(), P(), P(), P(), P(), P(), P(), P(), P(),
        P("region", "patch", None, None), P(AXES), P(AXES),
    )
    out_specs = (P(AXES, None), P(AXES, None), P(AXES), P())
    return jax.shard_map(
        per_device, mesh=mesh, in_specs=in_specs, out_specs=out_specs, check_vma=False
    )
```
